32 devices in a mesh: grp: 4 (over x, core), dev: 8 (over z, y).
Axes of the slice: x: 2, y: 2, z: 4, core: 2. Of those that a mesh axis runs over, the one named last changes fastest.
Arguments:
- amplitudes: bfloat16 [32, 128, 128], P(('grp', 'dev')), may hold values from -2 to 2
- bases: bfloat16 [32, 256, 128], P(('grp', 'dev')), may hold values from -0.375 to 0.375
- factors: bfloat16 [32, 32, 256, 256], P(('grp', 'dev')), may hold values from -0.1875 to 0.1875
- intersections: bfloat16 [32, 4, 128, 128], P(('grp', 'dev')), may hold values from -0.25 to 0.25
- pair_integrals: float32 [32, 128, 128], P(('grp', 'dev')), may hold values from -6 to 6
- pno_energies: float32 [32, 128], P(('grp', 'dev')), may hold values from 0.3 to 3
- pair_shift: float32 [32], P(('grp', 'dev')), may hold values from 0.5 to 4
- pair_atoms: int32 [32, 2], P('grp'), may hold values from 0 to 7, all different within a row; in each aligned block of 8 rows (0 to 7, 8 to 15, ...) at most 3 rows name the same one
- pair_next: int32 [32, 4], P(('grp', 'dev')), may hold values from 0 to 15, as said below
Outputs:
- new_amplitudes: float32 [32, 128, 128], P(('grp', 'dev'))
The draws below stay inside these ranges and needn't reach their ends.
Inputs may be any that keep to these rules, and one draw needn't show every extreme that they name: `pair_atoms`: each pair lists 2 different atoms of its own group. Within a group no atom is listed by more than 3 pairs, and some atom is listed by exactly 3 pairs of its group. `pair_next`: each pair lists 4 different pairs other than itself; a number below 8 is a pair of its own group, a number m from 8 on is pair m - 8 of the next group. Pairs of the last group list only pairs of their own group.
All inputs are finite; a program needn't handle non-finite values.
Results may differ from the reference program's by a relative error of at most 0.008.
Values may be sent and summed in bfloat16 or wider, within the bound.
No kernel may reach another device: no remote copies, remote signals or barrier semaphores. Data moves between devices by JAX's collectives and lax.ppermute only.
A program may use at most 128 MiB of HBM per device.

```python
import math
import jax
import jax.numpy as jnp
import numpy as np
from jax import lax

NPNO = 128
NPAO = 256
KAUX = 32
DOM = 2
CAP = 3
NOV = 4
ITERS = 2
GROUPS = 4
PAIR_GRP = 8
PAIRS = 32
ATOMS = 32


def draw_pair_next(key, part):
    row_ids = jnp.arange(PAIRS, dtype=jnp.int32)
    local_index = row_ids % PAIR_GRP
    group_index = row_ids // PAIR_GRP
    candidates = jnp.arange(2 * PAIR_GRP, dtype=jnp.int32)
    scores = jax.random.randint(key, (PAIRS, 2 * PAIR_GRP), 0, 2 ** 20, dtype=jnp.int32) * (4 * PAIR_GRP) + candidates[None, :]
    excluded = (candidates[None, :] == local_index[:, None]) | (group_index[:, None] == GROUPS - 1) & (candidates[None, :] >= PAIR_GRP)
    scores = jnp.where(excluded, -1, scores)
    top_scores, picked = lax.top_k(scores, NOV)
    return picked.astype(jnp.int32)


def block_levels(rng, extent, split, least, largest):
    level, own = 1.0, jax.random.fold_in(rng, 6)
    for position, parts in split:
        draws = jnp.exp(jax.random.uniform(jax.random.fold_in(own, position), (parts,), jnp.float32, least / len(split), largest / len(split)))
        level = level * jnp.repeat(draws, extent[position] // parts).reshape([-1 if axis == position else 1 for axis in range(len(extent))])
    return level


def shared_out(key, own, number, rows, count, top, most, skew):
    ranking = jax.random.permutation(key, count)
    heavy_load, usual = shares(count, rows * top, most, skew, True), shares(count, rows * top, most, skew, False)
    places = jnp.arange(count)

    def named(lengths, rotation):
        used = int((lengths > 0).sum())
        fixed = max(1, used // 4)
        moved = fixed + (places - fixed + rotation * (used - fixed)) % max(1, count - fixed)
        return jnp.zeros((count,), jnp.int32).at[ranking[jnp.where(places < fixed, places, moved)]].set(jnp.asarray(lengths, jnp.int32))

    lengths = jnp.where(number % 4 == 0, named(heavy_load, number // 4), named(usual, number - number // 4 - 1))
    mixed = jax.random.permutation(jax.random.fold_in(own, 3), count)
    donor, sink = mixed[0:count // 2 * 2:2], mixed[1:count // 2 * 2:2]
    slack = jnp.minimum(lengths[donor] - 1, most - lengths[sink]) // 2
    slack = jnp.where((donor == ranking[0]) | (sink == ranking[0]) | (lengths[sink] == 0), 0, jnp.maximum(slack, 0))
    moved = jax.random.randint(jax.random.fold_in(own, 4), (count // 2,), 0, 1 << 20) % (slack + 1)
    lengths = lengths.at[donor].add(-moved).at[sink].add(moved)
    items = jnp.searchsorted(jnp.cumsum(lengths), jnp.arange(rows * top), side="right").astype(jnp.int32)
    grid = items.reshape(top, rows).T
    grid = grid[jax.random.permutation(jax.random.fold_in(own, 1), rows)]
    rotation = jax.random.randint(jax.random.fold_in(own, 2), (rows, 1), 0, top)
    return jnp.take_along_axis(grid, (jnp.arange(top)[None, :] + rotation) % top, axis=1)


def shares(count, total, reach, lean, full):
    loads = [(1 << 20) // math.isqrt(rank ** lean) + 1 for rank in range(1, count + 1)]
    largest = reach if full else min(reach, max(-(-total // count), total * loads[0] // sum(loads)))
    least = 1 if total - largest >= count - 1 else 0
    holding, spare = [largest] + [least] * (count - 1), total - largest - least * (count - 1)
    while spare > 0:
        free = [i for i in range(1, count) if holding[i] < largest] or [i for i in range(1, count) if holding[i] < reach]
        pool, budget = sum([loads[i] for i in free]), spare
        for i in free:
            extra = min(reach - holding[i], max(1, budget * loads[i] // pool), spare)
            holding[i] = holding[i] + extra
            spare = spare - extra
    return np.array(holding)


def scatter_about(key, shape, spread, most, cuts=(), kind=jnp.bfloat16):
    drawn = jax.random.normal(key, shape, jnp.float32) * spread
    if len(cuts) > 0:
        drawn = block_levels(key, shape, cuts, -0.22, 0.18) * drawn
    return jnp.clip(drawn, min=-most, max=most).astype(kind)


def setup_inputs(seed: int = 0) -> dict:
    streams_of = jax.random.split(jax.random.key(seed), 10)
    amplitudes = scatter_about(streams_of[0], (PAIRS, NPNO, NPNO), 0.3, 2.0, ((0, 32),))
    bases = scatter_about(streams_of[1], (PAIRS, NPAO, NPNO), NPAO ** -0.5, 0.375, ((0, 32),))
    factors = scatter_about(streams_of[2], (ATOMS, KAUX, NPAO, NPAO), (4 * NPAO) ** -0.5, 0.1875, ((0, 32),))
    intersections = scatter_about(streams_of[3], (PAIRS, NOV, NPNO, NPNO), (4 * NPNO) ** -0.5, 0.25, ((0, 32),))
    pair_integrals = scatter_about(streams_of[4], (PAIRS, NPNO, NPNO), 1.0, 6.0, ((0, 32),), jnp.float32)
    pno_energies = jnp.clip(jnp.exp(math.log(3.0) - 2.3025851 * jax.random.uniform(streams_of[5], (PAIRS, NPNO), jnp.float32) ** block_levels(streams_of[5], (PAIRS, NPNO), ((0, 32),), -0.2, 0.2)), 0.3, 3.0)
    pair_shift = jnp.clip(jnp.exp(math.log(4.0) - 2.0794415 * jax.random.uniform(streams_of[6], (PAIRS,), jnp.float32) ** block_levels(streams_of[6], (PAIRS,), ((0, 32),), -0.2, 0.2)), 0.5, 4.0)
    pair_atoms_keys = jax.random.split(jax.random.fold_in(streams_of[7], 1), PAIRS // PAIR_GRP)
    pair_atoms_turns = jax.random.permutation(jax.random.fold_in(streams_of[7], 3), PAIRS // PAIR_GRP)
    pair_atoms = jax.vmap(lambda own, number: shared_out(jax.random.fold_in(streams_of[7], 2), own, number, PAIR_GRP, PAIR_GRP, DOM, CAP, 1))(pair_atoms_keys, pair_atoms_turns).reshape((PAIRS, DOM))
    pair_next = draw_pair_next(jax.random.fold_in(streams_of[9], 71), 0)
    return {"amplitudes": amplitudes, "bases": bases, "factors": factors, "intersections": intersections, "pair_integrals": pair_integrals, "pno_energies": pno_energies, "pair_shift": pair_shift, "pair_atoms": pair_atoms, "pair_next": pair_next}


def sandwich(factor_block, expanded):
    aux_count = factor_block.shape[0]
    pao_width = factor_block.shape[1]
    flat_factor = factor_block.reshape(aux_count * pao_width, pao_width)
    squeezed = jnp.dot(flat_factor, expanded, preferred_element_type=jnp.float32).astype(jnp.bfloat16)
    squeezed = squeezed.reshape(aux_count, pao_width, pao_width)
    return jnp.einsum('kad,kbd->ab', squeezed.astype(jnp.float32), factor_block.astype(jnp.float32))


def reference(amplitudes, bases, factors, intersections, pair_integrals, pno_energies, pair_shift, pair_atoms, pair_next):
    starts = (jnp.arange(PAIRS, dtype=jnp.int32) // PAIR_GRP) * PAIR_GRP
    atom_ids = (pair_atoms + starts[:, None]).astype(jnp.int32)
    near_ids = (pair_next + starts[:, None]).astype(jnp.int32)
    denominator = pno_energies[:, :, None] + pno_energies[:, None, :] + pair_shift[:, None, None]
    current = amplitudes
    update = None
    for iteration in range(ITERS):
        def one_pair(pair_index):
            pair_base = bases[pair_index]
            halfway = jnp.dot(pair_base, current[pair_index], preferred_element_type=jnp.float32).astype(jnp.bfloat16)
            expanded = jnp.dot(halfway, pair_base.T, preferred_element_type=jnp.float32).astype(jnp.bfloat16)

            def one_atom(running, atom_index):
                return running + sandwich(factors[atom_index], expanded), None

            ladder_pao, unused = lax.scan(one_atom, jnp.zeros((NPAO, NPAO), jnp.float32), atom_ids[pair_index])
            base_wide = pair_base.astype(jnp.float32)
            left_side = jnp.dot(base_wide.T, ladder_pao, precision=lax.Precision.HIGHEST)
            ladder = jnp.dot(left_side, base_wide, precision=lax.Precision.HIGHEST)
            neighbours = current[near_ids[pair_index]].astype(jnp.float32)
            pair_intersections = intersections[pair_index].astype(jnp.float32)
            mixed = jnp.einsum('nij,njk->nik', pair_intersections, neighbours).astype(jnp.bfloat16)
            coupling = jnp.einsum('nik,nlk->il', mixed.astype(jnp.float32), pair_intersections)
            return -(pair_integrals[pair_index] + ladder + coupling) / denominator[pair_index]

        update = lax.map(one_pair, jnp.arange(PAIRS, dtype=jnp.int32))
        if iteration + 1 < ITERS:
            current = update.astype(jnp.bfloat16)
    return update
```

```python
import functools

import jax
import jax.numpy as jnp
from jax import lax
from jax.experimental import pallas as pl
from jax.experimental.pallas import tpu as pltpu
from jax.sharding import PartitionSpec as P

CAP = 3
ITERS = 2
F32 = jnp.float32
BF16 = jnp.bfloat16


def vmem_spec():
    return pl.BlockSpec(memory_space=pltpu.VMEM)


def smem_spec():
    return pl.BlockSpec(memory_space=pltpu.SMEM)


def params(mib):
    return pltpu.CompilerParams(vmem_limit_bytes=mib * 2**20)


def gather_xor(value, axis):
    count = lax.axis_size(axis)
    bit = 1
    blocks = value
    while bit < count:
        other = lax.ppermute(blocks, axis, [(d, d ^ bit) for d in range(count)])
        blocks = jnp.concatenate([blocks, other], axis=0)
        bit *= 2
    return blocks


def from_next(value, axis):
    count = lax.axis_size(axis)
    return lax.ppermute(value, axis, [(d, d - 1) for d in range(1, count)])


def project_kernel(slots, bases_ref, factors_ref, out_ref, wide, narrow, half):
    aux, width, npno = factors_ref.shape[0], bases_ref.shape[1], bases_ref.shape[2]

    @pl.when(pl.program_id(0) == 0)
    def _():
        for s in range(CAP):
            base = bases_ref[slots[s]]
            narrow[s] = base
            wide[pl.ds(s * npno, npno), :] = base.astype(F32).T.astype(BF16)

    for k in range(aux):
        left = jnp.dot(wide[...], factors_ref[k], preferred_element_type=F32).astype(BF16)
        for s in range(CAP):
            half[s, pl.ds(k * npno, npno), :] = left[s * npno : (s + 1) * npno]
    for s in range(CAP):
        both = jnp.dot(half[s], narrow[s], preferred_element_type=F32).astype(BF16)
        for k in range(aux):
            out_ref[s, k // 2, :, pl.ds((k % 2) * npno, npno)] = both[k * npno : (k + 1) * npno]


def project(slots, group_bases, factor_block, step=8):
    aux, width, _ = factor_block.shape
    count, _, npno = group_bases.shape
    step = min(step, aux)
    return pl.pallas_call(
        project_kernel,
        grid=(aux // step,),
        in_specs=[
            smem_spec(),
            pl.BlockSpec((count, width, npno), lambda i: (0, 0, 0)),
            pl.BlockSpec((step, width, width), lambda i: (i, 0, 0)),
        ],
        out_specs=pl.BlockSpec((CAP, step // 2, npno, 2 * npno), lambda i: (0, i, 0, 0)),
        out_shape=jax.ShapeDtypeStruct((CAP, aux // 2, npno, 2 * npno), BF16),
        scratch_shapes=[
            pltpu.VMEM((CAP * npno, width), BF16),
            pltpu.VMEM((CAP, width, npno), BF16),
            pltpu.VMEM((CAP, step * npno, width), BF16),
        ],
        compiler_params=params(48),
        name="project",
    )(slots, group_bases, factor_block)


def ladder_kernel(slots, pairs, amps_ref, proj_ref, out_ref, twice, mixed):
    half, npno = proj_ref.shape[1], proj_ref.shape[2]
    out_ref[...] = jnp.zeros_like(out_ref)
    twice[...] = jnp.zeros_like(twice)
    for s in range(CAP):
        amp = amps_ref[slots[s]]
        twice[pl.ds(0, npno), pl.ds(0, npno)] = amp
        twice[pl.ds(npno, npno), pl.ds(npno, npno)] = amp
        flat = proj_ref[s].reshape(half * npno, 2 * npno)
        mixed[...] = jnp.dot(flat, twice[...], preferred_element_type=F32).astype(BF16)
        total = jnp.zeros((npno, npno), F32)
        for m in range(half):
            total = total + lax.dot_general(
                mixed[pl.ds(m * npno, npno), :],
                proj_ref[s, m],
                (((1,), (1,)), ((), ())),
                preferred_element_type=F32,
            )

        @pl.when(pairs[s] >= 0)
        def _():
            out_ref[jnp.maximum(pairs[s], 0)] = total.astype(BF16)


def ladder(slots, pairs, group_amps, projected):
    count, npno, _ = group_amps.shape
    half = projected.shape[1]
    return pl.pallas_call(
        ladder_kernel,
        in_specs=[smem_spec(), smem_spec(), vmem_spec(), vmem_spec()],
        out_specs=vmem_spec(),
        out_shape=jax.ShapeDtypeStruct((count, npno, npno), BF16),
        scratch_shapes=[
            pltpu.VMEM((2 * npno, 2 * npno), BF16),
            pltpu.VMEM((half * npno, 2 * npno), BF16),
        ],
        compiler_params=params(32),
        name="ladder",
    )(slots, pairs, group_amps, projected)


def coupling_kernel(near, own_ref, next_ref, inter_ref, ints_ref, out_ref):
    count = own_ref.shape[0]
    total = ints_ref[...]
    for n in range(inter_ref.shape[0]):
        at = near[n]
        own = own_ref[jnp.minimum(at, count - 1)]
        far = next_ref[jnp.maximum(at - count, 0)]
        amp = jnp.where(at < count, own, far)
        inter = inter_ref[n]
        mixed = jnp.dot(inter, amp, preferred_element_type=F32).astype(BF16)
        total = total + lax.dot_general(
            mixed, inter, (((1,), (1,)), ((), ())), preferred_element_type=F32
        )
    out_ref[...] = total


def coupling(near, own, following, inter, ints):
    return pl.pallas_call(
        coupling_kernel,
        in_specs=[smem_spec()] + [vmem_spec()] * 4,
        out_specs=vmem_spec(),
        out_shape=jax.ShapeDtypeStruct(ints.shape, F32),
        compiler_params=params(32),
        name="coupling",
    )(near, own, following, inter, ints)


def update_kernel(atoms, rest_ref, terms_ref, across_ref, down_ref, shift, out_ref):
    total = rest_ref[...]
    for j in range(atoms.shape[0]):
        total = total + terms_ref[atoms[j]].astype(F32)
    denominator = down_ref[...] + across_ref[...] + shift[0]
    out_ref[...] = (-total / denominator).astype(out_ref.dtype)


def update_pair(atoms, rest, terms, across, down, shift, dtype):
    return pl.pallas_call(
        update_kernel,
        in_specs=[smem_spec()] + [vmem_spec()] * 4 + [smem_spec()],
        out_specs=vmem_spec(),
        out_shape=jax.ShapeDtypeStruct(rest.shape, dtype),
        compiler_params=params(32),
        name="update",
    )(atoms, rest, terms, across, down, shift)


def on_device(
    amplitudes,
    bases,
    factors,
    intersections,
    pair_integrals,
    pno_energies,
    pair_shift,
    pair_atoms,
    pair_next,
):
    me = lax.axis_index("dev")
    count = lax.axis_size("dev")
    listed = jnp.any(pair_atoms == me, axis=1)
    order = jnp.sort(jnp.where(listed, jnp.arange(count), count))[:CAP].astype(jnp.int32)
    pairs = jnp.where(order < count, order, -1)
    slots = jnp.where(order < count, order ^ me, 0)
    near = pair_next[0]
    near = jnp.where(near < count, near ^ me, ((near - count) ^ me) + count)
    atoms = pair_atoms[me]
    across = pno_energies
    down = pno_energies.reshape(-1, 1)
    inter = intersections[0]
    ints = pair_integrals[0]

    group_bases = gather_xor(bases, "dev")
    group_amps = gather_xor(amplitudes, "dev")
    projected = project(slots, group_bases, factors[0])
    for iteration in range(ITERS):
        terms = ladder(slots, pairs, group_amps, projected)
        arrived = lax.all_to_all(terms, "dev", split_axis=0, concat_axis=0, tiled=True)
        next_amps = from_next(group_amps, "grp")
        rest = coupling(near, group_amps, next_amps, inter, ints)
        last = iteration + 1 == ITERS
        update = update_pair(
            atoms, rest, arrived, across, down, pair_shift, F32 if last else BF16
        )
        if not last:
            group_amps = gather_xor(update[None], "dev")
    return update[None]


def solution(mesh):
    return jax.shard_map(
        on_device,
        mesh=mesh,
        in_specs=(
            P(("grp", "dev"), None, None),
            P(("grp", "dev"), None, None),
            P(("grp", "dev"), None, None, None),
            P(("grp", "dev"), None, None, None),
            P(("grp", "dev"), None, None),
            P(("grp", "dev"), None),
            P(("grp", "dev")),
            P("grp", None),
            P(("grp", "dev"), None),
        ),
        out_specs=P(("grp", "dev"), None, None),
        check_vma=False,
    )
```

```python
import functools

import jax
import jax.numpy as jnp
from jax import lax
from jax.experimental import pallas as pl
from jax.experimental.pallas import tpu as pltpu
from jax.sharding import PartitionSpec as P

CAP = 3
ITERS = 2
F32 = jnp.float32
BF16 = jnp.bfloat16


def vmem_spec():
    return pl.BlockSpec(memory_space=pltpu.VMEM)


def smem_spec():
    return pl.BlockSpec(memory_space=pltpu.SMEM)


def params(mib):
    return pltpu.CompilerParams(vmem_limit_bytes=mib * 2**20)


def gather_group(value, axis):
    count = lax.axis_size(axis)
    spread = jnp.broadcast_to(value, (count,) + value.shape[1:])
    return lax.all_to_all(spread, axis, split_axis=0, concat_axis=0, tiled=True)


def from_next(value, axis):
    count = lax.axis_size(axis)
    return lax.ppermute(value, axis, [(d, d - 1) for d in range(1, count)])


def project_kernel(slots, bases_ref, factors_ref, out_ref, wide, narrow, half):
    aux, width, npno = factors_ref.shape[0], bases_ref.shape[1], bases_ref.shape[2]

    @pl.when(pl.program_id(0) == 0)
    def _():
        for s in range(CAP):
            base = bases_ref[slots[s]]
            narrow[s] = base
            wide[pl.ds(s * npno, npno), :] = base.astype(F32).T.astype(BF16)

    for k in range(aux):
        left = jnp.dot(wide[...], factors_ref[k], preferred_element_type=F32).astype(BF16)
        for s in range(CAP):
            half[s, pl.ds(k * npno, npno), :] = left[s * npno : (s + 1) * npno]
    for s in range(CAP):
        both = jnp.dot(half[s], narrow[s], preferred_element_type=F32).astype(BF16)
        for k in range(aux):
            out_ref[s, k // 2, :, pl.ds((k % 2) * npno, npno)] = both[k * npno : (k + 1) * npno]


def project(slots, group_bases, factor_block, step=8):
    aux, width, _ = factor_block.shape
    count, _, npno = group_bases.shape
    step = min(step, aux)
    return pl.pallas_call(
        project_kernel,
        grid=(aux // step,),
        in_specs=[
            smem_spec(),
            pl.BlockSpec((count, width, npno), lambda i: (0, 0, 0)),
            pl.BlockSpec((step, width, width), lambda i: (i, 0, 0)),
        ],
        out_specs=pl.BlockSpec((CAP, step // 2, npno, 2 * npno), lambda i: (0, i, 0, 0)),
        out_shape=jax.ShapeDtypeStruct((CAP, aux // 2, npno, 2 * npno), BF16),
        scratch_shapes=[
            pltpu.VMEM((CAP * npno, width), BF16),
            pltpu.VMEM((CAP, width, npno), BF16),
            pltpu.VMEM((CAP, step * npno, width), BF16),
        ],
        compiler_params=params(48),
        cost_estimate=pl.CostEstimate(
            flops=4 * CAP * aux * npno * width * (width + npno) // 2,
            bytes_accessed=2 * aux * width * width,
            transcendentals=0,
        ),
        name="project",
    )(slots, group_bases, factor_block)


def ladder_kernel(slots, pairs, amps_ref, proj_ref, out_ref, twice, mixed):
    half, npno = proj_ref.shape[1], proj_ref.shape[2]
    twice[...] = jnp.zeros_like(twice)
    for s in range(CAP):
        amp = amps_ref[slots[s]]
        twice[pl.ds(0, npno), pl.ds(0, npno)] = amp
        twice[pl.ds(npno, npno), pl.ds(npno, npno)] = amp
        flat = proj_ref[s].reshape(half * npno, 2 * npno)
        mixed[...] = jnp.dot(flat, twice[...], preferred_element_type=F32).astype(BF16)
        total = jnp.zeros((npno, npno), F32)
        for m in range(half):
            total = total + lax.dot_general(
                mixed[pl.ds(m * npno, npno), :],
                proj_ref[s, m],
                (((1,), (1,)), ((), ())),
                preferred_element_type=F32,
            )

        @pl.when(pairs[s] >= 0)
        def _():
            out_ref[jnp.maximum(pairs[s], 0)] = total.astype(BF16)


def ladder(slots, pairs, group_amps, projected):
    count, npno, _ = group_amps.shape
    half = projected.shape[1]
    return pl.pallas_call(
        ladder_kernel,
        in_specs=[smem_spec(), smem_spec(), vmem_spec(), vmem_spec()],
        out_specs=vmem_spec(),
        out_shape=jax.ShapeDtypeStruct((count, npno, npno), BF16),
        scratch_shapes=[
            pltpu.VMEM((2 * npno, 2 * npno), BF16),
            pltpu.VMEM((half * npno, 2 * npno), BF16),
        ],
        compiler_params=params(32),
        cost_estimate=pl.CostEstimate(
            flops=12 * CAP * half * npno**3,
            bytes_accessed=4 * CAP * half * npno**2,
            transcendentals=0,
        ),
        name="ladder",
    )(slots, pairs, group_amps, projected)


def coupling_kernel(near, own_ref, next_ref, inter_ref, ints_ref, out_ref):
    count = own_ref.shape[0]
    total = ints_ref[...]
    for n in range(inter_ref.shape[0]):
        at = near[n]
        own = own_ref[jnp.minimum(at, count - 1)]
        far = next_ref[jnp.maximum(at - count, 0)]
        amp = jnp.where(at < count, own, far)
        inter = inter_ref[n]
        mixed = jnp.dot(inter, amp, preferred_element_type=F32).astype(BF16)
        total = total + lax.dot_general(
            mixed, inter, (((1,), (1,)), ((), ())), preferred_element_type=F32
        )
    out_ref[...] = total


def coupling(near, own, following, inter, ints):
    return pl.pallas_call(
        coupling_kernel,
        in_specs=[smem_spec()] + [vmem_spec()] * 4,
        out_specs=vmem_spec(),
        out_shape=jax.ShapeDtypeStruct(ints.shape, F32),
        compiler_params=params(32),
        name="coupling",
    )(near, own, following, inter, ints)


def update_kernel(atoms, rest_ref, terms_ref, across_ref, down_ref, shift, out_ref):
    total = rest_ref[...]
    for j in range(atoms.shape[0]):
        total = total + terms_ref[atoms[j]].astype(F32)
    denominator = down_ref[...] + across_ref[...] + shift[0]
    out_ref[...] = (-total / denominator).astype(out_ref.dtype)


def update_pair(atoms, rest, terms, across, down, shift, dtype):
    return pl.pallas_call(
        update_kernel,
        in_specs=[smem_spec()] + [vmem_spec()] * 4 + [smem_spec()],
        out_specs=vmem_spec(),
        out_shape=jax.ShapeDtypeStruct(rest.shape, dtype),
        compiler_params=params(32),
        name="update",
    )(atoms, rest, terms, across, down, shift)


def on_device(
    amplitudes,
    bases,
    factors,
    intersections,
    pair_integrals,
    pno_energies,
    pair_shift,
    pair_atoms,
    pair_next,
):
    me = lax.axis_index("dev")
    count = lax.axis_size("dev")
    listed = jnp.any(pair_atoms == me, axis=1)
    order = jnp.sort(jnp.where(listed, jnp.arange(count), count))[:CAP].astype(jnp.int32)
    pairs = jnp.where(order < count, order, -1)
    slots = jnp.where(order < count, order, 0)
    near = pair_next[0]
    atoms = pair_atoms[me]
    across = pno_energies
    down = pno_energies.reshape(-1, 1)
    inter = intersections[0]
    ints = pair_integrals[0]

    group_bases = gather_group(bases, "dev")
    group_amps = gather_group(amplitudes, "dev")
    projected = project(slots, group_bases, factors[0])
    for iteration in range(ITERS):
        terms = ladder(slots, pairs, group_amps, projected)
        arrived = lax.all_to_all(terms, "dev", split_axis=0, concat_axis=0, tiled=True)
        next_amps = from_next(group_amps, "grp")
        rest = coupling(near, group_amps, next_amps, inter, ints)
        last = iteration + 1 == ITERS
        update = update_pair(
            atoms, rest, arrived, across, down, pair_shift, F32 if last else BF16
        )
        if not last:
            group_amps = gather_group(update[None], "dev")
    return update[None]


def solution(mesh):
    return jax.shard_map(
        on_device,
        mesh=mesh,
        in_specs=(
            P(("grp", "dev"), None, None),
            P(("grp", "dev"), None, None),
            P(("grp", "dev"), None, None, None),
            P(("grp", "dev"), None, None, None),
            P(("grp", "dev"), None, None),
            P(("grp", "dev"), None),
            P(("grp", "dev")),
            P("grp", None),
            P(("grp", "dev"), None),
        ),
        out_specs=P(("grp", "dev"), None, None),
        check_vma=False,
    )
```

```python
import jax
import jax.numpy as jnp
from jax import lax
from jax.experimental import pallas as pl
from jax.experimental.pallas import tpu as pltpu
from jax.sharding import PartitionSpec as P

CAP = 3
ITERS = 2
F32 = jnp.float32
BF16 = jnp.bfloat16


def vmem_spec():
    return pl.BlockSpec(memory_space=pltpu.VMEM)


def smem_spec():
    return pl.BlockSpec(memory_space=pltpu.SMEM)


def params(mib):
    return pltpu.CompilerParams(vmem_limit_bytes=mib * 2**20)


def exchange(value, axis, offset):
    count = lax.axis_size(axis)
    return lax.ppermute(value, axis, [(d, d ^ offset) for d in range(count)])


def gather_relay(value, axis):
    count = lax.axis_size(axis)
    half = count // 2
    found = [value] + [None] * (count - 1)
    for j in range(half, 0, -1):
        found[j] = exchange(value, axis, j)
    for j in range(half + 1, count):
        found[j] = exchange(found[half], axis, j - half)
    return found


def gather_group(value, axis):
    count = lax.axis_size(axis)
    spread = jnp.broadcast_to(value, (count,) + value.shape[1:])
    return lax.all_to_all(spread, axis, split_axis=0, concat_axis=0, tiled=True)


def from_next(value, axis):
    count = lax.axis_size(axis)
    return lax.ppermute(value, axis, [(d, d - 1) for d in range(1, count)])


def project_kernel(count, slots, *refs):
    base_refs, (factors_ref, out_ref, wide, narrow, half) = refs[:count], refs[count:]
    aux, npno = factors_ref.shape[0], narrow.shape[2]

    @pl.when(pl.program_id(0) == 0)
    def _():
        for s in range(CAP):
            for j in range(count):

                @pl.when(slots[s] == j)
                def _():
                    narrow[s] = base_refs[j][0]

            wide[pl.ds(s * npno, npno), :] = narrow[s].astype(F32).T.astype(BF16)

    for k in range(aux):
        left = jnp.dot(wide[...], factors_ref[k], preferred_element_type=F32).astype(BF16)
        for s in range(CAP):
            half[s, pl.ds(k * npno, npno), :] = left[s * npno : (s + 1) * npno]
    for s in range(CAP):
        both = jnp.dot(half[s], narrow[s], preferred_element_type=F32).astype(BF16)
        for k in range(aux):
            out_ref[s, k // 2, :, pl.ds((k % 2) * npno, npno)] = both[k * npno : (k + 1) * npno]


def project(slots, group_bases, factor_block, step=8):
    aux, width, _ = factor_block.shape
    count = len(group_bases)
    npno = group_bases[0].shape[2]
    step = min(step, aux)

    def kernel(*refs):
        project_kernel(count, *refs)

    return pl.pallas_call(
        kernel,
        grid=(aux // step,),
        in_specs=[smem_spec()]
        + [pl.BlockSpec((1, width, npno), lambda i: (0, 0, 0))] * count
        + [pl.BlockSpec((step, width, width), lambda i: (i, 0, 0))],
        out_specs=pl.BlockSpec((CAP, step // 2, npno, 2 * npno), lambda i: (0, i, 0, 0)),
        out_shape=jax.ShapeDtypeStruct((CAP, aux // 2, npno, 2 * npno), BF16),
        scratch_shapes=[
            pltpu.VMEM((CAP * npno, width), BF16),
            pltpu.VMEM((CAP, width, npno), BF16),
            pltpu.VMEM((CAP, step * npno, width), BF16),
        ],
        compiler_params=params(48),
        cost_estimate=pl.CostEstimate(
            flops=4 * CAP * aux * npno * width * (width + npno) // 2,
            bytes_accessed=2 * aux * width * width,
            transcendentals=0,
        ),
        name="project",
    )(slots, *group_bases, factor_block)


def ladder_kernel(count, given, slots, pairs, *refs):
    amp_refs, proj_ref, out_refs = refs[:given], refs[given], refs[given + 1 : given + count + 1]
    twice, mixed = refs[given + count + 1 :]
    half, npno = proj_ref.shape[1], proj_ref.shape[2]
    twice[...] = jnp.zeros_like(twice)
    for s in range(CAP):
        for j in range(given):

            @pl.when((slots[s] == j) | (given == 1))
            def _():
                amp = amp_refs[j][pairs[s] if given == 1 else 0]
                twice[pl.ds(0, npno), pl.ds(0, npno)] = amp
                twice[pl.ds(npno, npno), pl.ds(npno, npno)] = amp

        flat = proj_ref[s].reshape(half * npno, 2 * npno)
        mixed[...] = jnp.dot(flat, twice[...], preferred_element_type=F32).astype(BF16)
        total = jnp.zeros((npno, npno), F32)
        for m in range(half):
            total = total + lax.dot_general(
                mixed[pl.ds(m * npno, npno), :],
                proj_ref[s, m],
                (((1,), (1,)), ((), ())),
                preferred_element_type=F32,
            )
        narrow = total.astype(BF16)
        for j in range(count):

            @pl.when(slots[s] == j)
            def _():
                out_refs[j][0] = narrow


def ladder(count, slots, pairs, group_amps, projected):
    given = len(group_amps)
    npno = group_amps[0].shape[1]
    half = projected.shape[1]

    def kernel(*refs):
        ladder_kernel(count, given, *refs)

    return pl.pallas_call(
        kernel,
        in_specs=[smem_spec()] * 2 + [vmem_spec()] * (given + 1),
        out_specs=[vmem_spec()] * count,
        out_shape=[jax.ShapeDtypeStruct((1, npno, npno), BF16)] * count,
        scratch_shapes=[
            pltpu.VMEM((2 * npno, 2 * npno), BF16),
            pltpu.VMEM((half * npno, 2 * npno), BF16),
        ],
        compiler_params=params(16),
        cost_estimate=pl.CostEstimate(
            flops=12 * CAP * half * npno**3,
            bytes_accessed=4 * CAP * half * npno**2,
            transcendentals=0,
        ),
        name="ladder",
    )(slots, pairs, *group_amps, projected)


def coupling_kernel(near, own_ref, next_ref, inter_ref, ints_ref, out_ref):
    count = own_ref.shape[0]
    total = ints_ref[...]
    for n in range(inter_ref.shape[0]):
        at = near[n]
        own = own_ref[jnp.minimum(at, count - 1)]
        far = next_ref[jnp.maximum(at - count, 0)]
        amp = jnp.where(at < count, own, far)
        inter = inter_ref[n]
        mixed = jnp.dot(inter, amp, preferred_element_type=F32).astype(BF16)
        total = total + lax.dot_general(
            mixed, inter, (((1,), (1,)), ((), ())), preferred_element_type=F32
        )
    out_ref[...] = total


def coupling(near, own, following, inter, ints):
    return pl.pallas_call(
        coupling_kernel,
        in_specs=[smem_spec()] + [vmem_spec()] * 4,
        out_specs=vmem_spec(),
        out_shape=jax.ShapeDtypeStruct(ints.shape, F32),
        compiler_params=params(16),
        name="coupling",
    )(near, own, following, inter, ints)


def update_kernel(count, atoms, *refs):
    term_refs, (rest_ref, across_ref, down_ref, shift, out_ref, total) = refs[:count], refs[count:]
    total[...] = rest_ref[...]
    for t in range(atoms.shape[0]):
        for j in range(count):

            @pl.when(atoms[t] == j)
            def _():
                total[...] += term_refs[j][0].astype(F32)

    denominator = down_ref[...] + across_ref[...] + shift[0]
    out_ref[...] = (-total[...] / denominator).astype(out_ref.dtype)


def update_pair(atoms, terms, rest, across, down, shift, dtype):
    count = len(terms)

    def kernel(*refs):
        update_kernel(count, *refs)

    return pl.pallas_call(
        kernel,
        in_specs=[smem_spec()] + [vmem_spec()] * (count + 3) + [smem_spec()],
        out_specs=vmem_spec(),
        out_shape=jax.ShapeDtypeStruct(rest.shape, dtype),
        scratch_shapes=[pltpu.VMEM(rest.shape, F32)],
        compiler_params=params(16),
        name="update",
    )(atoms, *terms, rest, across, down, shift)


def on_device(
    amplitudes,
    bases,
    factors,
    intersections,
    pair_integrals,
    pno_energies,
    pair_shift,
    pair_atoms,
    pair_next,
):
    me = lax.axis_index("dev")
    count = lax.axis_size("dev")
    listed = jnp.any(pair_atoms == me, axis=1)
    order = jnp.sort(jnp.where(listed, jnp.arange(count), count))[:CAP].astype(jnp.int32)
    slots = jnp.where(order < count, order ^ me, count)
    pairs = jnp.minimum(order, count - 1)
    atoms = pair_atoms[me] ^ me
    across = pno_energies
    down = pno_energies.reshape(-1, 1)
    inter = intersections[0]
    ints = pair_integrals[0]

    group_bases = gather_relay(bases, "dev")
    first, group_bases[count // 2] = lax.optimization_barrier(
        (amplitudes, group_bases[count // 2])
    )
    stacked = gather_group(first, "dev")
    near = pair_next[0]
    group_amps = [stacked]
    projected = project(slots, group_bases, factors[0])
    for iteration in range(ITERS):
        terms = ladder(count, slots, pairs, group_amps, projected)
        arrived = [terms[0]] + [exchange(terms[j], "dev", j) for j in range(1, count)]
        following = from_next(stacked, "grp")
        rest = coupling(near, stacked, following, inter, ints)
        last = iteration + 1 == ITERS
        update = update_pair(
            atoms, arrived, rest, across, down, pair_shift, F32 if last else BF16
        )
        if not last:
            group_amps = gather_relay(update[None], "dev")
            stacked = jnp.concatenate(group_amps, axis=0)
            near = jnp.where(near < count, near ^ me, ((near - count) ^ me) + count)
    return update[None]


def solution(mesh):
    return jax.shard_map(
        on_device,
        mesh=mesh,
        in_specs=(
            P(("grp", "dev"), None, None),
            P(("grp", "dev"), None, None),
            P(("grp", "dev"), None, None, None),
            P(("grp", "dev"), None, None, None),
            P(("grp", "dev"), None, None),
            P(("grp", "dev"), None),
            P(("grp", "dev")),
            P("grp", None),
            P(("grp", "dev"), None),
        ),
        out_specs=P(("grp", "dev"), None, None),
        check_vma=False,
    )
```

```python
import jax
import jax.numpy as jnp
from jax import lax
from jax.experimental import pallas as pl
from jax.experimental.pallas import tpu as pltpu
from jax.sharding import PartitionSpec as P

CAP = 3
ITERS = 2
F32 = jnp.float32
BF16 = jnp.bfloat16


def vmem_spec():
    return pl.BlockSpec(memory_space=pltpu.VMEM)


def smem_spec():
    return pl.BlockSpec(memory_space=pltpu.SMEM)


def params(mib):
    return pltpu.CompilerParams(vmem_limit_bytes=mib * 2**20)


def exchange(value, axis, offset):
    count = lax.axis_size(axis)
    return lax.ppermute(value, axis, [(d, d ^ offset) for d in range(count)])


def gather_across(value, axis):
    other = exchange(value, axis, lax.axis_size(axis) // 2)
    return jnp.concatenate([value, other], axis=0)


def gather_near(pair, axis):
    half = lax.axis_size(axis) // 2
    return [pair] + [exchange(pair, axis, j) for j in range(1, half)]


def from_next(value, axis):
    count = lax.axis_size(axis)
    return lax.ppermute(value, axis, [(d, d - 1) for d in range(1, count)])


def project_kernel(given, slots, *refs):
    base_refs, (factors_ref, out_ref, wide, narrow, half) = refs[:given], refs[given:]
    aux, npno = factors_ref.shape[0], narrow.shape[2]

    @pl.when(pl.program_id(0) == 0)
    def _():
        for s in range(CAP):
            for j in range(given):

                @pl.when(lax.rem(slots[s], given) == j)
                def _():
                    narrow[s] = base_refs[j][slots[s] // given]

            wide[pl.ds(s * npno, npno), :] = narrow[s].astype(F32).T.astype(BF16)

    for k in range(aux):
        left = jnp.dot(wide[...], factors_ref[k], preferred_element_type=F32).astype(BF16)
        for s in range(CAP):
            half[s, pl.ds(k * npno, npno), :] = left[s * npno : (s + 1) * npno]
    for s in range(CAP):
        both = jnp.dot(half[s], narrow[s], preferred_element_type=F32).astype(BF16)
        for k in range(aux):
            out_ref[s, k // 2, :, pl.ds((k % 2) * npno, npno)] = both[k * npno : (k + 1) * npno]


def project(slots, group_bases, factor_block, step=8):
    aux, width, _ = factor_block.shape
    given = len(group_bases)
    npno = group_bases[0].shape[2]
    step = min(step, aux)

    def kernel(*refs):
        project_kernel(given, *refs)

    return pl.pallas_call(
        kernel,
        grid=(aux // step,),
        in_specs=[smem_spec()]
        + [pl.BlockSpec((2, width, npno), lambda i: (0, 0, 0))] * given
        + [pl.BlockSpec((step, width, width), lambda i: (i, 0, 0))],
        out_specs=pl.BlockSpec((CAP, step // 2, npno, 2 * npno), lambda i: (0, i, 0, 0)),
        out_shape=jax.ShapeDtypeStruct((CAP, aux // 2, npno, 2 * npno), BF16),
        scratch_shapes=[
            pltpu.VMEM((CAP * npno, width), BF16),
            pltpu.VMEM((CAP, width, npno), BF16),
            pltpu.VMEM((CAP, step * npno, width), BF16),
        ],
        compiler_params=params(48),
        cost_estimate=pl.CostEstimate(
            flops=4 * CAP * aux * npno * width * (width + npno) // 2,
            bytes_accessed=2 * aux * width * width,
            transcendentals=0,
        ),
        name="project",
    )(slots, *group_bases, factor_block)


def ladder_kernel(given, slots, pairs, *refs):
    amp_refs, (proj_ref, out_ref, twice, mixed, narrow, sems) = refs[:given], refs[given:]
    half, npno = proj_ref.shape[1], proj_ref.shape[2]
    s = pl.program_id(0)

    @pl.when(s == 0)
    def _():
        twice[...] = jnp.zeros_like(twice)

    for j in range(given):

        @pl.when(lax.rem(slots[s], given) == j)
        def _():
            amp = amp_refs[j][slots[s] // given]
            twice[pl.ds(0, npno), pl.ds(0, npno)] = amp
            twice[pl.ds(npno, npno), pl.ds(npno, npno)] = amp

    flat = proj_ref[0].reshape(half * npno, 2 * npno)
    mixed[...] = jnp.dot(flat, twice[...], preferred_element_type=F32).astype(BF16)
    total = jnp.zeros((npno, npno), F32)
    for m in range(half):
        total = total + lax.dot_general(
            mixed[pl.ds(m * npno, npno), :],
            proj_ref[0, m],
            (((1,), (1,)), ((), ())),
            preferred_element_type=F32,
        )
    narrow[s] = total.astype(BF16)

    def copy(t):
        return pltpu.make_async_copy(narrow.at[t], out_ref.at[jnp.maximum(pairs[t], 0)], sems.at[t])

    @pl.when(pairs[s] >= 0)
    def _():
        copy(s).start()

    @pl.when(s == CAP - 1)
    def _():
        for t in range(CAP):

            @pl.when(pairs[t] >= 0)
            def _():
                copy(t).wait()


def ladder(count, slots, pairs, group_amps, projected):
    given = len(group_amps)
    npno = group_amps[0].shape[1]
    half = projected.shape[1]

    def kernel(*refs):
        ladder_kernel(given, *refs)

    return pl.pallas_call(
        kernel,
        grid=(CAP,),
        in_specs=[smem_spec()] * 2
        + [pl.BlockSpec(group_amps[0].shape, lambda s: (0, 0, 0))] * given
        + [pl.BlockSpec((1, half, npno, 2 * npno), lambda s: (s, 0, 0, 0))],
        out_specs=pl.BlockSpec(memory_space=pl.ANY),
        out_shape=jax.ShapeDtypeStruct((count, npno, npno), BF16),
        scratch_shapes=[
            pltpu.VMEM((2 * npno, 2 * npno), BF16),
            pltpu.VMEM((half * npno, 2 * npno), BF16),
            pltpu.VMEM((CAP, npno, npno), BF16),
            pltpu.SemaphoreType.DMA((CAP,)),
        ],
        compiler_params=params(24),
        cost_estimate=pl.CostEstimate(
            flops=0,
            bytes_accessed=16 * CAP * half * npno**2,
            transcendentals=0,
        ),
        name="ladder",
    )(slots, pairs, *group_amps, projected)


def coupling_kernel(near, own_ref, next_ref, inter_ref, ints_ref, out_ref):
    count = own_ref.shape[0]
    total = ints_ref[...]
    for n in range(inter_ref.shape[0]):
        at = near[n]
        own = own_ref[jnp.minimum(at, count - 1)]
        far = next_ref[jnp.maximum(at - count, 0)]
        amp = jnp.where(at < count, own, far)
        inter = inter_ref[n]
        mixed = jnp.dot(inter, amp, preferred_element_type=F32).astype(BF16)
        total = total + lax.dot_general(
            mixed, inter, (((1,), (1,)), ((), ())), preferred_element_type=F32
        )
    out_ref[...] = total


def coupling(near, own, following, inter, ints):
    return pl.pallas_call(
        coupling_kernel,
        in_specs=[smem_spec()] + [vmem_spec()] * 4,
        out_specs=vmem_spec(),
        out_shape=jax.ShapeDtypeStruct(ints.shape, F32),
        compiler_params=params(16),
        name="coupling",
    )(near, own, following, inter, ints)


def update_kernel(atoms, terms_ref, rest_ref, across_ref, down_ref, shift, out_ref):
    total = rest_ref[...]
    for t in range(atoms.shape[0]):
        total = total + terms_ref[atoms[t]].astype(F32)
    denominator = down_ref[...] + across_ref[...] + shift[0]
    out_ref[...] = (-total / denominator).astype(out_ref.dtype)


def update_pair(atoms, terms, rest, across, down, shift, dtype):
    return pl.pallas_call(
        update_kernel,
        in_specs=[smem_spec()] + [vmem_spec()] * 4 + [smem_spec()],
        out_specs=vmem_spec(),
        out_shape=jax.ShapeDtypeStruct(rest.shape, dtype),
        compiler_params=params(16),
        name="update",
    )(atoms, terms, rest, across, down, shift)


def on_device(
    amplitudes,
    bases,
    factors,
    intersections,
    pair_integrals,
    pno_energies,
    pair_shift,
    pair_atoms,
    pair_next,
):
    me = lax.axis_index("dev")
    count = lax.axis_size("dev")
    listed = jnp.any(pair_atoms == me, axis=1)
    order = jnp.sort(jnp.where(listed, jnp.arange(count), count))[:CAP].astype(jnp.int32)
    slots = jnp.where(order < count, order ^ me, 0)
    pairs = jnp.where(order < count, order, -1)
    atoms = pair_atoms[me]
    near = pair_next[0]
    near = jnp.where(near < count, near ^ me, ((near - count) ^ me) + count)
    across = pno_energies
    down = pno_energies.reshape(-1, 1)
    inter = intersections[0]
    ints = pair_integrals[0]

    group_bases = gather_near(gather_across(bases, "dev"), "dev")
    pair_amps, group_bases[1] = lax.optimization_barrier(
        (gather_across(amplitudes, "dev"), group_bases[1])
    )
    group_amps = gather_near(pair_amps, "dev")
    projected = project(slots, group_bases, factors[0])
    for iteration in range(ITERS):
        stacked = jnp.concatenate(
            [g[r : r + 1] for r in range(2) for g in group_amps], axis=0
        )
        following = from_next(stacked, "grp")
        terms = ladder(count, slots, pairs, group_amps, projected)
        terms, following = lax.optimization_barrier((terms, following))
        arrived = lax.all_to_all(terms, "dev", split_axis=0, concat_axis=0, tiled=True)
        rest = coupling(near, stacked, following, inter, ints)
        last = iteration + 1 == ITERS
        update = update_pair(
            atoms, arrived, rest, across, down, pair_shift, F32 if last else BF16
        )
        if not last:
            group_amps = gather_near(gather_across(update[None], "dev"), "dev")
    return update[None]


def solution(mesh):
    return jax.shard_map(
        on_device,
        mesh=mesh,
        in_specs=(
            P(("grp", "dev"), None, None),
            P(("grp", "dev"), None, None),
            P(("grp", "dev"), None, None, None),
            P(("grp", "dev"), None, None, None),
            P(("grp", "dev"), None, None),
            P(("grp", "dev"), None),
            P(("grp", "dev")),
            P("grp", None),
            P(("grp", "dev"), None),
        ),
        out_specs=P(("grp", "dev"), None, None),
        check_vma=False,
    )
```

```python
import jax
import jax.numpy as jnp
from jax import lax
from jax.experimental import pallas as pl
from jax.experimental.pallas import tpu as pltpu
from jax.sharding import PartitionSpec as P

CAP = 3
ITERS = 2
F32 = jnp.float32
BF16 = jnp.bfloat16


def vmem_spec():
    return pl.BlockSpec(memory_space=pltpu.VMEM)


def smem_spec():
    return pl.BlockSpec(memory_space=pltpu.SMEM)


def params(mib):
    return pltpu.CompilerParams(vmem_limit_bytes=mib * 2**20)


def exchange(value, axis, offset):
    count = lax.axis_size(axis)
    return lax.ppermute(value, axis, [(d, d ^ offset) for d in range(count)])


def gather_across(value, axis):
    other = exchange(value, axis, lax.axis_size(axis) // 2)
    return jnp.concatenate([value, other], axis=0)


def gather_near(pair, axis):
    half = lax.axis_size(axis) // 2
    return [pair] + [exchange(pair, axis, j) for j in range(1, half)]


def from_next(value, axis):
    count = lax.axis_size(axis)
    return lax.ppermute(value, axis, [(d, d - 1) for d in range(1, count)])


def project_kernel(given, slots, *refs):
    base_refs, (factors_ref, out_ref, wide, narrow, half) = refs[:given], refs[given:]
    aux, npno = factors_ref.shape[0], narrow.shape[2]

    @pl.when(pl.program_id(0) == 0)
    def _():
        for s in range(CAP):
            for j in range(given):

                @pl.when(lax.rem(slots[s], given) == j)
                def _():
                    narrow[s] = base_refs[j][slots[s] // given]

            wide[pl.ds(s * npno, npno), :] = narrow[s].astype(F32).T.astype(BF16)

    for k in range(aux):
        left = jnp.dot(wide[...], factors_ref[k], preferred_element_type=F32).astype(BF16)
        for s in range(CAP):
            half[s, pl.ds(k * npno, npno), :] = left[s * npno : (s + 1) * npno]
    for s in range(CAP):
        both = jnp.dot(half[s], narrow[s], preferred_element_type=F32).astype(BF16)
        for k in range(aux):
            out_ref[s, k // 2, :, pl.ds((k % 2) * npno, npno)] = both[k * npno : (k + 1) * npno]


def project(slots, group_bases, factor_block, step=8):
    aux, width, _ = factor_block.shape
    given = len(group_bases)
    npno = group_bases[0].shape[2]
    step = min(step, aux)

    def kernel(*refs):
        project_kernel(given, *refs)

    return pl.pallas_call(
        kernel,
        grid=(aux // step,),
        in_specs=[smem_spec()]
        + [pl.BlockSpec((2, width, npno), lambda i: (0, 0, 0))] * given
        + [pl.BlockSpec((step, width, width), lambda i: (i, 0, 0))],
        out_specs=pl.BlockSpec((CAP, step // 2, npno, 2 * npno), lambda i: (0, i, 0, 0)),
        out_shape=jax.ShapeDtypeStruct((CAP, aux // 2, npno, 2 * npno), BF16),
        scratch_shapes=[
            pltpu.VMEM((CAP * npno, width), BF16),
            pltpu.VMEM((CAP, width, npno), BF16),
            pltpu.VMEM((CAP, step * npno, width), BF16),
        ],
        compiler_params=params(48),
        cost_estimate=pl.CostEstimate(
            flops=4 * CAP * aux * npno * width * (width + npno) // 2,
            bytes_accessed=2 * aux * width * width,
            transcendentals=0,
        ),
        name="project",
    )(slots, *group_bases, factor_block)


def ladder_kernel(given, slots, pairs, *refs):
    amp_refs, (proj_ref, out_ref, twice, mixed, narrow, sems) = refs[:given], refs[given:]
    half, npno = proj_ref.shape[1], proj_ref.shape[2]
    s = pl.program_id(0)

    @pl.when(s == 0)
    def _():
        twice[...] = jnp.zeros_like(twice)

    for j in range(given):

        @pl.when(lax.rem(slots[s], given) == j)
        def _():
            amp = amp_refs[j][slots[s] // given]
            twice[pl.ds(0, npno), pl.ds(0, npno)] = amp
            twice[pl.ds(npno, npno), pl.ds(npno, npno)] = amp

    flat = proj_ref[0].reshape(half * npno, 2 * npno)
    mixed[...] = jnp.dot(flat, twice[...], preferred_element_type=F32).astype(BF16)
    total = jnp.zeros((npno, npno), F32)
    for m in range(half):
        total = total + lax.dot_general(
            mixed[pl.ds(m * npno, npno), :],
            proj_ref[0, m],
            (((1,), (1,)), ((), ())),
            preferred_element_type=F32,
        )
    narrow[s] = total.astype(BF16)

    def copy(t):
        return pltpu.make_async_copy(narrow.at[t], out_ref.at[jnp.maximum(pairs[t], 0)], sems.at[t])

    @pl.when(pairs[s] >= 0)
    def _():
        copy(s).start()

    @pl.when(s == CAP - 1)
    def _():
        for t in range(CAP):

            @pl.when(pairs[t] >= 0)
            def _():
                copy(t).wait()


def ladder(count, slots, pairs, group_amps, projected):
    given = len(group_amps)
    npno = group_amps[0].shape[1]
    half = projected.shape[1]

    def kernel(*refs):
        ladder_kernel(given, *refs)

    return pl.pallas_call(
        kernel,
        grid=(CAP,),
        in_specs=[smem_spec()] * 2
        + [pl.BlockSpec(group_amps[0].shape, lambda s: (0, 0, 0))] * given
        + [pl.BlockSpec((1, half, npno, 2 * npno), lambda s: (s, 0, 0, 0))],
        out_specs=pl.BlockSpec(memory_space=pl.ANY),
        out_shape=jax.ShapeDtypeStruct((count, npno, npno), BF16),
        scratch_shapes=[
            pltpu.VMEM((2 * npno, 2 * npno), BF16),
            pltpu.VMEM((half * npno, 2 * npno), BF16),
            pltpu.VMEM((CAP, npno, npno), BF16),
            pltpu.SemaphoreType.DMA((CAP,)),
        ],
        compiler_params=params(24),
        cost_estimate=pl.CostEstimate(
            flops=0,
            bytes_accessed=16 * CAP * half * npno**2,
            transcendentals=0,
        ),
        name="ladder",
    )(slots, pairs, *group_amps, projected)


def coupling_kernel(near, own_ref, next_ref, inter_ref, ints_ref, out_ref):
    count = own_ref.shape[0]
    total = ints_ref[...]
    for n in range(inter_ref.shape[0]):
        at = near[n]
        own = own_ref[jnp.minimum(at, count - 1)]
        far = next_ref[jnp.maximum(at - count, 0)]
        amp = jnp.where(at < count, own, far)
        inter = inter_ref[n]
        mixed = jnp.dot(inter, amp, preferred_element_type=F32).astype(BF16)
        total = total + lax.dot_general(
            mixed, inter, (((1,), (1,)), ((), ())), preferred_element_type=F32
        )
    out_ref[...] = total


def coupling(near, own, following, inter, ints):
    return pl.pallas_call(
        coupling_kernel,
        in_specs=[smem_spec()] + [vmem_spec()] * 4,
        out_specs=vmem_spec(),
        out_shape=jax.ShapeDtypeStruct(ints.shape, F32),
        compiler_params=params(16),
        name="coupling",
    )(near, own, following, inter, ints)


def update_kernel(atoms, terms_ref, rest_ref, across_ref, down_ref, shift, out_ref):
    total = rest_ref[...]
    for t in range(atoms.shape[0]):
        total = total + terms_ref[atoms[t]].astype(F32)
    denominator = down_ref[...] + across_ref[...] + shift[0]
    out_ref[...] = (-total / denominator).astype(out_ref.dtype)


def update_pair(atoms, terms, rest, across, down, shift, dtype):
    return pl.pallas_call(
        update_kernel,
        in_specs=[smem_spec()] + [vmem_spec()] * 4 + [smem_spec()],
        out_specs=vmem_spec(),
        out_shape=jax.ShapeDtypeStruct(rest.shape, dtype),
        compiler_params=params(16),
        name="update",
    )(atoms, terms, rest, across, down, shift)


def on_device(
    amplitudes,
    bases,
    factors,
    intersections,
    pair_integrals,
    pno_energies,
    pair_shift,
    pair_atoms,
    pair_next,
):
    me = lax.axis_index("dev")
    count = lax.axis_size("dev")
    places = jnp.arange(count, dtype=jnp.int32)
    listed = jnp.any(pair_atoms == me, axis=1)
    rank = jnp.sum((places[None, :] < places[:, None]) & listed[None, :], axis=1)
    chosen = listed[None, :] & (rank[None, :] == jnp.arange(CAP)[:, None])
    pairs = jnp.sum(jnp.where(chosen, places[None, :] + 1, 0), axis=1) - 1
    slots = jnp.where(pairs >= 0, pairs ^ me, 0)
    atoms = pair_atoms[me]
    near = pair_next[0]
    near = jnp.where(near < count, near ^ me, ((near - count) ^ me) + count)
    across = pno_energies
    down = pno_energies.reshape(-1, 1)
    inter = intersections[0]
    ints = pair_integrals[0]

    group_bases = gather_near(gather_across(bases, "dev"), "dev")
    first, slots, pairs = lax.optimization_barrier((amplitudes, slots, pairs))
    pair_amps, group_bases[1] = lax.optimization_barrier(
        (gather_across(first, "dev"), group_bases[1])
    )
    group_amps = gather_near(pair_amps, "dev")
    projected = project(slots, group_bases, factors[0])
    group_amps, projected = lax.optimization_barrier((group_amps, projected))
    for iteration in range(ITERS):
        stacked = jnp.concatenate(
            [g[r : r + 1] for r in range(2) for g in group_amps], axis=0
        )
        following = from_next(stacked, "grp")
        terms = ladder(count, slots, pairs, group_amps, projected)
        terms, following = lax.optimization_barrier((terms, following))
        arrived = lax.all_to_all(terms, "dev", split_axis=0, concat_axis=0, tiled=True)
        rest = coupling(near, stacked, following, inter, ints)
        last = iteration + 1 == ITERS
        update = update_pair(
            atoms, arrived, rest, across, down, pair_shift, F32 if last else BF16
        )
        if not last:
            group_amps = gather_near(gather_across(update[None], "dev"), "dev")
    return update[None]


def solution(mesh):
    return jax.shard_map(
        on_device,
        mesh=mesh,
        in_specs=(
            P(("grp", "dev"), None, None),
            P(("grp", "dev"), None, None),
            P(("grp", "dev"), None, None, None),
            P(("grp", "dev"), None, None, None),
            P(("grp", "dev"), None, None),
            P(("grp", "dev"), None),
            P(("grp", "dev")),
            P("grp", None),
            P(("grp", "dev"), None),
        ),
        out_specs=P(("grp", "dev"), None, None),
        check_vma=False,
    )
```

```python
import jax
import jax.numpy as jnp
from jax import lax
from jax.experimental import pallas as pl
from jax.experimental.pallas import tpu as pltpu
from jax.sharding import PartitionSpec as P

CAP = 3
ITERS = 2
F32 = jnp.float32
BF16 = jnp.bfloat16
CONTRACT_LAST = (((1,), (1,)), ((), ()))


def vmem_spec():
    return pl.BlockSpec(memory_space=pltpu.VMEM)


def smem_spec():
    return pl.BlockSpec(memory_space=pltpu.SMEM)


def params(mib):
    return pltpu.CompilerParams(vmem_limit_bytes=mib * 2**20)


def exchange(value, axis, offset):
    count = lax.axis_size(axis)
    return lax.ppermute(value, axis, [(d, d ^ offset) for d in range(count)])


def gather_across(value, axis):
    other = exchange(value, axis, lax.axis_size(axis) // 2)
    return jnp.concatenate([value, other], axis=0)


def gather_near(pair, axis):
    half = lax.axis_size(axis) // 2
    return [pair] + [exchange(pair, axis, j) for j in range(1, half)]


def stack_offsets(found):
    return jnp.concatenate([g[r : r + 1] for r in range(2) for g in found], axis=0)


def from_next(value, axis):
    count = lax.axis_size(axis)
    return lax.ppermute(value, axis, [(d, d - 1) for d in range(1, count)])


def all_to_all(value):
    return lax.all_to_all(value, "dev", split_axis=0, concat_axis=0, tiled=True)


def project_kernel(given, slots, *refs):
    base_refs, (factors_ref, out_ref, wide, narrow, half) = refs[:given], refs[given:]
    aux, npno = factors_ref.shape[0], narrow.shape[2]

    @pl.when(pl.program_id(0) == 0)
    def _():
        for s in range(CAP):
            for j in range(given):

                @pl.when(lax.rem(slots[s], given) == j)
                def _():
                    narrow[s] = base_refs[j][slots[s] // given]

            wide[pl.ds(s * npno, npno), :] = narrow[s].astype(F32).T.astype(BF16)

    for k in range(aux):
        left = jnp.dot(wide[...], factors_ref[k], preferred_element_type=F32).astype(BF16)
        for s in range(CAP):
            half[s, pl.ds(k * npno, npno), :] = left[s * npno : (s + 1) * npno]
    for s in range(CAP):
        both = jnp.dot(half[s], narrow[s], preferred_element_type=F32).astype(BF16)
        for k in range(aux):
            out_ref[s, k // 2, :, pl.ds((k % 2) * npno, npno)] = both[k * npno : (k + 1) * npno]


def project(slots, group_bases, factor_block, step=8):
    aux, width, _ = factor_block.shape
    given = len(group_bases)
    npno = group_bases[0].shape[2]
    step = min(step, aux)

    def kernel(*refs):
        project_kernel(given, *refs)

    return pl.pallas_call(
        kernel,
        grid=(aux // step,),
        in_specs=[smem_spec()]
        + [pl.BlockSpec((2, width, npno), lambda i: (0, 0, 0))] * given
        + [pl.BlockSpec((step, width, width), lambda i: (i, 0, 0))],
        out_specs=pl.BlockSpec((CAP, step // 2, npno, 2 * npno), lambda i: (0, i, 0, 0)),
        out_shape=jax.ShapeDtypeStruct((CAP, aux // 2, npno, 2 * npno), BF16),
        scratch_shapes=[
            pltpu.VMEM((CAP * npno, width), BF16),
            pltpu.VMEM((CAP, width, npno), BF16),
            pltpu.VMEM((CAP, step * npno, width), BF16),
        ],
        compiler_params=params(48),
        cost_estimate=pl.CostEstimate(
            flops=4 * CAP * aux * npno * width * (width + npno) // 2,
            bytes_accessed=2 * aux * width * width,
            transcendentals=0,
        ),
        name="project",
    )(slots, *group_bases, factor_block)


def ladder_kernel(given, spread, chunked, slots, pairs, devices, *refs):
    amp_refs, (proj_ref, out_ref, amp_rows, twice, mixed), tail = (
        refs[:given],
        refs[given : given + 5],
        refs[given + 5 :],
    )
    half, npno = proj_ref.shape[1], proj_ref.shape[2]
    s = pl.program_id(0)

    @pl.when(s == 0)
    def _():
        twice[...] = jnp.zeros_like(twice)

    if chunked:
        pair = jnp.maximum(pairs[s], 0)
        rows = amp_refs[0].shape[2]
        for o in range(2 * given):
            first = pl.multiple_of(devices[o] * rows, rows)
            amp_rows[pl.ds(first, rows), :] = amp_refs[o % given][o // given, pair]
    else:
        for j in range(given):

            @pl.when(lax.rem(slots[s], given) == j)
            def _():
                amp_rows[...] = amp_refs[j][slots[s] // given]

    amp = amp_rows[...]
    twice[pl.ds(0, npno), pl.ds(0, npno)] = amp
    twice[pl.ds(npno, npno), pl.ds(npno, npno)] = amp
    flat = proj_ref[0].reshape(half * npno, 2 * npno)
    mixed[...] = jnp.dot(flat, twice[...], preferred_element_type=F32).astype(BF16)
    total = jnp.zeros((npno, npno), F32)
    for m in range(half):
        total = total + lax.dot_general(
            mixed[pl.ds(m * npno, npno), :],
            proj_ref[0, m],
            CONTRACT_LAST,
            preferred_element_type=F32,
        )
    if not spread:
        out_ref[0] = total.astype(BF16)
        return
    narrow, sems = tail
    narrow[s] = total.astype(BF16)

    def copy(t):
        return pltpu.make_async_copy(narrow.at[t], out_ref.at[jnp.maximum(pairs[t], 0)], sems.at[t])

    @pl.when(pairs[s] >= 0)
    def _():
        copy(s).start()

    @pl.when(s == CAP - 1)
    def _():
        for t in range(CAP):

            @pl.when(pairs[t] >= 0)
            def _():
                copy(t).wait()


def ladder(spread, slots, pairs, devices, group_amps, projected):
    count = devices.shape[0]
    given = len(group_amps)
    chunked = group_amps[0].ndim == 4
    half, npno = projected.shape[1:3]

    def kernel(*refs):
        ladder_kernel(given, spread, chunked, *refs)

    whole = group_amps[0].shape
    scratch = [
        pltpu.VMEM((npno, npno), BF16),
        pltpu.VMEM((2 * npno, 2 * npno), BF16),
        pltpu.VMEM((half * npno, 2 * npno), BF16),
    ]
    if spread:
        scratch += [pltpu.VMEM((CAP, npno, npno), BF16), pltpu.SemaphoreType.DMA((CAP,))]
    return pl.pallas_call(
        kernel,
        grid=(CAP,),
        in_specs=[smem_spec()] * 3
        + [pl.BlockSpec(whole, lambda s: (0,) * len(whole))] * given
        + [pl.BlockSpec((1, half, npno, 2 * npno), lambda s: (s, 0, 0, 0))],
        out_specs=pl.BlockSpec(memory_space=pltpu.HBM)
        if spread
        else pl.BlockSpec((1, npno, npno), lambda s: (s, 0, 0)),
        out_shape=jax.ShapeDtypeStruct((count if spread else CAP, npno, npno), BF16),
        scratch_shapes=scratch,
        compiler_params=params(24),
        cost_estimate=pl.CostEstimate(
            flops=0,
            bytes_accessed=16 * CAP * half * npno**2,
            transcendentals=0,
        ),
        name="ladder",
    )(slots, pairs, devices, *group_amps, projected)


def coupled(near, devices, own_ref, next_ref, inter_ref, total, amp_rows):
    count = own_ref.shape[0]
    for n in range(inter_ref.shape[0]):
        at = near[n]
        low, high = jnp.minimum(at, count - 1), jnp.maximum(at - count, 0)
        if len(own_ref.shape) == 4:
            rows = own_ref.shape[2]
            for o in range(count):
                first = pl.multiple_of(devices[o] * rows, rows)
                amp_rows[pl.ds(first, rows), :] = jnp.where(
                    at < count, own_ref[o, low], next_ref[o, high]
                )
            amp = amp_rows[...]
        else:
            amp = jnp.where(
                at < count, own_ref[low ^ devices[0]], next_ref[high ^ devices[0]]
            )
        inter = inter_ref[n]
        mixed = jnp.dot(inter, amp, preferred_element_type=F32).astype(BF16)
        total = total + lax.dot_general(
            mixed, inter, CONTRACT_LAST, preferred_element_type=F32
        )
    return total


def coupling_kernel(near, devices, own_ref, next_ref, inter_ref, ints_ref, out_ref, amp_rows):
    out_ref[...] = coupled(near, devices, own_ref, next_ref, inter_ref, ints_ref[...], amp_rows)


def coupling(near, devices, own, following, inter, ints):
    return pl.pallas_call(
        coupling_kernel,
        in_specs=[smem_spec()] * 2 + [vmem_spec()] * 4,
        out_specs=vmem_spec(),
        out_shape=jax.ShapeDtypeStruct(ints.shape, F32),
        scratch_shapes=[pltpu.VMEM(ints.shape, BF16)],
        compiler_params=params(16),
        name="coupling",
    )(near, devices, own, following, inter, ints)


def scatter_kernel(
    near, devices, own_ref, next_ref, inter_ref, ints_ref, across, down, shift, terms_ref, out_ref, amp_rows
):
    rest = coupled(near, devices, own_ref, next_ref, inter_ref, ints_ref[...], amp_rows)
    scale = -1.0 / (down[...] + across[...] + shift[0])
    count, _, rows, npno = out_ref.shape
    parts = [terms_ref[s] for s in range(CAP)] + [(rest * scale).astype(BF16), scale.astype(BF16)]
    for t, part in enumerate(parts):
        out_ref[:, t] = part.reshape(count, rows, npno)


def scatter_rows(near, devices, own, following, inter, ints, across, down, shift, terms):
    count, npno = own.shape[0], ints.shape[1]
    return pl.pallas_call(
        scatter_kernel,
        in_specs=[smem_spec()] * 2 + [vmem_spec()] * 6 + [smem_spec(), vmem_spec()],
        out_specs=vmem_spec(),
        out_shape=jax.ShapeDtypeStruct((count, CAP + 2, npno // count, npno), BF16),
        scratch_shapes=[pltpu.VMEM(ints.shape, BF16)],
        compiler_params=params(16),
        name="scatter_rows",
    )(near, devices, own, following, inter, ints, across, down, shift, terms)


def update_rows_kernel(atoms, ranks, rows_ref, out_ref):
    for p in range(out_ref.shape[0]):
        total = jnp.zeros(out_ref.shape[1:], F32)
        for t in range(atoms.shape[1]):
            total = total + rows_ref[atoms[p, t], ranks[p, t]].astype(F32)
        scale = rows_ref[p, CAP + 1].astype(F32)
        out_ref[p] = (total * scale + rows_ref[p, CAP].astype(F32)).astype(BF16)


def update_rows(atoms, ranks, arrived):
    count, _, rows, npno = arrived.shape
    return pl.pallas_call(
        update_rows_kernel,
        in_specs=[smem_spec()] * 2 + [vmem_spec()],
        out_specs=vmem_spec(),
        out_shape=jax.ShapeDtypeStruct((count, rows, npno), BF16),
        compiler_params=params(16),
        name="update_rows",
    )(atoms, ranks, arrived)


def update_kernel(atoms, terms_ref, rest_ref, across_ref, down_ref, shift, out_ref):
    total = rest_ref[...]
    for t in range(atoms.shape[0]):
        total = total + terms_ref[atoms[t]].astype(F32)
    denominator = down_ref[...] + across_ref[...] + shift[0]
    out_ref[...] = (-total / denominator).astype(out_ref.dtype)


def update_pair(atoms, terms, rest, across, down, shift, dtype):
    return pl.pallas_call(
        update_kernel,
        in_specs=[smem_spec()] + [vmem_spec()] * 4 + [smem_spec()],
        out_specs=vmem_spec(),
        out_shape=jax.ShapeDtypeStruct(rest.shape, dtype),
        compiler_params=params(16),
        name="update",
    )(atoms, terms, rest, across, down, shift)


def on_device(
    amplitudes,
    bases,
    factors,
    intersections,
    pair_integrals,
    pno_energies,
    pair_shift,
    pair_atoms,
    pair_next,
):
    me = lax.axis_index("dev")
    count = lax.axis_size("dev")
    places = jnp.arange(count, dtype=jnp.int32)
    devices = places ^ me
    listed = jnp.any(pair_atoms == me, axis=1)
    before = places[None, :] < places[:, None]
    rank = jnp.sum(before & listed[None, :], axis=1)
    chosen = listed[None, :] & (rank[None, :] == jnp.arange(CAP)[:, None])
    pairs = jnp.sum(jnp.where(chosen, places[None, :] + 1, 0), axis=1) - 1
    slots = jnp.where(pairs >= 0, pairs ^ me, 0)
    same = jnp.any(pair_atoms[:, :, None, None] == pair_atoms[None, None, :, :], axis=3)
    ranks = jnp.sum((before[:, None, :] & same).astype(jnp.int32), axis=2)
    atoms = pair_atoms[me]
    near = pair_next[0]
    across = pno_energies
    down = pno_energies.reshape(-1, 1)
    inter = intersections[0]
    ints = pair_integrals[0]
    chunked = ints.shape[0] % (16 * count) == 0

    group_bases = gather_near(gather_across(bases, "dev"), "dev")
    pair_amps, group_bases[1] = lax.optimization_barrier(
        (gather_across(amplitudes, "dev"), group_bases[1])
    )
    group_amps = gather_near(pair_amps, "dev")
    projected = project(slots, group_bases, factors[0])
    group_amps, projected = lax.optimization_barrier((group_amps, projected))
    for iteration in range(ITERS):
        last = iteration + 1 == ITERS
        stacked = stack_offsets(group_amps)
        following = from_next(stacked, "grp")
        direct = last or not chunked
        terms = ladder(direct, slots, pairs, devices, group_amps, projected)
        if direct:
            arrived = all_to_all(terms)
            rest = coupling(near, devices, stacked, following, inter, ints)
            update = update_pair(
                atoms, arrived, rest, across, down, pair_shift, F32 if last else BF16
            )
        else:
            rows = scatter_rows(
                near, devices, stacked, following, inter, ints, across, down, pair_shift, terms
            )
            update = update_rows(pair_atoms, ranks, all_to_all(rows))
        if not last:
            group_amps = gather_near(gather_across(update[None], "dev"), "dev")
    return update[None]


def solution(mesh):
    return jax.shard_map(
        on_device,
        mesh=mesh,
        in_specs=(
            P(("grp", "dev"), None, None),
            P(("grp", "dev"), None, None),
            P(("grp", "dev"), None, None, None),
            P(("grp", "dev"), None, None, None),
            P(("grp", "dev"), None, None),
            P(("grp", "dev"), None),
            P(("grp", "dev")),
            P("grp", None),
            P(("grp", "dev"), None),
        ),
        out_specs=P(("grp", "dev"), None, None),
        check_vma=False,
    )
```

```python
import jax
import jax.numpy as jnp
from jax import lax
from jax.experimental import pallas as pl
from jax.experimental.pallas import tpu as pltpu
from jax.sharding import PartitionSpec as P

CAP = 3
ITERS = 2
F32 = jnp.float32
BF16 = jnp.bfloat16
CONTRACT_LAST = (((1,), (1,)), ((), ()))


def vmem_spec():
    return pl.BlockSpec(memory_space=pltpu.VMEM)


def smem_spec():
    return pl.BlockSpec(memory_space=pltpu.SMEM)


def params(mib):
    return pltpu.CompilerParams(vmem_limit_bytes=mib * 2**20)


def exchange(value, axis, offset):
    count = lax.axis_size(axis)
    return lax.ppermute(value, axis, [(d, d ^ offset) for d in range(count)])


def opposite(axis):
    return 3 * lax.axis_size(axis) // 4


def gather_across(value, axis):
    return jnp.concatenate([value, exchange(value, axis, opposite(axis))], axis=0)


def exchange_near(entries, axis):
    return [entries[0]] + [exchange(entries[j], axis, j) for j in range(1, len(entries))]


def gather_near(pair, axis):
    return exchange_near([pair] * (lax.axis_size(axis) // 2), axis)


def place_of(device, axis):
    half = lax.axis_size(axis) // 2
    offset = device ^ lax.axis_index(axis)
    return jnp.where(offset < half, offset, half + (offset ^ opposite(axis)))


def from_next(value, axis):
    count = lax.axis_size(axis)
    return lax.ppermute(value, axis, [(d, d - 1) for d in range(1, count)])


def stack_kernel(*refs):
    entries, out_ref = refs[:-1], refs[-1]
    for j, entry in enumerate(entries):
        for r in range(2):
            out_ref[r * len(entries) + j] = entry[r]


def stack(entries):
    _, rows, columns = entries[0].shape
    return pl.pallas_call(
        stack_kernel,
        in_specs=[vmem_spec()] * len(entries),
        out_specs=vmem_spec(),
        out_shape=jax.ShapeDtypeStruct((2 * len(entries), rows, columns), entries[0].dtype),
        compiler_params=params(16),
        name="stack",
    )(*entries)


def project_kernel(given, slots, *refs):
    base_refs, (factors_ref, out_ref, wide, narrow, half) = refs[:given], refs[given:]
    aux, npno = factors_ref.shape[0], narrow.shape[2]

    @pl.when(pl.program_id(0) == 0)
    def _():
        for s in range(CAP):
            for j in range(given):

                @pl.when(lax.rem(slots[s], given) == j)
                def _():
                    narrow[s] = base_refs[j][slots[s] // given]

            wide[pl.ds(s * npno, npno), :] = narrow[s].astype(F32).T.astype(BF16)

    for k in range(aux):
        left = jnp.dot(wide[...], factors_ref[k], preferred_element_type=F32).astype(BF16)
        for s in range(CAP):
            half[s, pl.ds(k * npno, npno), :] = left[s * npno : (s + 1) * npno]
    for s in range(CAP):
        both = jnp.dot(half[s], narrow[s], preferred_element_type=F32).astype(BF16)
        for k in range(aux):
            out_ref[s, k // 2, :, pl.ds((k % 2) * npno, npno)] = both[k * npno : (k + 1) * npno]


def project(slots, group_bases, factor_block, step=8):
    aux, width, _ = factor_block.shape
    given = len(group_bases)
    npno = group_bases[0].shape[2]
    step = min(step, aux)

    def kernel(*refs):
        project_kernel(given, *refs)

    return pl.pallas_call(
        kernel,
        grid=(aux // step,),
        in_specs=[smem_spec()]
        + [pl.BlockSpec((2, width, npno), lambda i: (0, 0, 0))] * given
        + [pl.BlockSpec((step, width, width), lambda i: (i, 0, 0))],
        out_specs=pl.BlockSpec((CAP, step // 2, npno, 2 * npno), lambda i: (0, i, 0, 0)),
        out_shape=jax.ShapeDtypeStruct((CAP, aux // 2, npno, 2 * npno), BF16),
        scratch_shapes=[
            pltpu.VMEM((CAP * npno, width), BF16),
            pltpu.VMEM((CAP, width, npno), BF16),
            pltpu.VMEM((CAP, step * npno, width), BF16),
        ],
        compiler_params=params(48),
        cost_estimate=pl.CostEstimate(
            flops=4 * CAP * aux * npno * width * (width + npno) // 2,
            bytes_accessed=2 * aux * width * width,
            transcendentals=0,
        ),
        name="project",
    )(slots, *group_bases, factor_block)


def ladder_kernel(given, slots, pairs, *refs):
    amp_refs, proj_ref, out_refs = refs[:given], refs[given], refs[given + 1 : 2 * given + 1]
    twice, mixed = refs[2 * given + 1 :]
    half, npno = proj_ref.shape[1], proj_ref.shape[2]
    s = pl.program_id(0)

    @pl.when(s == 0)
    def _():
        twice[...] = jnp.zeros_like(twice)
        for out_ref in out_refs:
            out_ref[...] = jnp.zeros_like(out_ref)

    for j in range(given):

        @pl.when(lax.rem(slots[s], given) == j)
        def _():
            amp = amp_refs[j][slots[s] // given]
            twice[pl.ds(0, npno), pl.ds(0, npno)] = amp
            twice[pl.ds(npno, npno), pl.ds(npno, npno)] = amp

    flat = proj_ref[0].reshape(half * npno, 2 * npno)
    mixed[...] = jnp.dot(flat, twice[...], preferred_element_type=F32).astype(BF16)
    total = jnp.zeros((npno, npno), F32)
    for m in range(half):
        total = total + lax.dot_general(
            mixed[pl.ds(m * npno, npno), :],
            proj_ref[0, m],
            CONTRACT_LAST,
            preferred_element_type=F32,
        )
    narrow = total.astype(BF16)
    for j in range(given):

        @pl.when((pairs[s] >= 0) & (lax.rem(slots[s], given) == j))
        def _():
            out_refs[j][slots[s] // given] = narrow


def ladder(slots, pairs, group_amps, projected):
    given = len(group_amps)
    half, npno = projected.shape[1:3]

    def kernel(*refs):
        ladder_kernel(given, *refs)

    return pl.pallas_call(
        kernel,
        grid=(CAP,),
        in_specs=[smem_spec()] * 2
        + [vmem_spec()] * given
        + [pl.BlockSpec((1, half, npno, 2 * npno), lambda s: (s, 0, 0, 0))],
        out_specs=[vmem_spec()] * given,
        out_shape=[jax.ShapeDtypeStruct((2, npno, npno), BF16)] * given,
        scratch_shapes=[
            pltpu.VMEM((2 * npno, 2 * npno), BF16),
            pltpu.VMEM((half * npno, 2 * npno), BF16),
        ],
        compiler_params=params(24),
        cost_estimate=pl.CostEstimate(
            flops=0,
            bytes_accessed=16 * CAP * half * npno**2,
            transcendentals=0,
        ),
        name="ladder",
    )(slots, pairs, *group_amps, projected)


def coupling_kernel(near, own_ref, next_ref, inter_ref, ints_ref, out_ref):
    count = own_ref.shape[0]
    total = ints_ref[...]
    for n in range(inter_ref.shape[0]):
        at = near[n]
        own = own_ref[jnp.minimum(at, count - 1)]
        far = next_ref[jnp.maximum(at - count, 0)]
        amp = jnp.where(at < count, own, far)
        inter = inter_ref[n]
        mixed = jnp.dot(inter, amp, preferred_element_type=F32).astype(BF16)
        total = total + lax.dot_general(
            mixed, inter, CONTRACT_LAST, preferred_element_type=F32
        )
    out_ref[...] = total


def coupling(near, own, following, inter, ints):
    return pl.pallas_call(
        coupling_kernel,
        in_specs=[smem_spec()] + [vmem_spec()] * 4,
        out_specs=vmem_spec(),
        out_shape=jax.ShapeDtypeStruct(ints.shape, F32),
        compiler_params=params(16),
        name="coupling",
    )(near, own, following, inter, ints)


def fold_kernel(given, last, *refs):
    term_refs, (rest, down, across, far_down, far_across), (send, keep) = (
        refs[:given],
        refs[given : given + 5],
        refs[given + 5 :],
    )
    mine, other = (sum(ref[r].astype(F32) for ref in term_refs) for r in range(2))
    mine = mine + rest[...]
    keep[0] = mine
    if last:
        send[0] = other.astype(BF16)
    else:
        send[0] = other.astype(BF16)
        send[1] = (-mine / (down[...] + across[...])).astype(BF16)
        keep[1] = -other / (far_down[...] + far_across[...])


def fold(last, terms, rest, energies):
    given = len(terms)
    rows = 1 if last else 2

    def kernel(*refs):
        fold_kernel(given, last, *refs)

    return pl.pallas_call(
        kernel,
        in_specs=[vmem_spec()] * (given + 5),
        out_specs=[vmem_spec()] * 2,
        out_shape=[
            jax.ShapeDtypeStruct((rows,) + rest.shape, BF16),
            jax.ShapeDtypeStruct((rows,) + rest.shape, F32),
        ],
        compiler_params=params(16),
        name="fold",
    )(*terms, rest, *energies)


def finish_kernel(last, keep, got, down, across, out_ref):
    update = -(keep[0] + got[0].astype(F32)) / (down[...] + across[...])
    out_ref[0] = update.astype(out_ref.dtype)
    if not last:
        out_ref[1] = (keep[1] + got[1].astype(F32)).astype(out_ref.dtype)


def finish(last, keep, got, down, across):
    def kernel(*refs):
        finish_kernel(last, *refs)

    return pl.pallas_call(
        kernel,
        in_specs=[vmem_spec()] * 4,
        out_specs=vmem_spec(),
        out_shape=jax.ShapeDtypeStruct(keep.shape, F32 if last else BF16),
        compiler_params=params(16),
        name="finish",
    )(keep, got, down, across)


def on_device(
    amplitudes,
    bases,
    factors,
    intersections,
    pair_integrals,
    pno_energies,
    pair_shift,
    pair_atoms,
    pair_next,
):
    me = lax.axis_index("dev")
    count = lax.axis_size("dev")
    places = jnp.arange(count, dtype=jnp.int32)
    listed = jnp.any(pair_atoms == me, axis=1)
    before = places[None, :] < places[:, None]
    rank = jnp.sum(before & listed[None, :], axis=1)
    chosen = listed[None, :] & (rank[None, :] == jnp.arange(CAP)[:, None])
    pairs = jnp.sum(jnp.where(chosen, places[None, :] + 1, 0), axis=1) - 1
    slots = jnp.where(pairs >= 0, place_of(pairs, "dev"), 0)
    near = pair_next[0]
    near = jnp.where(
        near < count, place_of(near, "dev"), count + place_of(near - count, "dev")
    )
    inter = intersections[0]
    ints = pair_integrals[0]

    group_bases = gather_near(gather_across(bases, "dev"), "dev")
    pair_amps, group_bases[1] = lax.optimization_barrier(
        (gather_across(amplitudes, "dev"), group_bases[1])
    )
    group_amps = gather_near(pair_amps, "dev")
    shifted = pno_energies + 0.5 * pair_shift[:, None]
    far_shifted = exchange(shifted, "dev", opposite("dev"))
    energies = (shifted.reshape(-1, 1), shifted, far_shifted.reshape(-1, 1), far_shifted)
    projected = project(slots, group_bases, factors[0])
    group_amps, projected = lax.optimization_barrier((group_amps, projected))
    for iteration in range(ITERS):
        last = iteration + 1 == ITERS
        stacked = stack(group_amps)
        following = from_next(stacked, "grp")
        terms = list(ladder(slots, pairs, group_amps, projected))
        terms[1], following = lax.optimization_barrier((terms[1], following))
        rest = coupling(near, stacked, following, inter, ints)
        send, keep = fold(last, exchange_near(terms, "dev"), rest, energies)
        update = finish(last, keep, exchange(send, "dev", opposite("dev")), *energies[:2])
        if not last:
            group_amps = gather_near(update, "dev")
    return update


def solution(mesh):
    return jax.shard_map(
        on_device,
        mesh=mesh,
        in_specs=(
            P(("grp", "dev"), None, None),
            P(("grp", "dev"), None, None),
            P(("grp", "dev"), None, None, None),
            P(("grp", "dev"), None, None, None),
            P(("grp", "dev"), None, None),
            P(("grp", "dev"), None),
            P(("grp", "dev")),
            P("grp", None),
            P(("grp", "dev"), None),
        ),
        out_specs=P(("grp", "dev"), None, None),
        check_vma=False,
    )
```

```python
import jax
import jax.numpy as jnp
from jax import lax
from jax.experimental import pallas as pl
from jax.experimental.pallas import tpu as pltpu
from jax.sharding import PartitionSpec as P

CAP = 3
ITERS = 2
F32 = jnp.float32
BF16 = jnp.bfloat16
CONTRACT_LAST = (((1,), (1,)), ((), ()))


def vmem_spec():
    return pl.BlockSpec(memory_space=pltpu.VMEM)


def smem_spec():
    return pl.BlockSpec(memory_space=pltpu.SMEM)


def params(mib):
    return pltpu.CompilerParams(vmem_limit_bytes=mib * 2**20)


def exchange(value, axis, offset):
    count = lax.axis_size(axis)
    return lax.ppermute(value, axis, [(d, d ^ offset) for d in range(count)])


def opposite(axis):
    return lax.axis_size(axis) // 2


def gather_across(value, axis):
    return jnp.concatenate([value, exchange(value, axis, opposite(axis))], axis=0)


def exchange_near(entries, axis):
    return [entries[0]] + [exchange(entries[j], axis, j) for j in range(1, len(entries))]


def gather_near(pair, axis):
    return exchange_near([pair] * (lax.axis_size(axis) // 2), axis)


def place_of(device, axis):
    half = lax.axis_size(axis) // 2
    offset = device ^ lax.axis_index(axis)
    return jnp.where(offset < half, offset, half + (offset ^ opposite(axis)))


def from_next(value, axis):
    count = lax.axis_size(axis)
    return lax.ppermute(value, axis, [(d, d - 1) for d in range(1, count)])


def stack_kernel(*refs):
    entries, out_ref = refs[:-1], refs[-1]
    for j, entry in enumerate(entries):
        for r in range(2):
            out_ref[r * len(entries) + j] = entry[r]


def stack(entries):
    _, rows, columns = entries[0].shape
    return pl.pallas_call(
        stack_kernel,
        in_specs=[vmem_spec()] * len(entries),
        out_specs=vmem_spec(),
        out_shape=jax.ShapeDtypeStruct((2 * len(entries), rows, columns), entries[0].dtype),
        compiler_params=params(16),
        name="stack",
    )(*entries)


def project_kernel(given, slots, *refs):
    base_refs, (factors_ref, out_ref, wide, narrow, half) = refs[:given], refs[given:]
    aux, npno = factors_ref.shape[0], narrow.shape[2]

    @pl.when(pl.program_id(0) == 0)
    def _():
        for s in range(CAP):
            for j in range(given):

                @pl.when(lax.rem(slots[s], given) == j)
                def _():
                    narrow[s] = base_refs[j][slots[s] // given]

            wide[pl.ds(s * npno, npno), :] = narrow[s].astype(F32).T.astype(BF16)

    for k in range(aux):
        left = jnp.dot(wide[...], factors_ref[k], preferred_element_type=F32).astype(BF16)
        for s in range(CAP):
            half[s, pl.ds(k * npno, npno), :] = left[s * npno : (s + 1) * npno]
    for s in range(CAP):
        both = jnp.dot(half[s], narrow[s], preferred_element_type=F32).astype(BF16)
        for k in range(aux):
            out_ref[s, k // 2, :, pl.ds((k % 2) * npno, npno)] = both[k * npno : (k + 1) * npno]


def project(slots, group_bases, factor_block, step=8):
    aux, width, _ = factor_block.shape
    given = len(group_bases)
    npno = group_bases[0].shape[2]
    step = min(step, aux)

    def kernel(*refs):
        project_kernel(given, *refs)

    return pl.pallas_call(
        kernel,
        grid=(aux // step,),
        in_specs=[smem_spec()]
        + [pl.BlockSpec((2, width, npno), lambda i: (0, 0, 0))] * given
        + [pl.BlockSpec((step, width, width), lambda i: (i, 0, 0))],
        out_specs=pl.BlockSpec((CAP, step // 2, npno, 2 * npno), lambda i: (0, i, 0, 0)),
        out_shape=jax.ShapeDtypeStruct((CAP, aux // 2, npno, 2 * npno), BF16),
        scratch_shapes=[
            pltpu.VMEM((CAP * npno, width), BF16),
            pltpu.VMEM((CAP, width, npno), BF16),
            pltpu.VMEM((CAP, step * npno, width), BF16),
        ],
        compiler_params=params(48),
        cost_estimate=pl.CostEstimate(
            flops=4 * CAP * aux * npno * width * (width + npno) // 2,
            bytes_accessed=2 * aux * width * width,
            transcendentals=0,
        ),
        name="project",
    )(slots, *group_bases, factor_block)


def ladder_kernel(given, slots, pairs, *refs):
    amp_refs, proj_ref, out_refs = refs[:given], refs[given], refs[given + 1 : 2 * given + 1]
    twice, mixed = refs[2 * given + 1 :]
    half, npno = proj_ref.shape[1], proj_ref.shape[2]
    s = pl.program_id(0)

    @pl.when(s == 0)
    def _():
        twice[...] = jnp.zeros_like(twice)
        for out_ref in out_refs:
            out_ref[...] = jnp.zeros_like(out_ref)

    for j in range(given):

        @pl.when(lax.rem(slots[s], given) == j)
        def _():
            amp = amp_refs[j][slots[s] // given]
            twice[pl.ds(0, npno), pl.ds(0, npno)] = amp
            twice[pl.ds(npno, npno), pl.ds(npno, npno)] = amp

    flat = proj_ref[0].reshape(half * npno, 2 * npno)
    mixed[...] = jnp.dot(flat, twice[...], preferred_element_type=F32).astype(BF16)
    total = jnp.zeros((npno, npno), F32)
    for m in range(half):
        total = total + lax.dot_general(
            mixed[pl.ds(m * npno, npno), :],
            proj_ref[0, m],
            CONTRACT_LAST,
            preferred_element_type=F32,
        )
    narrow = total.astype(BF16)
    for j in range(given):

        @pl.when((pairs[s] >= 0) & (lax.rem(slots[s], given) == j))
        def _():
            out_refs[j][slots[s] // given] = narrow


def ladder(slots, pairs, group_amps, projected):
    given = len(group_amps)
    half, npno = projected.shape[1:3]

    def kernel(*refs):
        ladder_kernel(given, *refs)

    return pl.pallas_call(
        kernel,
        grid=(CAP,),
        in_specs=[smem_spec()] * 2
        + [vmem_spec()] * given
        + [pl.BlockSpec((1, half, npno, 2 * npno), lambda s: (s, 0, 0, 0))],
        out_specs=[vmem_spec()] * given,
        out_shape=[jax.ShapeDtypeStruct((2, npno, npno), BF16)] * given,
        scratch_shapes=[
            pltpu.VMEM((2 * npno, 2 * npno), BF16),
            pltpu.VMEM((half * npno, 2 * npno), BF16),
        ],
        compiler_params=params(24),
        cost_estimate=pl.CostEstimate(
            flops=0,
            bytes_accessed=16 * CAP * half * npno**2,
            transcendentals=0,
        ),
        name="ladder",
    )(slots, pairs, *group_amps, projected)


def coupling_kernel(near, own_ref, next_ref, inter_ref, ints_ref, out_ref):
    count = own_ref.shape[0]
    total = ints_ref[...]
    for n in range(inter_ref.shape[0]):
        at = near[n]
        own = own_ref[jnp.minimum(at, count - 1)]
        far = next_ref[jnp.maximum(at - count, 0)]
        amp = jnp.where(at < count, own, far)
        inter = inter_ref[n]
        mixed = jnp.dot(inter, amp, preferred_element_type=F32).astype(BF16)
        total = total + lax.dot_general(
            mixed, inter, CONTRACT_LAST, preferred_element_type=F32
        )
    out_ref[...] = total


def coupling(near, own, following, inter, ints):
    return pl.pallas_call(
        coupling_kernel,
        in_specs=[smem_spec()] + [pl.BlockSpec()] * 4,
        out_specs=vmem_spec(),
        out_shape=jax.ShapeDtypeStruct(ints.shape, F32),
        compiler_params=params(16),
        name="coupling",
    )(near, own, following, inter, ints)


def fold_kernel(given, last, *refs):
    term_refs, (rest, down, across, far_down, far_across), (send, keep) = (
        refs[:given],
        refs[given : given + 5],
        refs[given + 5 :],
    )
    mine, other = (sum(ref[r].astype(F32) for ref in term_refs) for r in range(2))
    mine = mine + rest[...]
    keep[0] = mine
    if last:
        send[0] = other.astype(BF16)
    else:
        send[0] = other.astype(BF16)
        send[1] = (-mine / (down[...] + across[...])).astype(BF16)
        keep[1] = -other / (far_down[...] + far_across[...])


def fold(last, terms, rest, energies):
    given = len(terms)
    rows = 1 if last else 2

    def kernel(*refs):
        fold_kernel(given, last, *refs)

    return pl.pallas_call(
        kernel,
        in_specs=[vmem_spec()] * (given + 5),
        out_specs=[vmem_spec()] * 2,
        out_shape=[
            jax.ShapeDtypeStruct((rows,) + rest.shape, BF16),
            jax.ShapeDtypeStruct((rows,) + rest.shape, F32),
        ],
        compiler_params=params(16),
        name="fold",
    )(*terms, rest, *energies)


def finish_kernel(last, keep, got, down, across, out_ref):
    update = -(keep[0] + got[0].astype(F32)) / (down[...] + across[...])
    out_ref[0] = update.astype(out_ref.dtype)
    if not last:
        out_ref[1] = (keep[1] + got[1].astype(F32)).astype(out_ref.dtype)


def finish(last, keep, got, down, across):
    def kernel(*refs):
        finish_kernel(last, *refs)

    return pl.pallas_call(
        kernel,
        in_specs=[vmem_spec()] * 4,
        out_specs=vmem_spec(),
        out_shape=jax.ShapeDtypeStruct(keep.shape, F32 if last else BF16),
        compiler_params=params(16),
        name="finish",
    )(keep, got, down, across)


def on_device(
    amplitudes,
    bases,
    factors,
    intersections,
    pair_integrals,
    pno_energies,
    pair_shift,
    pair_atoms,
    pair_next,
):
    me = lax.axis_index("dev")
    count = lax.axis_size("dev")
    places = jnp.arange(count, dtype=jnp.int32)
    listed = jnp.any(pair_atoms == me, axis=1)
    before = places[None, :] < places[:, None]
    rank = jnp.sum(before & listed[None, :], axis=1)
    chosen = listed[None, :] & (rank[None, :] == jnp.arange(CAP)[:, None])
    pairs = jnp.sum(jnp.where(chosen, places[None, :] + 1, 0), axis=1) - 1
    slots = jnp.where(pairs >= 0, place_of(pairs, "dev"), 0)
    near = pair_next[0]
    near = jnp.where(
        near < count, place_of(near, "dev"), count + place_of(near - count, "dev")
    )
    inter = intersections[0]
    ints = pair_integrals[0]

    far_amps = exchange(amplitudes, "dev", opposite("dev"))
    pair_bases = gather_across(bases, "dev")
    shifted = pno_energies + 0.5 * pair_shift[:, None]
    far_shifted = exchange(shifted, "dev", opposite("dev"))
    amps, far_amps, far_shifted, pair_bases = lax.optimization_barrier(
        (amplitudes, far_amps, far_shifted, pair_bases)
    )
    group_bases = gather_near(pair_bases, "dev")
    group_amps = gather_near(jnp.concatenate([amps, far_amps], axis=0), "dev")
    energies = (shifted.reshape(-1, 1), shifted, far_shifted.reshape(-1, 1), far_shifted)
    projected = project(slots, group_bases, factors[0])
    group_amps, projected = lax.optimization_barrier((group_amps, projected))
    for iteration in range(ITERS):
        last = iteration + 1 == ITERS
        stacked = stack(group_amps)
        group_amps, stacked = lax.optimization_barrier((group_amps, stacked))
        following = from_next(stacked, "grp")
        terms = ladder(slots, pairs, group_amps, projected)
        rest = coupling(near, stacked, following, inter, ints)
        send, keep = fold(last, exchange_near(terms, "dev"), rest, energies)
        update = finish(last, keep, exchange(send, "dev", opposite("dev")), *energies[:2])
        if not last:
            group_amps = gather_near(update, "dev")
    return update


def solution(mesh):
    return jax.shard_map(
        on_device,
        mesh=mesh,
        in_specs=(
            P(("grp", "dev"), None, None),
            P(("grp", "dev"), None, None),
            P(("grp", "dev"), None, None, None),
            P(("grp", "dev"), None, None, None),
            P(("grp", "dev"), None, None),
            P(("grp", "dev"), None),
            P(("grp", "dev")),
            P("grp", None),
            P(("grp", "dev"), None),
        ),
        out_specs=P(("grp", "dev"), None, None),
        check_vma=False,
    )
```

```python
import jax
import jax.numpy as jnp
from jax import lax
from jax.experimental import pallas as pl
from jax.experimental.pallas import tpu as pltpu
from jax.sharding import PartitionSpec as P

CAP = 3
ITERS = 2
F32 = jnp.float32
BF16 = jnp.bfloat16
CONTRACT_LAST = (((1,), (1,)), ((), ()))


def vmem_spec():
    return pl.BlockSpec(memory_space=pltpu.VMEM)


def smem_spec():
    return pl.BlockSpec(memory_space=pltpu.SMEM)


def params(mib):
    return pltpu.CompilerParams(vmem_limit_bytes=mib * 2**20)


def exchange(value, axis, offset):
    count = lax.axis_size(axis)
    return lax.ppermute(value, axis, [(d, d ^ offset) for d in range(count)])


def opposite(axis):
    return lax.axis_size(axis) // 2


def gather_across(value, axis):
    return jnp.concatenate([value, exchange(value, axis, opposite(axis))], axis=0)


def exchange_near(entries, axis):
    return [entries[0]] + [exchange(entries[j], axis, j) for j in range(1, len(entries))]


def gather_near(pair, axis):
    return exchange_near([pair] * (lax.axis_size(axis) // 2), axis)


def place_of(device, axis):
    half = lax.axis_size(axis) // 2
    offset = device ^ lax.axis_index(axis)
    return jnp.where(offset < half, offset, half + (offset ^ opposite(axis)))


def from_next(value, axis):
    count = lax.axis_size(axis)
    return lax.ppermute(value, axis, [(d, d - 1) for d in range(1, count)])


def stack_kernel(*refs):
    entries, out_ref = refs[:-1], refs[-1]
    for j, entry in enumerate(entries):
        for r in range(2):
            out_ref[r * len(entries) + j] = entry[r]


def stack(entries):
    _, rows, columns = entries[0].shape
    return pl.pallas_call(
        stack_kernel,
        in_specs=[vmem_spec()] * len(entries),
        out_specs=vmem_spec(),
        out_shape=jax.ShapeDtypeStruct((2 * len(entries), rows, columns), entries[0].dtype),
        compiler_params=params(16),
        name="stack",
    )(*entries)


def project_kernel(given, slots, *refs):
    base_refs, (factors_ref, out_ref, wide, narrow, half) = refs[:given], refs[given:]
    aux, npno = factors_ref.shape[0], narrow.shape[2]

    @pl.when(pl.program_id(0) == 0)
    def _():
        for s in range(CAP):
            for j in range(given):

                @pl.when(lax.rem(slots[s], given) == j)
                def _():
                    narrow[s] = base_refs[j][slots[s] // given]

            wide[pl.ds(s * npno, npno), :] = narrow[s].astype(F32).T.astype(BF16)

    for k in range(aux):
        left = jnp.dot(wide[...], factors_ref[k], preferred_element_type=F32).astype(BF16)
        for s in range(CAP):
            half[s, pl.ds(k * npno, npno), :] = left[s * npno : (s + 1) * npno]
    for s in range(CAP):
        both = jnp.dot(half[s], narrow[s], preferred_element_type=F32).astype(BF16)
        for k in range(aux):
            out_ref[s, k // 2, :, pl.ds((k % 2) * npno, npno)] = both[k * npno : (k + 1) * npno]


def project(slots, group_bases, factor_block, step=8):
    aux, width, _ = factor_block.shape
    given = len(group_bases)
    npno = group_bases[0].shape[2]
    step = min(step, aux)

    def kernel(*refs):
        project_kernel(given, *refs)

    return pl.pallas_call(
        kernel,
        grid=(aux // step,),
        in_specs=[smem_spec()]
        + [pl.BlockSpec((2, width, npno), lambda i: (0, 0, 0))] * given
        + [pl.BlockSpec((step, width, width), lambda i: (i, 0, 0))],
        out_specs=pl.BlockSpec((CAP, step // 2, npno, 2 * npno), lambda i: (0, i, 0, 0)),
        out_shape=jax.ShapeDtypeStruct((CAP, aux // 2, npno, 2 * npno), BF16),
        scratch_shapes=[
            pltpu.VMEM((CAP * npno, width), BF16),
            pltpu.VMEM((CAP, width, npno), BF16),
            pltpu.VMEM((CAP, step * npno, width), BF16),
        ],
        compiler_params=params(48),
        cost_estimate=pl.CostEstimate(
            flops=4 * CAP * aux * npno * width * (width + npno) // 2,
            bytes_accessed=2 * aux * width * width,
            transcendentals=0,
        ),
        name="project",
    )(slots, *group_bases, factor_block)


def ladder_kernel(given, slots, pairs, *refs):
    amp_refs, proj_ref, out_refs = refs[:given], refs[given], refs[given + 1 : 2 * given + 1]
    twice, mixed = refs[2 * given + 1 :]
    half, npno = proj_ref.shape[1], proj_ref.shape[2]
    s = pl.program_id(0)

    @pl.when(s == 0)
    def _():
        twice[...] = jnp.zeros_like(twice)
        for out_ref in out_refs:
            out_ref[...] = jnp.zeros_like(out_ref)

    for j in range(given):

        @pl.when(lax.rem(slots[s], given) == j)
        def _():
            amp = amp_refs[j][slots[s] // given]
            twice[pl.ds(0, npno), pl.ds(0, npno)] = amp
            twice[pl.ds(npno, npno), pl.ds(npno, npno)] = amp

    flat = proj_ref[0].reshape(half * npno, 2 * npno)
    mixed[...] = jnp.dot(flat, twice[...], preferred_element_type=F32).astype(BF16)
    total = jnp.zeros((npno, npno), F32)
    for m in range(half):
        total = total + lax.dot_general(
            mixed[pl.ds(m * npno, npno), :],
            proj_ref[0, m],
            CONTRACT_LAST,
            preferred_element_type=F32,
        )
    narrow = total.astype(BF16)
    for j in range(given):

        @pl.when((pairs[s] >= 0) & (lax.rem(slots[s], given) == j))
        def _():
            out_refs[j][slots[s] // given] = narrow


def ladder(slots, pairs, group_amps, projected):
    given = len(group_amps)
    half, npno = projected.shape[1:3]

    def kernel(*refs):
        ladder_kernel(given, *refs)

    return pl.pallas_call(
        kernel,
        grid=(CAP,),
        in_specs=[smem_spec()] * 2
        + [vmem_spec()] * given
        + [pl.BlockSpec((1, half, npno, 2 * npno), lambda s: (s, 0, 0, 0))],
        out_specs=[vmem_spec()] * given,
        out_shape=[jax.ShapeDtypeStruct((2, npno, npno), BF16)] * given,
        scratch_shapes=[
            pltpu.VMEM((2 * npno, 2 * npno), BF16),
            pltpu.VMEM((half * npno, 2 * npno), BF16),
        ],
        compiler_params=params(24),
        cost_estimate=pl.CostEstimate(
            flops=0,
            bytes_accessed=16 * CAP * half * npno**2,
            transcendentals=0,
        ),
        name="ladder",
    )(slots, pairs, *group_amps, projected)


def coupling_kernel(near, own_ref, next_ref, inter_ref, ints_ref, out_ref):
    count = own_ref.shape[0]
    total = ints_ref[0]
    for n in range(inter_ref.shape[1]):
        at = near[0, n]
        place = place_of(lax.rem(at, count), "dev")
        amp = jnp.where(at < count, own_ref[place], next_ref[place])
        inter = inter_ref[0, n]
        mixed = jnp.dot(inter, amp, preferred_element_type=F32).astype(BF16)
        total = total + lax.dot_general(
            mixed, inter, CONTRACT_LAST, preferred_element_type=F32
        )
    out_ref[...] = total


def coupling(near, own, following, inter, ints):
    return pl.pallas_call(
        coupling_kernel,
        in_specs=[smem_spec()] + [pl.BlockSpec()] * 4,
        out_specs=vmem_spec(),
        out_shape=jax.ShapeDtypeStruct(ints.shape[1:], F32),
        compiler_params=params(16),
        cost_estimate=pl.CostEstimate(
            flops=4 * inter.shape[1] * inter.shape[2] ** 3, bytes_accessed=0, transcendentals=0
        ),
        name="coupling",
    )(near, own, following, inter, ints)


def fold_kernel(given, last, *refs):
    term_refs, (rest, down, across, far_down, far_across), (send, keep) = (
        refs[:given],
        refs[given : given + 5],
        refs[given + 5 :],
    )
    mine, other = (sum(ref[r].astype(F32) for ref in term_refs) for r in range(2))
    mine = mine + rest[...]
    keep[0] = mine
    if last:
        send[0] = other.astype(BF16)
    else:
        send[0] = other.astype(BF16)
        send[1] = (-mine / (down[...] + across[...])).astype(BF16)
        keep[1] = -other / (far_down[...] + far_across[...])


def fold(last, terms, rest, energies):
    given = len(terms)
    rows = 1 if last else 2

    def kernel(*refs):
        fold_kernel(given, last, *refs)

    return pl.pallas_call(
        kernel,
        in_specs=[vmem_spec()] * (given + 5),
        out_specs=[vmem_spec()] * 2,
        out_shape=[
            jax.ShapeDtypeStruct((rows,) + rest.shape, BF16),
            jax.ShapeDtypeStruct((rows,) + rest.shape, F32),
        ],
        compiler_params=params(16),
        name="fold",
    )(*terms, rest, *energies)


def finish_kernel(last, keep, got, down, across, out_ref):
    update = -(keep[0] + got[0].astype(F32)) / (down[...] + across[...])
    out_ref[0] = update.astype(out_ref.dtype)
    if not last:
        out_ref[1] = (keep[1] + got[1].astype(F32)).astype(out_ref.dtype)


def finish(last, keep, got, down, across):
    def kernel(*refs):
        finish_kernel(last, *refs)

    return pl.pallas_call(
        kernel,
        in_specs=[vmem_spec()] * 4,
        out_specs=vmem_spec(),
        out_shape=jax.ShapeDtypeStruct(keep.shape, F32 if last else BF16),
        compiler_params=params(16),
        name="finish",
    )(keep, got, down, across)


def on_device(
    amplitudes,
    bases,
    factors,
    intersections,
    pair_integrals,
    pno_energies,
    pair_shift,
    pair_atoms,
    pair_next,
):
    me = lax.axis_index("dev")
    count = lax.axis_size("dev")
    places = jnp.arange(count, dtype=jnp.int32)
    listed = jnp.any(pair_atoms == me, axis=1)
    before = places[None, :] < places[:, None]
    rank = jnp.sum(before & listed[None, :], axis=1)
    chosen = listed[None, :] & (rank[None, :] == jnp.arange(CAP)[:, None])
    pairs = jnp.sum(jnp.where(chosen, places[None, :] + 1, 0), axis=1) - 1
    slots = jnp.where(pairs >= 0, place_of(pairs, "dev"), 0)

    shifted = pno_energies + 0.5 * pair_shift[:, None]
    far_shifted = exchange(shifted, "dev", opposite("dev"))
    pair_bases = gather_across(bases, "dev")
    amps, far_shifted = lax.optimization_barrier((amplitudes, far_shifted))
    far_amps = exchange(amps, "dev", opposite("dev"))
    amps, pair_bases = lax.optimization_barrier((amps, pair_bases))
    group_bases = gather_near(pair_bases, "dev")
    group_amps = gather_near(jnp.concatenate([amps, far_amps], axis=0), "dev")
    energies = (shifted.reshape(-1, 1), shifted, far_shifted.reshape(-1, 1), far_shifted)
    projected = project(slots, group_bases, factors[0])
    group_amps, projected = lax.optimization_barrier((group_amps, projected))
    for iteration in range(ITERS):
        last = iteration + 1 == ITERS
        stacked = stack(group_amps)
        group_amps, stacked = lax.optimization_barrier((group_amps, stacked))
        following = from_next(stacked, "grp")
        terms = ladder(slots, pairs, group_amps, projected)
        rest = coupling(pair_next, stacked, following, intersections, pair_integrals)
        send, keep = fold(last, exchange_near(terms, "dev"), rest, energies)
        update = finish(last, keep, exchange(send, "dev", opposite("dev")), *energies[:2])
        if not last:
            group_amps = gather_near(update, "dev")
    return update


def solution(mesh):
    return jax.shard_map(
        on_device,
        mesh=mesh,
        in_specs=(
            P(("grp", "dev"), None, None),
            P(("grp", "dev"), None, None),
            P(("grp", "dev"), None, None, None),
            P(("grp", "dev"), None, None, None),
            P(("grp", "dev"), None, None),
            P(("grp", "dev"), None),
            P(("grp", "dev")),
            P("grp", None),
            P(("grp", "dev"), None),
        ),
        out_specs=P(("grp", "dev"), None, None),
        check_vma=False,
    )
```

```python
import jax
import jax.numpy as jnp
from jax import lax
from jax.experimental import pallas as pl
from jax.experimental.pallas import tpu as pltpu
from jax.sharding import PartitionSpec as P

CAP = 3
ITERS = 2
F32 = jnp.float32
BF16 = jnp.bfloat16
CONTRACT_LAST = (((1,), (1,)), ((), ()))


def vmem_spec():
    return pl.BlockSpec(memory_space=pltpu.VMEM)


def smem_spec():
    return pl.BlockSpec(memory_space=pltpu.SMEM)


def in_hbm(value):
    return pltpu.with_memory_space_constraint(value, pltpu.HBM)


def params(mib):
    return pltpu.CompilerParams(vmem_limit_bytes=mib * 2**20)


def exchange(value, axis, offset):
    count = lax.axis_size(axis)
    return lax.ppermute(value, axis, [(d, d ^ offset) for d in range(count)])


def opposite(axis):
    return lax.axis_size(axis) // 2


def gather_across(value, axis):
    return jnp.concatenate([value, exchange(value, axis, opposite(axis))], axis=0)


def exchange_near(entries, axis):
    return [entries[0]] + [exchange(entries[j], axis, j) for j in range(1, len(entries))]


def gather_near(pair, axis):
    return exchange_near([pair] * (lax.axis_size(axis) // 2), axis)


def place_of(device, axis):
    half = lax.axis_size(axis) // 2
    offset = device ^ lax.axis_index(axis)
    return jnp.where(offset < half, offset, half + (offset ^ opposite(axis)))


def from_next(value, axis):
    count = lax.axis_size(axis)
    return lax.ppermute(value, axis, [(d, d - 1) for d in range(1, count)])


def stack_kernel(*refs):
    entries, out_ref = refs[:-1], refs[-1]
    for j, entry in enumerate(entries):
        for r in range(2):
            out_ref[r * len(entries) + j] = entry[r]


def stack(entries):
    _, rows, columns = entries[0].shape
    return pl.pallas_call(
        stack_kernel,
        in_specs=[vmem_spec()] * len(entries),
        out_specs=vmem_spec(),
        out_shape=pltpu.VMEM((2 * len(entries), rows, columns), entries[0].dtype),
        compiler_params=params(16),
        name="stack",
    )(*entries)


def project_kernel(given, slots, *refs):
    base_refs, (factors_ref, out_ref, wide, narrow, half) = refs[:given], refs[given:]
    aux, npno = factors_ref.shape[0], narrow.shape[2]

    @pl.when(pl.program_id(0) == 0)
    def _():
        for s in range(CAP):
            for j in range(given):

                @pl.when(lax.rem(slots[s], given) == j)
                def _():
                    narrow[s] = base_refs[j][slots[s] // given]

            wide[pl.ds(s * npno, npno), :] = narrow[s].astype(F32).T.astype(BF16)

    for k in range(aux):
        left = jnp.dot(wide[...], factors_ref[k], preferred_element_type=F32).astype(BF16)
        for s in range(CAP):
            half[s, pl.ds(k * npno, npno), :] = left[s * npno : (s + 1) * npno]
    for s in range(CAP):
        both = jnp.dot(half[s], narrow[s], preferred_element_type=F32).astype(BF16)
        for k in range(aux):
            out_ref[s, k // 2, :, pl.ds((k % 2) * npno, npno)] = both[k * npno : (k + 1) * npno]


def project(slots, group_bases, factor_block, step=8):
    aux, width, _ = factor_block.shape
    given = len(group_bases)
    npno = group_bases[0].shape[2]
    step = min(step, aux)

    def kernel(*refs):
        project_kernel(given, *refs)

    return pl.pallas_call(
        kernel,
        grid=(aux // step,),
        in_specs=[smem_spec()]
        + [pl.BlockSpec((2, width, npno), lambda i: (0, 0, 0))] * given
        + [pl.BlockSpec((step, width, width), lambda i: (i, 0, 0))],
        out_specs=pl.BlockSpec((CAP, step // 2, npno, 2 * npno), lambda i: (0, i, 0, 0)),
        out_shape=pltpu.HBM((CAP, aux // 2, npno, 2 * npno), BF16),
        scratch_shapes=[
            pltpu.VMEM((CAP * npno, width), BF16),
            pltpu.VMEM((CAP, width, npno), BF16),
            pltpu.VMEM((CAP, step * npno, width), BF16),
        ],
        compiler_params=params(24),
        cost_estimate=pl.CostEstimate(
            flops=4 * CAP * aux * npno * width * (width + npno) // 2,
            bytes_accessed=2 * aux * width * width,
            transcendentals=0,
        ),
        name="project",
    )(slots, *group_bases, in_hbm(factor_block))


def ladder_kernel(given, slots, pairs, *refs):
    amp_refs, proj_ref, out_refs = refs[:given], refs[given], refs[given + 1 : 2 * given + 1]
    twice, mixed = refs[2 * given + 1 :]
    half, npno = proj_ref.shape[1], proj_ref.shape[2]
    s = pl.program_id(0)

    @pl.when(s == 0)
    def _():
        twice[...] = jnp.zeros_like(twice)
        for out_ref in out_refs:
            out_ref[...] = jnp.zeros_like(out_ref)

    for j in range(given):

        @pl.when(lax.rem(slots[s], given) == j)
        def _():
            amp = amp_refs[j][slots[s] // given]
            twice[pl.ds(0, npno), pl.ds(0, npno)] = amp
            twice[pl.ds(npno, npno), pl.ds(npno, npno)] = amp

    flat = proj_ref[0].reshape(half * npno, 2 * npno)
    mixed[...] = jnp.dot(flat, twice[...], preferred_element_type=F32).astype(BF16)
    total = jnp.zeros((npno, npno), F32)
    for m in range(half):
        total = total + lax.dot_general(
            mixed[pl.ds(m * npno, npno), :],
            proj_ref[0, m],
            CONTRACT_LAST,
            preferred_element_type=F32,
        )
    narrow = total.astype(BF16)
    for j in range(given):

        @pl.when((pairs[s] >= 0) & (lax.rem(slots[s], given) == j))
        def _():
            out_refs[j][slots[s] // given] = narrow


def ladder(slots, pairs, group_amps, projected):
    given = len(group_amps)
    half, npno = projected.shape[1:3]

    def kernel(*refs):
        ladder_kernel(given, *refs)

    return pl.pallas_call(
        kernel,
        grid=(CAP,),
        in_specs=[smem_spec()] * 2
        + [vmem_spec()] * given
        + [pl.BlockSpec((1, half, npno, 2 * npno), lambda s: (s, 0, 0, 0))],
        out_specs=[vmem_spec()] * given,
        out_shape=[pltpu.VMEM((2, npno, npno), BF16)] * given,
        scratch_shapes=[
            pltpu.VMEM((2 * npno, 2 * npno), BF16),
            pltpu.VMEM((half * npno, 2 * npno), BF16),
        ],
        compiler_params=params(24),
        cost_estimate=pl.CostEstimate(
            flops=0,
            bytes_accessed=16 * CAP * half * npno**2,
            transcendentals=0,
        ),
        name="ladder",
    )(slots, pairs, *group_amps, in_hbm(projected))


def coupling_kernel(near, own_ref, next_ref, inter_ref, ints_ref, out_ref):
    count = own_ref.shape[0]
    total = ints_ref[0]
    for n in range(inter_ref.shape[1]):
        at = near[0, n]
        place = place_of(lax.rem(at, count), "dev")
        amp = jnp.where(at < count, own_ref[place], next_ref[place])
        inter = inter_ref[0, n]
        mixed = jnp.dot(inter, amp, preferred_element_type=F32).astype(BF16)
        total = total + lax.dot_general(
            mixed, inter, CONTRACT_LAST, preferred_element_type=F32
        )
    out_ref[...] = total


def coupling(near, own, following, inter, ints):
    return pl.pallas_call(
        coupling_kernel,
        in_specs=[smem_spec()] + [pl.BlockSpec()] * 4,
        out_specs=vmem_spec(),
        out_shape=pltpu.VMEM(ints.shape[1:], F32),
        compiler_params=params(16),
        cost_estimate=pl.CostEstimate(
            flops=4 * inter.shape[1] * inter.shape[2] ** 3, bytes_accessed=0, transcendentals=0
        ),
        name="coupling",
    )(near, own, following, in_hbm(inter), in_hbm(ints))


def fold_kernel(given, last, *refs):
    term_refs, (rest, down, across, far_down, far_across), (send, keep) = (
        refs[:given],
        refs[given : given + 5],
        refs[given + 5 :],
    )
    mine, other = (sum(ref[r].astype(F32) for ref in term_refs) for r in range(2))
    mine = mine + rest[...]
    keep[0] = mine
    if last:
        send[0] = other.astype(BF16)
    else:
        send[0] = other.astype(BF16)
        send[1] = (-mine / (down[...] + across[...])).astype(BF16)
        keep[1] = -other / (far_down[...] + far_across[...])


def fold(last, terms, rest, energies):
    given = len(terms)
    rows = 1 if last else 2

    def kernel(*refs):
        fold_kernel(given, last, *refs)

    return pl.pallas_call(
        kernel,
        in_specs=[vmem_spec()] * (given + 5),
        out_specs=[vmem_spec()] * 2,
        out_shape=[
            pltpu.VMEM((rows,) + rest.shape, BF16),
            pltpu.VMEM((rows,) + rest.shape, F32),
        ],
        compiler_params=params(16),
        name="fold",
    )(*terms, rest, *energies)


def finish_kernel(last, keep, got, down, across, out_ref):
    update = -(keep[0] + got[0].astype(F32)) / (down[...] + across[...])
    out_ref[0] = update.astype(out_ref.dtype)
    if not last:
        out_ref[1] = (keep[1] + got[1].astype(F32)).astype(out_ref.dtype)


def finish(last, keep, got, down, across):
    def kernel(*refs):
        finish_kernel(last, *refs)

    return pl.pallas_call(
        kernel,
        in_specs=[vmem_spec()] * 4,
        out_specs=vmem_spec(),
        out_shape=jax.ShapeDtypeStruct(keep.shape, F32) if last else pltpu.VMEM(keep.shape, BF16),
        compiler_params=params(16),
        name="finish",
    )(keep, got, down, across)


def on_device(
    amplitudes,
    bases,
    factors,
    intersections,
    pair_integrals,
    pno_energies,
    pair_shift,
    pair_atoms,
    pair_next,
):
    me = lax.axis_index("dev")
    count = lax.axis_size("dev")
    places = jnp.arange(count, dtype=jnp.int32)
    listed = jnp.any(pair_atoms == me, axis=1)
    before = places[None, :] < places[:, None]
    rank = jnp.sum(before & listed[None, :], axis=1)
    chosen = listed[None, :] & (rank[None, :] == jnp.arange(CAP)[:, None])
    pairs = jnp.sum(jnp.where(chosen, places[None, :] + 1, 0), axis=1) - 1
    slots = jnp.where(pairs >= 0, place_of(pairs, "dev"), 0)

    far_energies = exchange(pno_energies, "dev", opposite("dev"))
    far_shift = exchange(pair_shift, "dev", opposite("dev"))
    pair_bases = gather_across(bases, "dev")
    amps, far_energies = lax.optimization_barrier((amplitudes, far_energies))
    far_amps = exchange(amps, "dev", opposite("dev"))
    amps, pair_bases = lax.optimization_barrier((amps, pair_bases))
    group_bases = gather_near(pair_bases, "dev")
    group_amps = gather_near(jnp.concatenate([amps, far_amps], axis=0), "dev")
    shifted = pno_energies + 0.5 * pair_shift[:, None]
    far_shifted = far_energies + 0.5 * far_shift[:, None]
    energies = (shifted.reshape(-1, 1), shifted, far_shifted.reshape(-1, 1), far_shifted)
    projected = project(slots, group_bases, factors[0])
    group_amps, projected = lax.optimization_barrier((group_amps, projected))
    for iteration in range(ITERS):
        last = iteration + 1 == ITERS
        stacked = stack(group_amps)
        group_amps, stacked = lax.optimization_barrier((group_amps, stacked))
        following = from_next(stacked, "grp")
        terms = ladder(slots, pairs, group_amps, projected)
        rest = coupling(pair_next, stacked, following, intersections, pair_integrals)
        send, keep = fold(last, exchange_near(terms, "dev"), rest, energies)
        update = finish(last, keep, exchange(send, "dev", opposite("dev")), *energies[:2])
        if not last:
            group_amps = gather_near(update, "dev")
    return update


def solution(mesh):
    return jax.shard_map(
        on_device,
        mesh=mesh,
        in_specs=(
            P(("grp", "dev"), None, None),
            P(("grp", "dev"), None, None),
            P(("grp", "dev"), None, None, None),
            P(("grp", "dev"), None, None, None),
            P(("grp", "dev"), None, None),
            P(("grp", "dev"), None),
            P(("grp", "dev")),
            P("grp", None),
            P(("grp", "dev"), None),
        ),
        out_specs=P(("grp", "dev"), None, None),
        check_vma=False,
    )
```

```python
import jax
import jax.numpy as jnp
from jax import lax
from jax.experimental import pallas as pl
from jax.experimental.pallas import tpu as pltpu
from jax.sharding import PartitionSpec as P

CAP = 3
ITERS = 2
F32 = jnp.float32
BF16 = jnp.bfloat16
CONTRACT_LAST = (((1,), (1,)), ((), ()))


def vmem_spec():
    return pl.BlockSpec(memory_space=pltpu.VMEM)


def smem_spec():
    return pl.BlockSpec(memory_space=pltpu.SMEM)


def in_hbm(value):
    return pltpu.with_memory_space_constraint(value, pltpu.HBM)


def params(mib):
    return pltpu.CompilerParams(vmem_limit_bytes=mib * 2**20)


def exchange(value, axis, offset):
    count = lax.axis_size(axis)
    return lax.ppermute(value, axis, [(d, d ^ offset) for d in range(count)])


def opposite(axis):
    return lax.axis_size(axis) // 2


def gather_across(value, axis):
    return jnp.concatenate([value, exchange(value, axis, opposite(axis))], axis=0)


def exchange_near(entries, axis):
    found = list(entries)
    for j in range(len(entries) - 1, 0, -1):
        found[j] = exchange(entries[j], axis, j)
    return found


def gather_near(pair, axis):
    return exchange_near([pair] * (lax.axis_size(axis) // 2), axis)


def place_of(device, axis):
    half = lax.axis_size(axis) // 2
    offset = device ^ lax.axis_index(axis)
    return jnp.where(offset < half, offset, half + (offset ^ opposite(axis)))


def from_next(value, axis):
    count = lax.axis_size(axis)
    return lax.ppermute(value, axis, [(d, d - 1) for d in range(1, count)])


def stack_kernel(*refs):
    entries, out_ref = refs[:-1], refs[-1]
    for j, entry in enumerate(entries):
        for r in range(2):
            out_ref[r * len(entries) + j] = entry[r]


def stack(entries):
    _, rows, columns = entries[0].shape
    return pl.pallas_call(
        stack_kernel,
        in_specs=[vmem_spec()] * len(entries),
        out_specs=vmem_spec(),
        out_shape=pltpu.VMEM((2 * len(entries), rows, columns), entries[0].dtype),
        compiler_params=params(16),
        name="stack",
    )(*entries)


def project_kernel(given, slots, *refs):
    base_refs, (factors_ref, out_ref, wide, narrow, half) = refs[:given], refs[given:]
    aux, npno = factors_ref.shape[0], narrow.shape[2]

    @pl.when(pl.program_id(0) == 0)
    def _():
        for s in range(CAP):
            for j in range(given):

                @pl.when(lax.rem(slots[s], given) == j)
                def _():
                    narrow[s] = base_refs[j][slots[s] // given]

            wide[pl.ds(s * npno, npno), :] = narrow[s].astype(F32).T.astype(BF16)

    first = pl.program_id(0) * (aux // 2)
    for k in range(aux):
        left = jnp.dot(wide[...], factors_ref[k], preferred_element_type=F32).astype(BF16)
        for s in range(CAP):
            half[s, pl.ds(k * npno, npno), :] = left[s * npno : (s + 1) * npno]
    for s in range(CAP):
        both = jnp.dot(half[s], narrow[s], preferred_element_type=F32).astype(BF16)
        for k in range(aux):
            out_ref[s, first + k // 2, :, pl.ds((k % 2) * npno, npno)] = both[
                k * npno : (k + 1) * npno
            ]


def project(slots, group_bases, factor_block, step=8):
    aux, width, _ = factor_block.shape
    given = len(group_bases)
    npno = group_bases[0].shape[2]
    step = min(step, aux)

    def kernel(*refs):
        project_kernel(given, *refs)

    return pl.pallas_call(
        kernel,
        grid=(aux // step,),
        in_specs=[smem_spec()]
        + [vmem_spec()] * given
        + [pl.BlockSpec((step, width, width), lambda i: (i, 0, 0))],
        out_specs=vmem_spec(),
        out_shape=pltpu.VMEM((CAP, aux // 2, npno, 2 * npno), BF16),
        scratch_shapes=[
            pltpu.VMEM((CAP * npno, width), BF16),
            pltpu.VMEM((CAP, width, npno), BF16),
            pltpu.VMEM((CAP, step * npno, width), BF16),
        ],
        compiler_params=params(24),
        cost_estimate=pl.CostEstimate(
            flops=4 * CAP * aux * npno * width * (width + npno) // 2,
            bytes_accessed=2 * aux * width * width,
            transcendentals=0,
        ),
        name="project",
    )(slots, *group_bases, in_hbm(factor_block))


def ladder_kernel(given, slots, pairs, *refs):
    amp_refs, proj_ref, out_refs = refs[:given], refs[given], refs[given + 1 : 2 * given + 1]
    twice, mixed = refs[2 * given + 1 :]
    half, npno = proj_ref.shape[1], proj_ref.shape[2]
    twice[...] = jnp.zeros_like(twice)
    for out_ref in out_refs:
        out_ref[...] = jnp.zeros_like(out_ref)
    for s in range(CAP):
        for j in range(given):

            @pl.when(lax.rem(slots[s], given) == j)
            def _():
                amp = amp_refs[j][slots[s] // given]
                twice[pl.ds(0, npno), pl.ds(0, npno)] = amp
                twice[pl.ds(npno, npno), pl.ds(npno, npno)] = amp

        flat = proj_ref[s].reshape(half * npno, 2 * npno)
        mixed[...] = jnp.dot(flat, twice[...], preferred_element_type=F32).astype(BF16)
        total = jnp.zeros((npno, npno), F32)
        for m in range(half):
            total = total + lax.dot_general(
                mixed[pl.ds(m * npno, npno), :],
                proj_ref[s, m],
                CONTRACT_LAST,
                preferred_element_type=F32,
            )
        narrow = total.astype(BF16)
        for j in range(given):

            @pl.when((pairs[s] >= 0) & (lax.rem(slots[s], given) == j))
            def _():
                out_refs[j][slots[s] // given] = narrow


def ladder(slots, pairs, group_amps, projected):
    given = len(group_amps)
    half, npno = projected.shape[1:3]

    def kernel(*refs):
        ladder_kernel(given, *refs)

    return pl.pallas_call(
        kernel,
        in_specs=[smem_spec()] * 2 + [vmem_spec()] * (given + 1),
        out_specs=[vmem_spec()] * given,
        out_shape=[pltpu.VMEM((2, npno, npno), BF16)] * given,
        scratch_shapes=[
            pltpu.VMEM((2 * npno, 2 * npno), BF16),
            pltpu.VMEM((half * npno, 2 * npno), BF16),
        ],
        compiler_params=params(24),
        cost_estimate=pl.CostEstimate(
            flops=0,
            bytes_accessed=16 * CAP * half * npno**2,
            transcendentals=0,
        ),
        name="ladder",
    )(slots, pairs, *group_amps, projected)


def coupling_kernel(near, own_ref, next_ref, inter_ref, ints_ref, out_ref):
    count = own_ref.shape[0]
    total = ints_ref[0]
    for n in range(inter_ref.shape[1]):
        at = near[0, n]
        place = place_of(lax.rem(at, count), "dev")
        amp = jnp.where(at < count, own_ref[place], next_ref[place])
        inter = inter_ref[0, n]
        mixed = jnp.dot(inter, amp, preferred_element_type=F32).astype(BF16)
        total = total + lax.dot_general(
            mixed, inter, CONTRACT_LAST, preferred_element_type=F32
        )
    out_ref[...] = total


def coupling(near, own, following, inter, ints):
    return pl.pallas_call(
        coupling_kernel,
        in_specs=[smem_spec()] + [pl.BlockSpec()] * 4,
        out_specs=vmem_spec(),
        out_shape=pltpu.VMEM(ints.shape[1:], F32),
        compiler_params=params(16),
        cost_estimate=pl.CostEstimate(
            flops=4 * inter.shape[1] * inter.shape[2] ** 3, bytes_accessed=0, transcendentals=0
        ),
        name="coupling",
    )(near, own, following, in_hbm(inter), in_hbm(ints))


def fold_kernel(given, last, *refs):
    term_refs, (rest, down, across, far_down, far_across), (send, keep) = (
        refs[:given],
        refs[given : given + 5],
        refs[given + 5 :],
    )
    mine, other = (sum(ref[r].astype(F32) for ref in term_refs) for r in range(2))
    mine = mine + rest[...]
    keep[0] = mine
    if last:
        send[0] = other.astype(BF16)
    else:
        send[0] = other.astype(BF16)
        send[1] = (-mine / (down[...] + across[...])).astype(BF16)
        keep[1] = -other / (far_down[...] + far_across[...])


def fold(last, terms, rest, energies):
    given = len(terms)
    rows = 1 if last else 2

    def kernel(*refs):
        fold_kernel(given, last, *refs)

    return pl.pallas_call(
        kernel,
        in_specs=[vmem_spec()] * (given + 5),
        out_specs=[vmem_spec()] * 2,
        out_shape=[
            pltpu.VMEM((rows,) + rest.shape, BF16),
            pltpu.VMEM((rows,) + rest.shape, F32),
        ],
        compiler_params=params(16),
        name="fold",
    )(*terms, rest, *energies)


def finish_kernel(last, keep, got, down, across, out_ref):
    update = -(keep[0] + got[0].astype(F32)) / (down[...] + across[...])
    out_ref[0] = update.astype(out_ref.dtype)
    if not last:
        out_ref[1] = (keep[1] + got[1].astype(F32)).astype(out_ref.dtype)


def finish(last, keep, got, down, across):
    def kernel(*refs):
        finish_kernel(last, *refs)

    return pl.pallas_call(
        kernel,
        in_specs=[vmem_spec()] * 4,
        out_specs=vmem_spec(),
        out_shape=jax.ShapeDtypeStruct(keep.shape, F32) if last else pltpu.VMEM(keep.shape, BF16),
        compiler_params=params(16),
        name="finish",
    )(keep, got, down, across)


def on_device(
    amplitudes,
    bases,
    factors,
    intersections,
    pair_integrals,
    pno_energies,
    pair_shift,
    pair_atoms,
    pair_next,
):
    me = lax.axis_index("dev")
    count = lax.axis_size("dev")
    places = jnp.arange(count, dtype=jnp.int32)
    listed = jnp.any(pair_atoms == me, axis=1)
    before = places[None, :] < places[:, None]
    rank = jnp.sum(before & listed[None, :], axis=1)
    chosen = listed[None, :] & (rank[None, :] == jnp.arange(CAP)[:, None])
    pairs = jnp.sum(jnp.where(chosen, places[None, :] + 1, 0), axis=1) - 1
    slots = jnp.where(pairs >= 0, place_of(pairs, "dev"), 0)

    far_energies = exchange(pno_energies, "dev", opposite("dev"))
    far_shift = exchange(pair_shift, "dev", opposite("dev"))
    pair_bases = gather_across(bases, "dev")
    amps, far_energies = lax.optimization_barrier((amplitudes, far_energies))
    far_amps = exchange(amps, "dev", opposite("dev"))
    amps, pair_bases = lax.optimization_barrier((amps, pair_bases))
    group_bases = gather_near(pair_bases, "dev")
    group_amps = gather_near(jnp.concatenate([amps, far_amps], axis=0), "dev")
    shifted = pno_energies + 0.5 * pair_shift[:, None]
    far_shifted = far_energies + 0.5 * far_shift[:, None]
    energies = (shifted.reshape(-1, 1), shifted, far_shifted.reshape(-1, 1), far_shifted)
    projected = project(slots, group_bases, factors[0])
    group_amps, projected = lax.optimization_barrier((group_amps, projected))
    for iteration in range(ITERS):
        last = iteration + 1 == ITERS
        stacked = stack(group_amps)
        group_amps, stacked = lax.optimization_barrier((group_amps, stacked))
        following = from_next(stacked, "grp")
        terms = ladder(slots, pairs, group_amps, projected)
        rest = coupling(pair_next, stacked, following, intersections, pair_integrals)
        send, keep = fold(last, exchange_near(terms, "dev"), rest, energies)
        update = finish(last, keep, exchange(send, "dev", opposite("dev")), *energies[:2])
        if not last:
            group_amps = gather_near(update, "dev")
    return update


def solution(mesh):
    return jax.shard_map(
        on_device,
        mesh=mesh,
        in_specs=(
            P(("grp", "dev"), None, None),
            P(("grp", "dev"), None, None),
            P(("grp", "dev"), None, None, None),
            P(("grp", "dev"), None, None, None),
            P(("grp", "dev"), None, None),
            P(("grp", "dev"), None),
            P(("grp", "dev")),
            P("grp", None),
            P(("grp", "dev"), None),
        ),
        out_specs=P(("grp", "dev"), None, None),
        check_vma=False,
    )
```

```python
import jax
import jax.numpy as jnp
from jax import lax
from jax.experimental import pallas as pl
from jax.experimental.pallas import tpu as pltpu
from jax.sharding import PartitionSpec as P

CAP = 3
ITERS = 2
F32 = jnp.float32
BF16 = jnp.bfloat16
CONTRACT_LAST = (((1,), (1,)), ((), ()))


def vmem_spec():
    return pl.BlockSpec(memory_space=pltpu.VMEM)


def smem_spec():
    return pl.BlockSpec(memory_space=pltpu.SMEM)


def in_hbm(value):
    return pltpu.with_memory_space_constraint(value, pltpu.HBM)


def params(mib):
    return pltpu.CompilerParams(vmem_limit_bytes=mib * 2**20)


def exchange(value, axis, offset):
    count = lax.axis_size(axis)
    return lax.ppermute(value, axis, [(d, d ^ offset) for d in range(count)])


def opposite(axis):
    return lax.axis_size(axis) // 2


def gather_across(value, axis):
    return jnp.concatenate([value, exchange(value, axis, opposite(axis))], axis=0)


def exchange_near(entries, axis):
    found = list(entries)
    for j in range(len(entries) - 1, 0, -1):
        found[j] = exchange(entries[j], axis, j)
    return found


def gather_near(pair, axis):
    return exchange_near([pair] * (lax.axis_size(axis) // 2), axis)


def place_of(device, axis):
    half = lax.axis_size(axis) // 2
    offset = device ^ lax.axis_index(axis)
    return jnp.where(offset < half, offset, half + (offset ^ opposite(axis)))


def from_next(value, axis):
    count = lax.axis_size(axis)
    return lax.ppermute(value, axis, [(d, d - 1) for d in range(1, count)])


def stack_kernel(*refs):
    entries, out_ref = refs[:-1], refs[-1]
    for j, entry in enumerate(entries):
        for r in range(2):
            out_ref[r * len(entries) + j] = entry[r]


def stack(entries):
    _, rows, columns = entries[0].shape
    return pl.pallas_call(
        stack_kernel,
        in_specs=[vmem_spec()] * len(entries),
        out_specs=vmem_spec(),
        out_shape=pltpu.VMEM((2 * len(entries), rows, columns), entries[0].dtype),
        compiler_params=params(16),
        name="stack",
    )(*entries)


def project_kernel(given, slots, *refs):
    base_refs, (factors_ref, out_ref, tail_ref, wide, narrow, half) = refs[:given], refs[given:]
    aux, npno = factors_ref.shape[0], narrow.shape[2]

    @pl.when(pl.program_id(0) == 0)
    def _():
        for s in range(CAP):
            for j in range(given):

                @pl.when(lax.rem(slots[s], given) == j)
                def _():
                    narrow[s] = base_refs[j][slots[s] // given]

            wide[pl.ds(s * npno, npno), :] = narrow[s].astype(F32).T.astype(BF16)

    first = pl.program_id(0) * (aux // 2)
    for k in range(aux):
        left = jnp.dot(wide[...], factors_ref[k], preferred_element_type=F32).astype(BF16)
        for s in range(CAP):
            half[s, pl.ds(k * npno, npno), :] = left[s * npno : (s + 1) * npno]
    for s in range(CAP):
        both = jnp.dot(half[s], narrow[s], preferred_element_type=F32).astype(BF16)
        for k in range(aux):
            block = both[k * npno : (k + 1) * npno]
            if s < CAP - 1:
                out_ref[s, first + k // 2, :, pl.ds((k % 2) * npno, npno)] = block
            else:
                tail_ref[k // 2, :, pl.ds((k % 2) * npno, npno)] = block


def project(slots, group_bases, factor_block, step=8):
    aux, width, _ = factor_block.shape
    given = len(group_bases)
    npno = group_bases[0].shape[2]
    step = min(step, aux)

    def kernel(*refs):
        project_kernel(given, *refs)

    return pl.pallas_call(
        kernel,
        grid=(aux // step,),
        in_specs=[smem_spec()]
        + [vmem_spec()] * given
        + [pl.BlockSpec((step, width, width), lambda i: (i, 0, 0))],
        out_specs=[
            vmem_spec(),
            pl.BlockSpec((step // 2, npno, 2 * npno), lambda i: (i, 0, 0)),
        ],
        out_shape=[
            pltpu.VMEM((CAP - 1, aux // 2, npno, 2 * npno), BF16),
            pltpu.HBM((aux // 2, npno, 2 * npno), BF16),
        ],
        scratch_shapes=[
            pltpu.VMEM((CAP * npno, width), BF16),
            pltpu.VMEM((CAP, width, npno), BF16),
            pltpu.VMEM((CAP, step * npno, width), BF16),
        ],
        compiler_params=params(24),
        cost_estimate=pl.CostEstimate(
            flops=4 * CAP * aux * npno * width * (width + npno) // 2,
            bytes_accessed=2 * aux * width * width,
            transcendentals=0,
        ),
        name="project",
    )(slots, *group_bases, in_hbm(factor_block))


def ladder_kernel(given, slots, pairs, *refs):
    amp_refs, (proj_ref, tail_ref) = refs[:given], refs[given : given + 2]
    out_refs, (twice, mixed, tail, sem) = refs[given + 2 : 2 * given + 2], refs[2 * given + 2 :]
    half, npno = proj_ref.shape[1], proj_ref.shape[2]
    fetch = pltpu.make_async_copy(tail_ref, tail, sem)
    fetch.start()
    twice[...] = jnp.zeros_like(twice)
    for out_ref in out_refs:
        out_ref[...] = jnp.zeros_like(out_ref)
    for s in range(CAP):
        for j in range(given):

            @pl.when(lax.rem(slots[s], given) == j)
            def _():
                amp = amp_refs[j][slots[s] // given]
                twice[pl.ds(0, npno), pl.ds(0, npno)] = amp
                twice[pl.ds(npno, npno), pl.ds(npno, npno)] = amp

        if s == CAP - 1:
            fetch.wait()
            source = tail
        else:
            source = proj_ref.at[s]
        flat = source[...].reshape(half * npno, 2 * npno)
        mixed[...] = jnp.dot(flat, twice[...], preferred_element_type=F32).astype(BF16)
        total = jnp.zeros((npno, npno), F32)
        for m in range(half):
            total = total + lax.dot_general(
                mixed[pl.ds(m * npno, npno), :],
                source[m],
                CONTRACT_LAST,
                preferred_element_type=F32,
            )
        narrow = total.astype(BF16)
        for j in range(given):

            @pl.when((pairs[s] >= 0) & (lax.rem(slots[s], given) == j))
            def _():
                out_refs[j][slots[s] // given] = narrow


def ladder(slots, pairs, group_amps, projected):
    given = len(group_amps)
    main, tail = projected
    half, npno = tail.shape[:2]

    def kernel(*refs):
        ladder_kernel(given, *refs)

    return pl.pallas_call(
        kernel,
        in_specs=[smem_spec()] * 2
        + [vmem_spec()] * (given + 1)
        + [pl.BlockSpec(memory_space=pl.ANY)],
        out_specs=[vmem_spec()] * given,
        out_shape=[pltpu.VMEM((2, npno, npno), BF16)] * given,
        scratch_shapes=[
            pltpu.VMEM((2 * npno, 2 * npno), BF16),
            pltpu.VMEM((half * npno, 2 * npno), BF16),
            pltpu.VMEM(tail.shape, BF16),
            pltpu.SemaphoreType.DMA,
        ],
        compiler_params=params(24),
        cost_estimate=pl.CostEstimate(
            flops=0,
            bytes_accessed=16 * CAP * half * npno**2,
            transcendentals=0,
        ),
        name="ladder",
    )(slots, pairs, *group_amps, main, in_hbm(tail))


def coupling_kernel(near, own_ref, next_ref, inter_ref, ints_ref, out_ref):
    count = own_ref.shape[0]
    total = ints_ref[0]
    for n in range(inter_ref.shape[1]):
        at = near[0, n]
        place = place_of(lax.rem(at, count), "dev")
        amp = jnp.where(at < count, own_ref[place], next_ref[place])
        inter = inter_ref[0, n]
        mixed = jnp.dot(inter, amp, preferred_element_type=F32).astype(BF16)
        total = total + lax.dot_general(
            mixed, inter, CONTRACT_LAST, preferred_element_type=F32
        )
    out_ref[...] = total


def coupling(near, own, following, inter, ints):
    return pl.pallas_call(
        coupling_kernel,
        in_specs=[smem_spec()] + [pl.BlockSpec()] * 4,
        out_specs=vmem_spec(),
        out_shape=pltpu.VMEM(ints.shape[1:], F32),
        compiler_params=params(16),
        cost_estimate=pl.CostEstimate(
            flops=4 * inter.shape[1] * inter.shape[2] ** 3, bytes_accessed=0, transcendentals=0
        ),
        name="coupling",
    )(near, own, following, in_hbm(inter), in_hbm(ints))


def fold_kernel(given, last, *refs):
    term_refs, (rest, down, across, far_down, far_across), (send, keep) = (
        refs[:given],
        refs[given : given + 5],
        refs[given + 5 :],
    )
    mine, other = (sum(ref[r].astype(F32) for ref in term_refs) for r in range(2))
    mine = mine + rest[...]
    keep[0] = mine
    if last:
        send[0] = other.astype(BF16)
    else:
        send[0] = other.astype(BF16)
        send[1] = (-mine / (down[...] + across[...])).astype(BF16)
        keep[1] = -other / (far_down[...] + far_across[...])


def fold(last, terms, rest, energies):
    given = len(terms)
    rows = 1 if last else 2

    def kernel(*refs):
        fold_kernel(given, last, *refs)

    return pl.pallas_call(
        kernel,
        in_specs=[vmem_spec()] * (given + 5),
        out_specs=[vmem_spec()] * 2,
        out_shape=[
            pltpu.VMEM((rows,) + rest.shape, BF16),
            pltpu.VMEM((rows,) + rest.shape, F32),
        ],
        compiler_params=params(16),
        name="fold",
    )(*terms, rest, *energies)


def finish_kernel(last, keep, got, down, across, out_ref):
    update = -(keep[0] + got[0].astype(F32)) / (down[...] + across[...])
    out_ref[0] = update.astype(out_ref.dtype)
    if not last:
        out_ref[1] = (keep[1] + got[1].astype(F32)).astype(out_ref.dtype)


def finish(last, keep, got, down, across):
    def kernel(*refs):
        finish_kernel(last, *refs)

    return pl.pallas_call(
        kernel,
        in_specs=[vmem_spec()] * 4,
        out_specs=vmem_spec(),
        out_shape=jax.ShapeDtypeStruct(keep.shape, F32) if last else pltpu.VMEM(keep.shape, BF16),
        compiler_params=params(16),
        name="finish",
    )(keep, got, down, across)


def on_device(
    amplitudes,
    bases,
    factors,
    intersections,
    pair_integrals,
    pno_energies,
    pair_shift,
    pair_atoms,
    pair_next,
):
    me = lax.axis_index("dev")
    count = lax.axis_size("dev")
    places = jnp.arange(count, dtype=jnp.int32)
    listed = jnp.any(pair_atoms == me, axis=1)
    before = places[None, :] < places[:, None]
    rank = jnp.sum(before & listed[None, :], axis=1)
    chosen = listed[None, :] & (rank[None, :] == jnp.arange(CAP)[:, None])
    pairs = jnp.sum(jnp.where(chosen, places[None, :] + 1, 0), axis=1) - 1
    slots = jnp.where(pairs >= 0, place_of(pairs, "dev"), 0)

    shifted = pno_energies + 0.5 * pair_shift[:, None]
    far_shifted = exchange(shifted, "dev", opposite("dev"))
    pair_bases = gather_across(bases, "dev")
    amps, far_shifted = lax.optimization_barrier((amplitudes, far_shifted))
    far_amps = exchange(amps, "dev", opposite("dev"))
    amps, pair_bases = lax.optimization_barrier((amps, pair_bases))
    group_bases = gather_near(pair_bases, "dev")
    group_amps = gather_near(jnp.concatenate([amps, far_amps], axis=0), "dev")
    energies = (shifted.reshape(-1, 1), shifted, far_shifted.reshape(-1, 1), far_shifted)
    projected = project(slots, group_bases, factors[0])
    group_amps, projected = lax.optimization_barrier((group_amps, projected))
    for iteration in range(ITERS):
        last = iteration + 1 == ITERS
        stacked = stack(group_amps)
        group_amps, stacked = lax.optimization_barrier((group_amps, stacked))
        following = from_next(stacked, "grp")
        terms = ladder(slots, pairs, group_amps, projected)
        rest = coupling(pair_next, stacked, following, intersections, pair_integrals)
        send, keep = fold(last, exchange_near(terms, "dev"), rest, energies)
        update = finish(last, keep, exchange(send, "dev", opposite("dev")), *energies[:2])
        if not last:
            group_amps = gather_near(update, "dev")
    return update


def solution(mesh):
    return jax.shard_map(
        on_device,
        mesh=mesh,
        in_specs=(
            P(("grp", "dev"), None, None),
            P(("grp", "dev"), None, None),
            P(("grp", "dev"), None, None, None),
            P(("grp", "dev"), None, None, None),
            P(("grp", "dev"), None, None),
            P(("grp", "dev"), None),
            P(("grp", "dev")),
            P("grp", None),
            P(("grp", "dev"), None),
        ),
        out_specs=P(("grp", "dev"), None, None),
        check_vma=False,
    )
```

```python
import jax
import jax.numpy as jnp
from jax import lax
from jax.experimental import pallas as pl
from jax.experimental.pallas import tpu as pltpu
from jax.sharding import PartitionSpec as P

CAP = 3
ITERS = 2
F32 = jnp.float32
BF16 = jnp.bfloat16
CONTRACT_LAST = (((1,), (1,)), ((), ()))


def vmem_spec():
    return pl.BlockSpec(memory_space=pltpu.VMEM)


def smem_spec():
    return pl.BlockSpec(memory_space=pltpu.SMEM)


def in_hbm(value):
    return pltpu.with_memory_space_constraint(value, pltpu.HBM)


def params(mib):
    return pltpu.CompilerParams(vmem_limit_bytes=mib * 2**20)


def exchange(value, axis, offset):
    count = lax.axis_size(axis)
    return lax.ppermute(value, axis, [(d, d ^ offset) for d in range(count)])


def opposite(axis):
    return lax.axis_size(axis) // 2


def copy_kernel(value_ref, out_ref):
    out_ref[...] = value_ref[...]


def in_vmem(value):
    return pl.pallas_call(
        copy_kernel,
        in_specs=[vmem_spec()],
        out_specs=vmem_spec(),
        out_shape=pltpu.VMEM(value.shape, value.dtype),
        compiler_params=params(16),
        name="in_vmem",
    )(value)


def join_kernel(value_ref, other_ref, out_ref):
    out_ref[0] = value_ref[0]
    out_ref[1] = other_ref[0]


def join(value, other):
    return pl.pallas_call(
        join_kernel,
        in_specs=[vmem_spec()] * 2,
        out_specs=vmem_spec(),
        out_shape=pltpu.VMEM((2,) + value.shape[1:], value.dtype),
        compiler_params=params(16),
        name="join",
    )(value, other)


def exchange_near(entries, axis):
    found = list(entries)
    for j in range(len(entries) - 1, 0, -1):
        found[j] = exchange(entries[j], axis, j)
    return found


def gather_near(pair, axis):
    return exchange_near([pair] * (lax.axis_size(axis) // 2), axis)


def place_of(device, axis):
    half = lax.axis_size(axis) // 2
    offset = device ^ lax.axis_index(axis)
    return jnp.where(offset < half, offset, half + (offset ^ opposite(axis)))


def from_next(value, axis):
    count = lax.axis_size(axis)
    return lax.ppermute(value, axis, [(d, d - 1) for d in range(1, count)])


def stack_kernel(*refs):
    entries, out_ref = refs[:-1], refs[-1]
    for j, entry in enumerate(entries):
        for r in range(2):
            out_ref[r * len(entries) + j] = entry[r]


def stack(entries):
    _, rows, columns = entries[0].shape
    return pl.pallas_call(
        stack_kernel,
        in_specs=[vmem_spec()] * len(entries),
        out_specs=vmem_spec(),
        out_shape=pltpu.VMEM((2 * len(entries), rows, columns), entries[0].dtype),
        compiler_params=params(16),
        name="stack",
    )(*entries)


def project_kernel(given, step, slots, *refs):
    base_refs, (factors_ref, out_ref, tail_ref) = refs[:given], refs[given : given + 3]
    held, wide, narrow, half, tail, in_sems, out_sems = refs[given + 3 :]
    aux, npno = held.shape[0], narrow.shape[2]
    blocks = step // 2

    def fetch(i):
        part = pl.ds(i * step, step)
        return pltpu.make_async_copy(factors_ref.at[part], held.at[part], in_sems.at[i])

    def put(i):
        part = pl.ds(i * blocks, blocks)
        return pltpu.make_async_copy(tail.at[part], tail_ref.at[part], out_sems.at[i])

    for i in range(aux // step):
        fetch(i).start()
    for s in range(CAP):
        for j in range(given):

            @pl.when(lax.rem(slots[s], given) == j)
            def _():
                narrow[s] = base_refs[j][slots[s] // given]

        wide[pl.ds(s * npno, npno), :] = narrow[s].astype(F32).T.astype(BF16)

    def body(i, carry):
        fetch(i).wait()
        for k in range(step):
            left = jnp.dot(wide[...], held[i * step + k], preferred_element_type=F32).astype(BF16)
            for s in range(CAP):
                half[s, pl.ds(k * npno, npno), :] = left[s * npno : (s + 1) * npno]
        for s in range(CAP - 1, -1, -1):
            both = jnp.dot(half[s], narrow[s], preferred_element_type=F32).astype(BF16)
            for k in range(step):
                block = both[k * npno : (k + 1) * npno]
                place = i * blocks + k // 2
                if s < CAP - 1:
                    out_ref[s, place, :, pl.ds((k % 2) * npno, npno)] = block
                else:
                    tail[place, :, pl.ds((k % 2) * npno, npno)] = block
            if s == CAP - 1:
                put(i).start()
        return carry

    lax.fori_loop(0, aux // step, body, 0)
    for i in range(aux // step):
        put(i).wait()


def project(slots, group_bases, factor_block, step=8):
    aux, width, _ = factor_block.shape
    given = len(group_bases)
    npno = group_bases[0].shape[2]
    step = min(step, aux)

    def kernel(*refs):
        project_kernel(given, step, *refs)

    return pl.pallas_call(
        kernel,
        in_specs=[smem_spec()] + [vmem_spec()] * given + [pl.BlockSpec(memory_space=pl.ANY)],
        out_specs=[vmem_spec(), pl.BlockSpec(memory_space=pl.ANY)],
        out_shape=[
            pltpu.VMEM((CAP - 1, aux // 2, npno, 2 * npno), BF16),
            pltpu.HBM((aux // 2, npno, 2 * npno), BF16),
        ],
        scratch_shapes=[
            pltpu.VMEM(factor_block.shape, BF16),
            pltpu.VMEM((CAP * npno, width), BF16),
            pltpu.VMEM((CAP, width, npno), BF16),
            pltpu.VMEM((CAP, step * npno, width), BF16),
            pltpu.VMEM((aux // 2, npno, 2 * npno), BF16),
            pltpu.SemaphoreType.DMA((aux // step,)),
            pltpu.SemaphoreType.DMA((aux // step,)),
        ],
        compiler_params=params(24),
        cost_estimate=pl.CostEstimate(
            flops=4 * CAP * aux * npno * width * (width + npno) // 2,
            bytes_accessed=2 * aux * width * width,
            transcendentals=0,
        ),
        name="project",
    )(slots, *group_bases, in_hbm(factor_block))


def ladder_kernel(given, slots, pairs, *refs):
    amp_refs, (proj_ref, tail_ref) = refs[:given], refs[given : given + 2]
    out_refs, (twice, mixed, tail, sem) = refs[given + 2 : 2 * given + 2], refs[2 * given + 2 :]
    half, npno = proj_ref.shape[1], proj_ref.shape[2]
    fetch = pltpu.make_async_copy(tail_ref, tail, sem)
    fetch.start()
    twice[...] = jnp.zeros_like(twice)
    for out_ref in out_refs:
        out_ref[...] = jnp.zeros_like(out_ref)
    for s in range(CAP):
        for j in range(given):

            @pl.when(lax.rem(slots[s], given) == j)
            def _():
                amp = amp_refs[j][slots[s] // given]
                twice[pl.ds(0, npno), pl.ds(0, npno)] = amp
                twice[pl.ds(npno, npno), pl.ds(npno, npno)] = amp

        if s == CAP - 1:
            fetch.wait()
            source = tail
        else:
            source = proj_ref.at[s]
        flat = source[...].reshape(half * npno, 2 * npno)
        mixed[...] = jnp.dot(flat, twice[...], preferred_element_type=F32).astype(BF16)
        total = jnp.zeros((npno, npno), F32)
        for m in range(half):
            total = total + lax.dot_general(
                mixed[pl.ds(m * npno, npno), :],
                source[m],
                CONTRACT_LAST,
                preferred_element_type=F32,
            )
        narrow = total.astype(BF16)
        for j in range(given):

            @pl.when((pairs[s] >= 0) & (lax.rem(slots[s], given) == j))
            def _():
                out_refs[j][slots[s] // given] = narrow


def ladder(slots, pairs, group_amps, projected):
    given = len(group_amps)
    main, tail = projected
    half, npno = tail.shape[:2]

    def kernel(*refs):
        ladder_kernel(given, *refs)

    return pl.pallas_call(
        kernel,
        in_specs=[smem_spec()] * 2
        + [vmem_spec()] * (given + 1)
        + [pl.BlockSpec(memory_space=pl.ANY)],
        out_specs=[vmem_spec()] * given,
        out_shape=[pltpu.VMEM((2, npno, npno), BF16)] * given,
        scratch_shapes=[
            pltpu.VMEM((2 * npno, 2 * npno), BF16),
            pltpu.VMEM((half * npno, 2 * npno), BF16),
            pltpu.VMEM(tail.shape, BF16),
            pltpu.SemaphoreType.DMA,
        ],
        compiler_params=params(24),
        cost_estimate=pl.CostEstimate(
            flops=0,
            bytes_accessed=16 * CAP * half * npno**2,
            transcendentals=0,
        ),
        name="ladder",
    )(slots, pairs, *group_amps, main, in_hbm(tail))


def coupling_kernel(near, own_ref, next_ref, inter_ref, ints_ref, out_ref):
    count = own_ref.shape[0]
    total = ints_ref[0]
    for n in range(inter_ref.shape[1]):
        at = near[0, n]
        place = place_of(lax.rem(at, count), "dev")
        amp = jnp.where(at < count, own_ref[place], next_ref[place])
        inter = inter_ref[0, n]
        mixed = jnp.dot(inter, amp, preferred_element_type=F32).astype(BF16)
        total = total + lax.dot_general(
            mixed, inter, CONTRACT_LAST, preferred_element_type=F32
        )
    out_ref[...] = total


def coupling(near, own, following, inter, ints):
    return pl.pallas_call(
        coupling_kernel,
        in_specs=[smem_spec()] + [pl.BlockSpec()] * 4,
        out_specs=vmem_spec(),
        out_shape=pltpu.VMEM(ints.shape[1:], F32),
        compiler_params=params(16),
        cost_estimate=pl.CostEstimate(
            flops=4 * inter.shape[1] * inter.shape[2] ** 3, bytes_accessed=0, transcendentals=0
        ),
        name="coupling",
    )(near, own, following, in_hbm(inter), in_hbm(ints))


def fold_kernel(given, last, *refs):
    term_refs, (rest, down, across, far_down, far_across), (send, keep) = (
        refs[:given],
        refs[given : given + 5],
        refs[given + 5 :],
    )
    mine, other = (sum(ref[r].astype(F32) for ref in term_refs) for r in range(2))
    mine = mine + rest[...]
    keep[0] = mine
    if last:
        send[0] = other.astype(BF16)
    else:
        send[0] = other.astype(BF16)
        send[1] = (-mine / (down[...] + across[...])).astype(BF16)
        keep[1] = -other / (far_down[...] + far_across[...])


def fold(last, terms, rest, energies):
    given = len(terms)
    rows = 1 if last else 2

    def kernel(*refs):
        fold_kernel(given, last, *refs)

    return pl.pallas_call(
        kernel,
        in_specs=[vmem_spec()] * (given + 5),
        out_specs=[vmem_spec()] * 2,
        out_shape=[
            pltpu.VMEM((rows,) + rest.shape, BF16),
            pltpu.VMEM((rows,) + rest.shape, F32),
        ],
        compiler_params=params(16),
        name="fold",
    )(*terms, rest, *energies)


def finish_kernel(last, keep, got, down, across, out_ref):
    update = -(keep[0] + got[0].astype(F32)) / (down[...] + across[...])
    out_ref[0] = update.astype(out_ref.dtype)
    if not last:
        out_ref[1] = (keep[1] + got[1].astype(F32)).astype(out_ref.dtype)


def finish(last, keep, got, down, across):
    def kernel(*refs):
        finish_kernel(last, *refs)

    return pl.pallas_call(
        kernel,
        in_specs=[vmem_spec()] * 4,
        out_specs=vmem_spec(),
        out_shape=jax.ShapeDtypeStruct(keep.shape, F32) if last else pltpu.VMEM(keep.shape, BF16),
        compiler_params=params(16),
        name="finish",
    )(keep, got, down, across)


def on_device(
    amplitudes,
    bases,
    factors,
    intersections,
    pair_integrals,
    pno_energies,
    pair_shift,
    pair_atoms,
    pair_next,
):
    me = lax.axis_index("dev")
    count = lax.axis_size("dev")
    places = jnp.arange(count, dtype=jnp.int32)
    listed = jnp.any(pair_atoms == me, axis=1)
    before = places[None, :] < places[:, None]
    rank = jnp.sum(before & listed[None, :], axis=1)
    chosen = listed[None, :] & (rank[None, :] == jnp.arange(CAP)[:, None])
    pairs = jnp.sum(jnp.where(chosen, places[None, :] + 1, 0), axis=1) - 1
    slots = jnp.where(pairs >= 0, place_of(pairs, "dev"), 0)

    shifted = pno_energies + 0.5 * pair_shift[:, None]
    far_shifted = exchange(shifted, "dev", opposite("dev"))
    pair_bases = join(in_vmem(bases), exchange(bases, "dev", opposite("dev")))
    amps, far_shifted = lax.optimization_barrier((amplitudes, far_shifted))
    far_amps = exchange(amps, "dev", opposite("dev"))
    amps, pair_bases = lax.optimization_barrier((amps, pair_bases))
    group_bases = gather_near(pair_bases, "dev")
    group_amps = gather_near(jnp.concatenate([amps, far_amps], axis=0), "dev")
    energies = (shifted.reshape(-1, 1), shifted, far_shifted.reshape(-1, 1), far_shifted)
    projected = project(slots, group_bases, factors[0])
    group_amps, projected = lax.optimization_barrier((group_amps, projected))
    for iteration in range(ITERS):
        last = iteration + 1 == ITERS
        stacked = stack(group_amps)
        group_amps, stacked = lax.optimization_barrier((group_amps, stacked))
        following = from_next(stacked, "grp")
        terms = ladder(slots, pairs, group_amps, projected)
        rest = coupling(pair_next, stacked, following, intersections, pair_integrals)
        send, keep = fold(last, exchange_near(terms, "dev"), rest, energies)
        update = finish(last, keep, exchange(send, "dev", opposite("dev")), *energies[:2])
        if not last:
            group_amps = gather_near(update, "dev")
    return update


def solution(mesh):
    return jax.shard_map(
        on_device,
        mesh=mesh,
        in_specs=(
            P(("grp", "dev"), None, None),
            P(("grp", "dev"), None, None),
            P(("grp", "dev"), None, None, None),
            P(("grp", "dev"), None, None, None),
            P(("grp", "dev"), None, None),
            P(("grp", "dev"), None),
            P(("grp", "dev")),
            P("grp", None),
            P(("grp", "dev"), None),
        ),
        out_specs=P(("grp", "dev"), None, None),
        check_vma=False,
    )
```

```python
import jax
import jax.numpy as jnp
from jax import lax
from jax.experimental import pallas as pl
from jax.experimental.pallas import tpu as pltpu
from jax.sharding import PartitionSpec as P

CAP = 3
ITERS = 2
F32 = jnp.float32
BF16 = jnp.bfloat16
CONTRACT_LAST = (((1,), (1,)), ((), ()))


def vmem_spec():
    return pl.BlockSpec(memory_space=pltpu.VMEM)


def smem_spec():
    return pl.BlockSpec(memory_space=pltpu.SMEM)


def in_hbm(value):
    return pltpu.with_memory_space_constraint(value, pltpu.HBM)


def params(mib):
    return pltpu.CompilerParams(vmem_limit_bytes=mib * 2**20)


def exchange(value, axis, offset):
    count = lax.axis_size(axis)
    return lax.ppermute(value, axis, [(d, d ^ offset) for d in range(count)])


def opposite(axis):
    return lax.axis_size(axis) // 2


def copy_kernel(value_ref, out_ref):
    out_ref[...] = value_ref[...]


def in_vmem(value):
    return pl.pallas_call(
        copy_kernel,
        in_specs=[vmem_spec()],
        out_specs=vmem_spec(),
        out_shape=pltpu.VMEM(value.shape, value.dtype),
        compiler_params=params(16),
        name="in_vmem",
    )(value)


def join_kernel(value_ref, other_ref, out_ref):
    out_ref[0] = value_ref[0]
    out_ref[1] = other_ref[0]


def join(value, other):
    return pl.pallas_call(
        join_kernel,
        in_specs=[vmem_spec()] * 2,
        out_specs=vmem_spec(),
        out_shape=pltpu.VMEM((2,) + value.shape[1:], value.dtype),
        compiler_params=params(16),
        name="join",
    )(value, other)


def exchange_near(entries, axis):
    found = list(entries)
    for j in range(len(entries) - 1, 0, -1):
        found[j] = exchange(entries[j], axis, j)
    return found


def gather_near(pair, axis):
    return exchange_near([pair] * (lax.axis_size(axis) // 2), axis)


def place_of(device, axis):
    half = lax.axis_size(axis) // 2
    offset = device ^ lax.axis_index(axis)
    return jnp.where(offset < half, offset, half + (offset ^ opposite(axis)))


def from_next(value, axis):
    count = lax.axis_size(axis)
    return lax.ppermute(value, axis, [(d, d - 1) for d in range(1, count)])


def stack_kernel(*refs):
    entries, out_ref = refs[:-1], refs[-1]
    for j, entry in enumerate(entries):
        for r in range(2):
            out_ref[r * len(entries) + j] = entry[r]


def stack(entries):
    _, rows, columns = entries[0].shape
    return pl.pallas_call(
        stack_kernel,
        in_specs=[vmem_spec()] * len(entries),
        out_specs=vmem_spec(),
        out_shape=pltpu.VMEM((2 * len(entries), rows, columns), entries[0].dtype),
        compiler_params=params(16),
        name="stack",
    )(*entries)


def project_kernel(given, step, slots, *refs):
    base_refs, (factors_ref, out_ref, tail_ref) = refs[:given], refs[given : given + 3]
    held, wide, narrow, half, tail, in_sems, out_sems = refs[given + 3 :]
    aux, npno = held.shape[0], narrow.shape[2]
    blocks = step // 2

    def fetch(i):
        part = pl.ds(i * step, step)
        return pltpu.make_async_copy(factors_ref.at[part], held.at[part], in_sems.at[i])

    def put(i):
        part = pl.ds(i * blocks, blocks)
        return pltpu.make_async_copy(tail.at[part], tail_ref.at[part], out_sems.at[i])

    for i in range(aux // step):
        fetch(i).start()
    for s in range(CAP):
        for j in range(given):

            @pl.when(lax.rem(slots[s], given) == j)
            def _():
                narrow[s] = base_refs[j][slots[s] // given]

        wide[pl.ds(s * npno, npno), :] = narrow[s].astype(F32).T.astype(BF16)

    def body(i, carry):
        fetch(i).wait()
        for k in range(step):
            left = jnp.dot(wide[...], held[i * step + k], preferred_element_type=F32).astype(BF16)
            for s in range(CAP):
                half[s, pl.ds(k * npno, npno), :] = left[s * npno : (s + 1) * npno]
        for s in range(CAP - 1, -1, -1):
            both = jnp.dot(half[s], narrow[s], preferred_element_type=F32).astype(BF16)
            for k in range(step):
                block = both[k * npno : (k + 1) * npno]
                place = i * blocks + k // 2
                if s < CAP - 1:
                    out_ref[s, place, :, pl.ds((k % 2) * npno, npno)] = block
                else:
                    tail[place, :, pl.ds((k % 2) * npno, npno)] = block
            if s == CAP - 1:
                put(i).start()
        return carry

    lax.fori_loop(0, aux // step, body, 0)
    for i in range(aux // step):
        put(i).wait()


def project(slots, group_bases, factor_block, step=8):
    aux, width, _ = factor_block.shape
    given = len(group_bases)
    npno = group_bases[0].shape[2]
    step = min(step, aux)

    def kernel(*refs):
        project_kernel(given, step, *refs)

    return pl.pallas_call(
        kernel,
        in_specs=[smem_spec()] + [vmem_spec()] * given + [pl.BlockSpec(memory_space=pl.ANY)],
        out_specs=[vmem_spec(), pl.BlockSpec(memory_space=pl.ANY)],
        out_shape=[
            pltpu.VMEM((CAP - 1, aux // 2, npno, 2 * npno), BF16),
            pltpu.HBM((aux // 2, npno, 2 * npno), BF16),
        ],
        scratch_shapes=[
            pltpu.VMEM(factor_block.shape, BF16),
            pltpu.VMEM((CAP * npno, width), BF16),
            pltpu.VMEM((CAP, width, npno), BF16),
            pltpu.VMEM((CAP, step * npno, width), BF16),
            pltpu.VMEM((aux // 2, npno, 2 * npno), BF16),
            pltpu.SemaphoreType.DMA((aux // step,)),
            pltpu.SemaphoreType.DMA((aux // step,)),
        ],
        compiler_params=params(24),
        cost_estimate=pl.CostEstimate(
            flops=4 * CAP * aux * npno * width * (width + npno) // 2,
            bytes_accessed=2 * aux * width * width,
            transcendentals=0,
        ),
        name="project",
    )(slots, *group_bases, in_hbm(factor_block))


def ladder_kernel(given, slots, pairs, *refs):
    amp_refs, (proj_ref, tail_ref) = refs[:given], refs[given : given + 2]
    out_refs, (twice, mixed, tail, sem) = refs[given + 2 : 2 * given + 2], refs[2 * given + 2 :]
    half, npno = proj_ref.shape[1], proj_ref.shape[2]
    fetch = pltpu.make_async_copy(tail_ref, tail, sem)
    fetch.start()
    twice[...] = jnp.zeros_like(twice)
    for out_ref in out_refs:
        out_ref[...] = jnp.zeros_like(out_ref)
    for s in range(CAP):
        for j in range(given):

            @pl.when(lax.rem(slots[s], given) == j)
            def _():
                amp = amp_refs[j][slots[s] // given]
                twice[pl.ds(0, npno), pl.ds(0, npno)] = amp
                twice[pl.ds(npno, npno), pl.ds(npno, npno)] = amp

        if s == CAP - 1:
            fetch.wait()
            source = tail
        else:
            source = proj_ref.at[s]
        total = jnp.zeros((npno, npno), F32)
        chunk = min(4, half)
        for c in range(0, half, chunk):
            part = pl.ds(c * npno, chunk * npno)
            flat = source[pl.ds(c, chunk)].reshape(chunk * npno, 2 * npno)
            mixed[part, :] = jnp.dot(flat, twice[...], preferred_element_type=F32).astype(BF16)
            for m in range(c, c + chunk):
                total = total + lax.dot_general(
                    mixed[pl.ds(m * npno, npno), :],
                    source[m],
                    CONTRACT_LAST,
                    preferred_element_type=F32,
                )
        narrow = total.astype(BF16)
        for j in range(given):

            @pl.when((pairs[s] >= 0) & (lax.rem(slots[s], given) == j))
            def _():
                out_refs[j][slots[s] // given] = narrow


def ladder(slots, pairs, group_amps, projected):
    given = len(group_amps)
    main, tail = projected
    half, npno = tail.shape[:2]

    def kernel(*refs):
        ladder_kernel(given, *refs)

    return pl.pallas_call(
        kernel,
        in_specs=[smem_spec()] * 2
        + [vmem_spec()] * (given + 1)
        + [pl.BlockSpec(memory_space=pl.ANY)],
        out_specs=[vmem_spec()] * given,
        out_shape=[pltpu.VMEM((2, npno, npno), BF16)] * given,
        scratch_shapes=[
            pltpu.VMEM((2 * npno, 2 * npno), BF16),
            pltpu.VMEM((half * npno, 2 * npno), BF16),
            pltpu.VMEM(tail.shape, BF16),
            pltpu.SemaphoreType.DMA,
        ],
        compiler_params=params(24),
        cost_estimate=pl.CostEstimate(
            flops=0,
            bytes_accessed=16 * CAP * half * npno**2,
            transcendentals=0,
        ),
        name="ladder",
    )(slots, pairs, *group_amps, main, in_hbm(tail))


def coupling_kernel(near, own_ref, next_ref, inter_ref, ints_ref, out_ref):
    count = own_ref.shape[0]
    total = ints_ref[0]
    for n in range(inter_ref.shape[1]):
        at = near[0, n]
        place = place_of(lax.rem(at, count), "dev")
        amp = jnp.where(at < count, own_ref[place], next_ref[place])
        inter = inter_ref[0, n]
        mixed = jnp.dot(inter, amp, preferred_element_type=F32).astype(BF16)
        total = total + lax.dot_general(
            mixed, inter, CONTRACT_LAST, preferred_element_type=F32
        )
    out_ref[...] = total


def coupling(near, own, following, inter, ints):
    return pl.pallas_call(
        coupling_kernel,
        in_specs=[smem_spec()] + [pl.BlockSpec()] * 4,
        out_specs=vmem_spec(),
        out_shape=pltpu.VMEM(ints.shape[1:], F32),
        compiler_params=params(16),
        cost_estimate=pl.CostEstimate(
            flops=4 * inter.shape[1] * inter.shape[2] ** 3, bytes_accessed=0, transcendentals=0
        ),
        name="coupling",
    )(near, own, following, in_hbm(inter), in_hbm(ints))


def fold_kernel(given, last, *refs):
    term_refs, (rest, down, across, far_down, far_across), (send, keep) = (
        refs[:given],
        refs[given : given + 5],
        refs[given + 5 :],
    )
    mine, other = (sum(ref[r].astype(F32) for ref in term_refs) for r in range(2))
    mine = mine + rest[...]
    keep[0] = mine
    if last:
        send[0] = other.astype(BF16)
    else:
        send[0] = other.astype(BF16)
        send[1] = (-mine / (down[...] + across[...])).astype(BF16)
        keep[1] = -other / (far_down[...] + far_across[...])


def fold(last, terms, rest, energies):
    given = len(terms)
    rows = 1 if last else 2

    def kernel(*refs):
        fold_kernel(given, last, *refs)

    return pl.pallas_call(
        kernel,
        in_specs=[vmem_spec()] * (given + 5),
        out_specs=[vmem_spec()] * 2,
        out_shape=[
            pltpu.VMEM((rows,) + rest.shape, BF16),
            pltpu.VMEM((rows,) + rest.shape, F32),
        ],
        compiler_params=params(16),
        name="fold",
    )(*terms, rest, *energies)


def finish_kernel(last, keep, got, down, across, out_ref):
    update = -(keep[0] + got[0].astype(F32)) / (down[...] + across[...])
    out_ref[0] = update.astype(out_ref.dtype)
    if not last:
        out_ref[1] = (keep[1] + got[1].astype(F32)).astype(out_ref.dtype)


def finish(last, keep, got, down, across):
    def kernel(*refs):
        finish_kernel(last, *refs)

    return pl.pallas_call(
        kernel,
        in_specs=[vmem_spec()] * 4,
        out_specs=vmem_spec(),
        out_shape=jax.ShapeDtypeStruct(keep.shape, F32) if last else pltpu.VMEM(keep.shape, BF16),
        compiler_params=params(16),
        name="finish",
    )(keep, got, down, across)


def on_device(
    amplitudes,
    bases,
    factors,
    intersections,
    pair_integrals,
    pno_energies,
    pair_shift,
    pair_atoms,
    pair_next,
):
    me = lax.axis_index("dev")
    count = lax.axis_size("dev")
    places = jnp.arange(count, dtype=jnp.int32)
    listed = jnp.any(pair_atoms == me, axis=1)
    before = places[None, :] < places[:, None]
    rank = jnp.sum(before & listed[None, :], axis=1)
    chosen = listed[None, :] & (rank[None, :] == jnp.arange(CAP)[:, None])
    pairs = jnp.sum(jnp.where(chosen, places[None, :] + 1, 0), axis=1) - 1
    slots = jnp.where(pairs >= 0, place_of(pairs, "dev"), 0)

    shifted = pno_energies + 0.5 * pair_shift[:, None]
    far_shifted = exchange(shifted, "dev", opposite("dev"))
    pair_bases = join(in_vmem(bases), exchange(bases, "dev", opposite("dev")))
    amps, far_shifted = lax.optimization_barrier((amplitudes, far_shifted))
    far_amps = exchange(amps, "dev", opposite("dev"))
    amps, pair_bases = lax.optimization_barrier((amps, pair_bases))
    group_bases = gather_near(pair_bases, "dev")
    group_amps = gather_near(jnp.concatenate([amps, far_amps], axis=0), "dev")
    energies = (shifted.reshape(-1, 1), shifted, far_shifted.reshape(-1, 1), far_shifted)
    projected = project(slots, group_bases, factors[0])
    group_amps, projected = lax.optimization_barrier((group_amps, projected))
    for iteration in range(ITERS):
        last = iteration + 1 == ITERS
        stacked = stack(group_amps)
        group_amps, stacked = lax.optimization_barrier((group_amps, stacked))
        following = from_next(stacked, "grp")
        terms = ladder(slots, pairs, group_amps, projected)
        rest = coupling(pair_next, stacked, following, intersections, pair_integrals)
        send, keep = fold(last, exchange_near(terms, "dev"), rest, energies)
        update = finish(last, keep, exchange(send, "dev", opposite("dev")), *energies[:2])
        if not last:
            group_amps = gather_near(update, "dev")
    return update


def solution(mesh):
    return jax.shard_map(
        on_device,
        mesh=mesh,
        in_specs=(
            P(("grp", "dev"), None, None),
            P(("grp", "dev"), None, None),
            P(("grp", "dev"), None, None, None),
            P(("grp", "dev"), None, None, None),
            P(("grp", "dev"), None, None),
            P(("grp", "dev"), None),
            P(("grp", "dev")),
            P("grp", None),
            P(("grp", "dev"), None),
        ),
        out_specs=P(("grp", "dev"), None, None),
        check_vma=False,
    )
```

```python
import jax
import jax.numpy as jnp
from jax import lax
from jax.experimental import pallas as pl
from jax.experimental.pallas import tpu as pltpu
from jax.sharding import PartitionSpec as P

CAP = 3
ITERS = 2
F32 = jnp.float32
BF16 = jnp.bfloat16
CONTRACT_LAST = (((1,), (1,)), ((), ()))


def vmem_spec():
    return pl.BlockSpec(memory_space=pltpu.VMEM)


def smem_spec():
    return pl.BlockSpec(memory_space=pltpu.SMEM)


def in_hbm(value):
    return pltpu.with_memory_space_constraint(value, pltpu.HBM)


def params(mib):
    return pltpu.CompilerParams(vmem_limit_bytes=mib * 2**20)


def exchange(value, axis, offset):
    count = lax.axis_size(axis)
    return lax.ppermute(value, axis, [(d, d ^ offset) for d in range(count)])


def opposite(axis):
    return lax.axis_size(axis) // 2


def copy_kernel(value_ref, out_ref):
    out_ref[...] = value_ref[...]


def in_vmem(value):
    return pl.pallas_call(
        copy_kernel,
        in_specs=[vmem_spec()],
        out_specs=vmem_spec(),
        out_shape=pltpu.VMEM(value.shape, value.dtype),
        compiler_params=params(16),
        name="in_vmem",
    )(value)


def join_kernel(value_ref, other_ref, out_ref):
    out_ref[0] = value_ref[0]
    out_ref[1] = other_ref[0]


def join(value, other):
    return pl.pallas_call(
        join_kernel,
        in_specs=[vmem_spec()] * 2,
        out_specs=vmem_spec(),
        out_shape=pltpu.VMEM((2,) + value.shape[1:], value.dtype),
        compiler_params=params(16),
        name="join",
    )(value, other)


def exchange_near(entries, axis):
    found = list(entries)
    for j in range(len(entries) - 1, 0, -1):
        found[j] = exchange(entries[j], axis, j)
    return found


def gather_near(pair, axis):
    return exchange_near([pair] * (lax.axis_size(axis) // 2), axis)


def place_of(device, axis):
    half = lax.axis_size(axis) // 2
    offset = device ^ lax.axis_index(axis)
    return jnp.where(offset < half, offset, half + (offset ^ opposite(axis)))


def from_next(value, axis):
    count = lax.axis_size(axis)
    return lax.ppermute(value, axis, [(d, d - 1) for d in range(1, count)])


def stack_kernel(*refs):
    entries, out_ref = refs[:-1], refs[-1]
    for j, entry in enumerate(entries):
        for r in range(2):
            out_ref[r * len(entries) + j] = entry[r]


def stack(entries):
    _, rows, columns = entries[0].shape
    return pl.pallas_call(
        stack_kernel,
        in_specs=[vmem_spec()] * len(entries),
        out_specs=vmem_spec(),
        out_shape=pltpu.VMEM((2 * len(entries), rows, columns), entries[0].dtype),
        compiler_params=params(16),
        name="stack",
    )(*entries)


def project_kernel(given, step, slots, *refs):
    base_refs, (factors_ref, out_ref, tail_ref) = refs[:given], refs[given : given + 3]
    held, wide, narrow, half, tail, in_sems, out_sems = refs[given + 3 :]
    aux, npno = held.shape[0], narrow.shape[2]
    blocks = step // 2

    def fetch(i):
        part = pl.ds(i * step, step)
        return pltpu.make_async_copy(factors_ref.at[part], held.at[part], in_sems.at[i])

    def put(i):
        part = pl.ds(i * blocks, blocks)
        return pltpu.make_async_copy(tail.at[part], tail_ref.at[part], out_sems.at[i])

    for i in range(aux // step):
        fetch(i).start()
    for s in range(CAP):
        for j in range(given):

            @pl.when(lax.rem(slots[s], given) == j)
            def _():
                narrow[s] = base_refs[j][slots[s] // given]

        wide[pl.ds(s * npno, npno), :] = narrow[s].astype(F32).T.astype(BF16)

    def body(i):
        fetch(i).wait()
        for k in range(step):
            left = jnp.dot(wide[...], held[i * step + k], preferred_element_type=F32).astype(BF16)
            for s in range(CAP):
                half[s, pl.ds(k * npno, npno), :] = left[s * npno : (s + 1) * npno]
        for s in range(CAP - 1, -1, -1):
            both = jnp.dot(half[s], narrow[s], preferred_element_type=F32).astype(BF16)
            for k in range(step):
                block = both[k * npno : (k + 1) * npno]
                place = i * blocks + k // 2
                if s < CAP - 1:
                    out_ref[s, place, :, pl.ds((k % 2) * npno, npno)] = block
                else:
                    tail[place, :, pl.ds((k % 2) * npno, npno)] = block
            if s == CAP - 1:
                put(i).start()

    for i in range(aux // step):
        body(i)
    for i in range(aux // step):
        put(i).wait()


def project(slots, group_bases, factor_block, step=8):
    aux, width, _ = factor_block.shape
    given = len(group_bases)
    npno = group_bases[0].shape[2]
    step = min(step, aux)

    def kernel(*refs):
        project_kernel(given, step, *refs)

    return pl.pallas_call(
        kernel,
        in_specs=[smem_spec()] + [vmem_spec()] * given + [pl.BlockSpec(memory_space=pl.ANY)],
        out_specs=[vmem_spec(), pl.BlockSpec(memory_space=pl.ANY)],
        out_shape=[
            pltpu.VMEM((CAP - 1, aux // 2, npno, 2 * npno), BF16),
            pltpu.HBM((aux // 2, npno, 2 * npno), BF16),
        ],
        scratch_shapes=[
            pltpu.VMEM(factor_block.shape, BF16),
            pltpu.VMEM((CAP * npno, width), BF16),
            pltpu.VMEM((CAP, width, npno), BF16),
            pltpu.VMEM((CAP, step * npno, width), BF16),
            pltpu.VMEM((aux // 2, npno, 2 * npno), BF16),
            pltpu.SemaphoreType.DMA((aux // step,)),
            pltpu.SemaphoreType.DMA((aux // step,)),
        ],
        compiler_params=params(24),
        cost_estimate=pl.CostEstimate(
            flops=4 * CAP * aux * npno * width * (width + npno) // 2,
            bytes_accessed=2 * aux * width * width,
            transcendentals=0,
        ),
        name="project",
    )(slots, *group_bases, in_hbm(factor_block))


def ladder_kernel(given, slots, pairs, *refs):
    amp_refs, (proj_ref, tail_ref) = refs[:given], refs[given : given + 2]
    out_refs, (twice, mixed, tail, sem) = refs[given + 2 : 2 * given + 2], refs[2 * given + 2 :]
    half, npno = proj_ref.shape[1], proj_ref.shape[2]
    fetch = pltpu.make_async_copy(tail_ref, tail, sem)
    fetch.start()
    twice[...] = jnp.zeros_like(twice)
    for out_ref in out_refs:
        out_ref[...] = jnp.zeros_like(out_ref)
    for s in range(CAP):
        for j in range(given):

            @pl.when(lax.rem(slots[s], given) == j)
            def _():
                amp = amp_refs[j][slots[s] // given]
                twice[pl.ds(0, npno), pl.ds(0, npno)] = amp
                twice[pl.ds(npno, npno), pl.ds(npno, npno)] = amp

        if s == CAP - 1:
            fetch.wait()
            source = tail
        else:
            source = proj_ref.at[s]
        flat = source[...].reshape(half * npno, 2 * npno)
        mixed[...] = jnp.dot(flat, twice[...], preferred_element_type=F32).astype(BF16)
        total = jnp.zeros((npno, npno), F32)
        for m in range(half):
            total = total + lax.dot_general(
                mixed[pl.ds(m * npno, npno), :],
                source[m],
                CONTRACT_LAST,
                preferred_element_type=F32,
            )
        narrow = total.astype(BF16)
        for j in range(given):

            @pl.when((pairs[s] >= 0) & (lax.rem(slots[s], given) == j))
            def _():
                out_refs[j][slots[s] // given] = narrow


def ladder(slots, pairs, group_amps, projected):
    given = len(group_amps)
    main, tail = projected
    half, npno = tail.shape[:2]

    def kernel(*refs):
        ladder_kernel(given, *refs)

    return pl.pallas_call(
        kernel,
        in_specs=[smem_spec()] * 2
        + [vmem_spec()] * (given + 1)
        + [pl.BlockSpec(memory_space=pl.ANY)],
        out_specs=[vmem_spec()] * given,
        out_shape=[pltpu.VMEM((2, npno, npno), BF16)] * given,
        scratch_shapes=[
            pltpu.VMEM((2 * npno, 2 * npno), BF16),
            pltpu.VMEM((half * npno, 2 * npno), BF16),
            pltpu.VMEM(tail.shape, BF16),
            pltpu.SemaphoreType.DMA,
        ],
        compiler_params=params(24),
        cost_estimate=pl.CostEstimate(
            flops=0,
            bytes_accessed=16 * CAP * half * npno**2,
            transcendentals=0,
        ),
        name="ladder",
    )(slots, pairs, *group_amps, main, in_hbm(tail))


def coupling_kernel(near, own_ref, next_ref, inter_ref, ints_ref, out_ref):
    count = own_ref.shape[0]
    total = ints_ref[0]
    for n in range(inter_ref.shape[1]):
        at = near[0, n]
        place = place_of(lax.rem(at, count), "dev")
        amp = jnp.where(at < count, own_ref[place], next_ref[place])
        inter = inter_ref[0, n]
        mixed = jnp.dot(inter, amp, preferred_element_type=F32).astype(BF16)
        total = total + lax.dot_general(
            mixed, inter, CONTRACT_LAST, preferred_element_type=F32
        )
    out_ref[...] = total


def coupling(near, own, following, inter, ints):
    return pl.pallas_call(
        coupling_kernel,
        in_specs=[smem_spec()] + [pl.BlockSpec()] * 4,
        out_specs=vmem_spec(),
        out_shape=pltpu.VMEM(ints.shape[1:], F32),
        compiler_params=params(16),
        cost_estimate=pl.CostEstimate(
            flops=4 * inter.shape[1] * inter.shape[2] ** 3, bytes_accessed=0, transcendentals=0
        ),
        name="coupling",
    )(near, own, following, in_hbm(inter), in_hbm(ints))


def fold_kernel(given, last, *refs):
    term_refs, (rest, down, across, far_down, far_across), (send, keep) = (
        refs[:given],
        refs[given : given + 5],
        refs[given + 5 :],
    )
    mine, other = (sum(ref[r].astype(F32) for ref in term_refs) for r in range(2))
    mine = mine + rest[...]
    keep[0] = mine
    if last:
        send[0] = other.astype(BF16)
    else:
        send[0] = other.astype(BF16)
        send[1] = (-mine / (down[...] + across[...])).astype(BF16)
        keep[1] = -other / (far_down[...] + far_across[...])


def fold(last, terms, rest, energies):
    given = len(terms)
    rows = 1 if last else 2

    def kernel(*refs):
        fold_kernel(given, last, *refs)

    return pl.pallas_call(
        kernel,
        in_specs=[vmem_spec()] * (given + 5),
        out_specs=[vmem_spec()] * 2,
        out_shape=[
            pltpu.VMEM((rows,) + rest.shape, BF16),
            pltpu.VMEM((rows,) + rest.shape, F32),
        ],
        compiler_params=params(16),
        name="fold",
    )(*terms, rest, *energies)


def finish_kernel(last, keep, got, down, across, out_ref):
    update = -(keep[0] + got[0].astype(F32)) / (down[...] + across[...])
    out_ref[0] = update.astype(out_ref.dtype)
    if not last:
        out_ref[1] = (keep[1] + got[1].astype(F32)).astype(out_ref.dtype)


def finish(last, keep, got, down, across):
    def kernel(*refs):
        finish_kernel(last, *refs)

    return pl.pallas_call(
        kernel,
        in_specs=[vmem_spec()] * 4,
        out_specs=vmem_spec(),
        out_shape=jax.ShapeDtypeStruct(keep.shape, F32) if last else pltpu.VMEM(keep.shape, BF16),
        compiler_params=params(16),
        name="finish",
    )(keep, got, down, across)


def on_device(
    amplitudes,
    bases,
    factors,
    intersections,
    pair_integrals,
    pno_energies,
    pair_shift,
    pair_atoms,
    pair_next,
):
    me = lax.axis_index("dev")
    count = lax.axis_size("dev")
    places = jnp.arange(count, dtype=jnp.int32)
    listed = jnp.any(pair_atoms == me, axis=1)
    before = places[None, :] < places[:, None]
    rank = jnp.sum(before & listed[None, :], axis=1)
    chosen = listed[None, :] & (rank[None, :] == jnp.arange(CAP)[:, None])
    pairs = jnp.sum(jnp.where(chosen, places[None, :] + 1, 0), axis=1) - 1
    slots = jnp.where(pairs >= 0, place_of(pairs, "dev"), 0)

    shifted = pno_energies + 0.5 * pair_shift[:, None]
    far_shifted = exchange(shifted, "dev", opposite("dev"))
    pair_bases = join(in_vmem(bases), exchange(bases, "dev", opposite("dev")))
    amps, far_shifted = lax.optimization_barrier((amplitudes, far_shifted))
    far_amps = exchange(amps, "dev", opposite("dev"))
    amps, pair_bases = lax.optimization_barrier((amps, pair_bases))
    group_bases = gather_near(pair_bases, "dev")
    group_amps = gather_near(jnp.concatenate([amps, far_amps], axis=0), "dev")
    energies = (shifted.reshape(-1, 1), shifted, far_shifted.reshape(-1, 1), far_shifted)
    projected = project(slots, group_bases, factors[0])
    group_amps, projected = lax.optimization_barrier((group_amps, projected))
    for iteration in range(ITERS):
        last = iteration + 1 == ITERS
        stacked = stack(group_amps)
        group_amps, stacked = lax.optimization_barrier((group_amps, stacked))
        following = from_next(stacked, "grp")
        terms = ladder(slots, pairs, group_amps, projected)
        rest = coupling(pair_next, stacked, following, intersections, pair_integrals)
        send, keep = fold(last, exchange_near(terms, "dev"), rest, energies)
        update = finish(last, keep, exchange(send, "dev", opposite("dev")), *energies[:2])
        if not last:
            group_amps = gather_near(update, "dev")
    return update


def solution(mesh):
    return jax.shard_map(
        on_device,
        mesh=mesh,
        in_specs=(
            P(("grp", "dev"), None, None),
            P(("grp", "dev"), None, None),
            P(("grp", "dev"), None, None, None),
            P(("grp", "dev"), None, None, None),
            P(("grp", "dev"), None, None),
            P(("grp", "dev"), None),
            P(("grp", "dev")),
            P("grp", None),
            P(("grp", "dev"), None),
        ),
        out_specs=P(("grp", "dev"), None, None),
        check_vma=False,
    )
```

```python
import jax
import jax.numpy as jnp
from jax import lax
from jax.experimental import pallas as pl
from jax.experimental.pallas import tpu as pltpu
from jax.sharding import PartitionSpec as P

CAP = 3
ITERS = 2
F32 = jnp.float32
BF16 = jnp.bfloat16
CONTRACT_LAST = (((1,), (1,)), ((), ()))


def vmem_spec():
    return pl.BlockSpec(memory_space=pltpu.VMEM)


def smem_spec():
    return pl.BlockSpec(memory_space=pltpu.SMEM)


def in_hbm(value):
    return pltpu.with_memory_space_constraint(value, pltpu.HBM)


def params(mib):
    return pltpu.CompilerParams(vmem_limit_bytes=mib * 2**20)


def exchange(value, axis, offset):
    count = lax.axis_size(axis)
    return lax.ppermute(value, axis, [(d, d ^ offset) for d in range(count)])


def opposite(axis):
    return lax.axis_size(axis) // 2


def copy_kernel(value_ref, out_ref):
    out_ref[...] = value_ref[...]


def in_vmem(value):
    return pl.pallas_call(
        copy_kernel,
        in_specs=[vmem_spec()],
        out_specs=vmem_spec(),
        out_shape=pltpu.VMEM(value.shape, value.dtype),
        compiler_params=params(16),
        name="in_vmem",
    )(value)


def join_kernel(value_ref, other_ref, out_ref):
    out_ref[0] = value_ref[0]
    out_ref[1] = other_ref[0]


def join(value, other):
    return pl.pallas_call(
        join_kernel,
        in_specs=[vmem_spec()] * 2,
        out_specs=vmem_spec(),
        out_shape=pltpu.VMEM((2,) + value.shape[1:], value.dtype),
        compiler_params=params(16),
        name="join",
    )(value, other)


def exchange_near(entries, axis):
    found = list(entries)
    for j in range(len(entries) - 1, 0, -1):
        found[j] = exchange(entries[j], axis, j)
    return found


def gather_near(pair, axis):
    return exchange_near([pair] * (lax.axis_size(axis) // 2), axis)


def place_of(device, axis):
    half = lax.axis_size(axis) // 2
    offset = device ^ lax.axis_index(axis)
    return jnp.where(offset < half, offset, half + (offset ^ opposite(axis)))


def from_next(value, axis):
    count = lax.axis_size(axis)
    return lax.ppermute(value, axis, [(d, d - 1) for d in range(1, count)])


def stack_kernel(*refs):
    entries, out_ref = refs[:-1], refs[-1]
    for j, entry in enumerate(entries):
        for r in range(2):
            out_ref[r * len(entries) + j] = entry[r]


def stack(entries):
    _, rows, columns = entries[0].shape
    return pl.pallas_call(
        stack_kernel,
        in_specs=[vmem_spec()] * len(entries),
        out_specs=vmem_spec(),
        out_shape=pltpu.VMEM((2 * len(entries), rows, columns), entries[0].dtype),
        compiler_params=params(16),
        name="stack",
    )(*entries)


def project_kernel(given, step, slots, *refs):
    base_refs, (factors_ref, out_ref, tail_ref) = refs[:given], refs[given : given + 3]
    held, wide, narrow, half, tail, in_sems, out_sems = refs[given + 3 :]
    aux, npno = held.shape[0], narrow.shape[2]
    blocks = step // 2

    def fetch(i):
        part = pl.ds(i * step, step)
        return pltpu.make_async_copy(factors_ref.at[part], held.at[part], in_sems.at[i])

    def put(i):
        part = pl.ds(i * blocks, blocks)
        return pltpu.make_async_copy(tail.at[part], tail_ref.at[part], out_sems.at[i])

    for i in range(aux // step):
        fetch(i).start()
    for s in range(CAP):
        for j in range(given):

            @pl.when(lax.rem(slots[s], given) == j)
            def _():
                narrow[s] = base_refs[j][slots[s] // given]

        wide[pl.ds(s * npno, npno), :] = narrow[s].astype(F32).T.astype(BF16)

    def body(i, carry):
        fetch(i).wait()
        for k in range(step):
            left = jnp.dot(wide[...], held[i * step + k], preferred_element_type=F32).astype(BF16)
            for s in range(CAP):
                half[s, pl.ds(k * npno, npno), :] = left[s * npno : (s + 1) * npno]
        for s in range(CAP - 1, -1, -1):
            both = jnp.dot(half[s], narrow[s], preferred_element_type=F32).astype(BF16)
            for k in range(step):
                block = both[k * npno : (k + 1) * npno]
                place = i * blocks + k // 2
                if s < CAP - 1:
                    out_ref[s, place, :, pl.ds((k % 2) * npno, npno)] = block
                else:
                    tail[place, :, pl.ds((k % 2) * npno, npno)] = block
            if s == CAP - 1:
                put(i).start()
        return carry

    lax.fori_loop(0, aux // step, body, 0)
    for i in range(aux // step):
        put(i).wait()


def project(slots, group_bases, factor_block, step=4):
    aux, width, _ = factor_block.shape
    given = len(group_bases)
    npno = group_bases[0].shape[2]
    step = min(step, aux)

    def kernel(*refs):
        project_kernel(given, step, *refs)

    return pl.pallas_call(
        kernel,
        in_specs=[smem_spec()] + [vmem_spec()] * given + [pl.BlockSpec(memory_space=pl.ANY)],
        out_specs=[vmem_spec(), pl.BlockSpec(memory_space=pl.ANY)],
        out_shape=[
            pltpu.VMEM((CAP - 1, aux // 2, npno, 2 * npno), BF16),
            pltpu.HBM((aux // 2, npno, 2 * npno), BF16),
        ],
        scratch_shapes=[
            pltpu.VMEM(factor_block.shape, BF16),
            pltpu.VMEM((CAP * npno, width), BF16),
            pltpu.VMEM((CAP, width, npno), BF16),
            pltpu.VMEM((CAP, step * npno, width), BF16),
            pltpu.VMEM((aux // 2, npno, 2 * npno), BF16),
            pltpu.SemaphoreType.DMA((aux // step,)),
            pltpu.SemaphoreType.DMA((aux // step,)),
        ],
        compiler_params=params(24),
        cost_estimate=pl.CostEstimate(
            flops=4 * CAP * aux * npno * width * (width + npno) // 2,
            bytes_accessed=2 * aux * width * width,
            transcendentals=0,
        ),
        name="project",
    )(slots, *group_bases, in_hbm(factor_block))


def ladder_kernel(given, slots, pairs, *refs):
    amp_refs, (proj_ref, tail_ref) = refs[:given], refs[given : given + 2]
    out_refs, (twice, mixed, tail, sem) = refs[given + 2 : 2 * given + 2], refs[2 * given + 2 :]
    half, npno = proj_ref.shape[1], proj_ref.shape[2]
    fetch = pltpu.make_async_copy(tail_ref, tail, sem)
    fetch.start()
    twice[...] = jnp.zeros_like(twice)
    for out_ref in out_refs:
        out_ref[...] = jnp.zeros_like(out_ref)
    for s in range(CAP):
        for j in range(given):

            @pl.when(lax.rem(slots[s], given) == j)
            def _():
                amp = amp_refs[j][slots[s] // given]
                twice[pl.ds(0, npno), pl.ds(0, npno)] = amp
                twice[pl.ds(npno, npno), pl.ds(npno, npno)] = amp

        if s == CAP - 1:
            fetch.wait()
            source = tail
        else:
            source = proj_ref.at[s]
        chunk = min(4, half)

        def body(c, total):
            flat = source[pl.ds(c * chunk, chunk)].reshape(chunk * npno, 2 * npno)
            mixed[...] = jnp.dot(flat, twice[...], preferred_element_type=F32).astype(BF16)
            for m in range(chunk):
                total = total + lax.dot_general(
                    mixed[pl.ds(m * npno, npno), :],
                    source[c * chunk + m],
                    CONTRACT_LAST,
                    preferred_element_type=F32,
                )
            return total

        total = lax.fori_loop(0, half // chunk, body, jnp.zeros((npno, npno), F32))
        narrow = total.astype(BF16)
        for j in range(given):

            @pl.when((pairs[s] >= 0) & (lax.rem(slots[s], given) == j))
            def _():
                out_refs[j][slots[s] // given] = narrow


def ladder(slots, pairs, group_amps, projected):
    given = len(group_amps)
    main, tail = projected
    half, npno = tail.shape[:2]

    def kernel(*refs):
        ladder_kernel(given, *refs)

    return pl.pallas_call(
        kernel,
        in_specs=[smem_spec()] * 2
        + [vmem_spec()] * (given + 1)
        + [pl.BlockSpec(memory_space=pl.ANY)],
        out_specs=[vmem_spec()] * given,
        out_shape=[pltpu.VMEM((2, npno, npno), BF16)] * given,
        scratch_shapes=[
            pltpu.VMEM((2 * npno, 2 * npno), BF16),
            pltpu.VMEM((min(4, half) * npno, 2 * npno), BF16),
            pltpu.VMEM(tail.shape, BF16),
            pltpu.SemaphoreType.DMA,
        ],
        compiler_params=params(24),
        cost_estimate=pl.CostEstimate(
            flops=0,
            bytes_accessed=16 * CAP * half * npno**2,
            transcendentals=0,
        ),
        name="ladder",
    )(slots, pairs, *group_amps, main, in_hbm(tail))


def coupling_kernel(near, own_ref, next_ref, inter_ref, ints_ref, out_ref):
    count = own_ref.shape[0]
    total = ints_ref[0]
    for n in range(inter_ref.shape[1]):
        at = near[0, n]
        place = place_of(lax.rem(at, count), "dev")
        amp = jnp.where(at < count, own_ref[place], next_ref[place])
        inter = inter_ref[0, n]
        mixed = jnp.dot(inter, amp, preferred_element_type=F32).astype(BF16)
        total = total + lax.dot_general(
            mixed, inter, CONTRACT_LAST, preferred_element_type=F32
        )
    out_ref[...] = total


def coupling(near, own, following, inter, ints):
    return pl.pallas_call(
        coupling_kernel,
        in_specs=[smem_spec()] + [pl.BlockSpec()] * 4,
        out_specs=vmem_spec(),
        out_shape=pltpu.VMEM(ints.shape[1:], F32),
        compiler_params=params(16),
        cost_estimate=pl.CostEstimate(
            flops=4 * inter.shape[1] * inter.shape[2] ** 3, bytes_accessed=0, transcendentals=0
        ),
        name="coupling",
    )(near, own, following, in_hbm(inter), in_hbm(ints))


def fold_kernel(given, last, *refs):
    term_refs, (rest, down, across, far_down, far_across), (send, keep) = (
        refs[:given],
        refs[given : given + 5],
        refs[given + 5 :],
    )
    mine, other = (sum(ref[r].astype(F32) for ref in term_refs) for r in range(2))
    mine = mine + rest[...]
    keep[0] = mine
    if last:
        send[0] = other.astype(BF16)
    else:
        send[0] = other.astype(BF16)
        send[1] = (-mine / (down[...] + across[...])).astype(BF16)
        keep[1] = -other / (far_down[...] + far_across[...])


def fold(last, terms, rest, energies):
    given = len(terms)
    rows = 1 if last else 2

    def kernel(*refs):
        fold_kernel(given, last, *refs)

    return pl.pallas_call(
        kernel,
        in_specs=[vmem_spec()] * (given + 5),
        out_specs=[vmem_spec()] * 2,
        out_shape=[
            pltpu.VMEM((rows,) + rest.shape, BF16),
            pltpu.VMEM((rows,) + rest.shape, F32),
        ],
        compiler_params=params(16),
        name="fold",
    )(*terms, rest, *energies)


def finish_kernel(last, keep, got, down, across, out_ref):
    update = -(keep[0] + got[0].astype(F32)) / (down[...] + across[...])
    out_ref[0] = update.astype(out_ref.dtype)
    if not last:
        out_ref[1] = (keep[1] + got[1].astype(F32)).astype(out_ref.dtype)


def finish(last, keep, got, down, across):
    def kernel(*refs):
        finish_kernel(last, *refs)

    return pl.pallas_call(
        kernel,
        in_specs=[vmem_spec()] * 4,
        out_specs=vmem_spec(),
        out_shape=jax.ShapeDtypeStruct(keep.shape, F32) if last else pltpu.VMEM(keep.shape, BF16),
        compiler_params=params(16),
        name="finish",
    )(keep, got, down, across)


def on_device(
    amplitudes,
    bases,
    factors,
    intersections,
    pair_integrals,
    pno_energies,
    pair_shift,
    pair_atoms,
    pair_next,
):
    me = lax.axis_index("dev")
    count = lax.axis_size("dev")
    places = jnp.arange(count, dtype=jnp.int32)
    listed = jnp.any(pair_atoms == me, axis=1)
    before = places[None, :] < places[:, None]
    rank = jnp.sum(before & listed[None, :], axis=1)
    chosen = listed[None, :] & (rank[None, :] == jnp.arange(CAP)[:, None])
    pairs = jnp.sum(jnp.where(chosen, places[None, :] + 1, 0), axis=1) - 1
    slots = jnp.where(pairs >= 0, place_of(pairs, "dev"), 0)

    shifted = pno_energies + 0.5 * pair_shift[:, None]
    far_shifted = exchange(shifted, "dev", opposite("dev"))
    pair_bases = join(in_vmem(bases), exchange(bases, "dev", opposite("dev")))
    amps, far_shifted = lax.optimization_barrier((amplitudes, far_shifted))
    far_amps = exchange(amps, "dev", opposite("dev"))
    amps, pair_bases = lax.optimization_barrier((amps, pair_bases))
    group_bases = gather_near(pair_bases, "dev")
    group_amps = gather_near(jnp.concatenate([amps, far_amps], axis=0), "dev")
    energies = (shifted.reshape(-1, 1), shifted, far_shifted.reshape(-1, 1), far_shifted)
    projected = project(slots, group_bases, factors[0])
    group_amps, projected = lax.optimization_barrier((group_amps, projected))
    for iteration in range(ITERS):
        last = iteration + 1 == ITERS
        stacked = stack(group_amps)
        group_amps, stacked = lax.optimization_barrier((group_amps, stacked))
        following = from_next(stacked, "grp")
        terms = ladder(slots, pairs, group_amps, projected)
        rest = coupling(pair_next, stacked, following, intersections, pair_integrals)
        send, keep = fold(last, exchange_near(terms, "dev"), rest, energies)
        update = finish(last, keep, exchange(send, "dev", opposite("dev")), *energies[:2])
        if not last:
            group_amps = gather_near(update, "dev")
    return update


def solution(mesh):
    return jax.shard_map(
        on_device,
        mesh=mesh,
        in_specs=(
            P(("grp", "dev"), None, None),
            P(("grp", "dev"), None, None),
            P(("grp", "dev"), None, None, None),
            P(("grp", "dev"), None, None, None),
            P(("grp", "dev"), None, None),
            P(("grp", "dev"), None),
            P(("grp", "dev")),
            P("grp", None),
            P(("grp", "dev"), None),
        ),
        out_specs=P(("grp", "dev"), None, None),
        check_vma=False,
    )
```
